32 devices in a mesh: dp: 8 (over z, x), seq: 4 (over y, core).
Axes of the slice: x: 2, y: 2, z: 4, core: 2. Of those that a mesh axis runs over, the one named last changes fastest.
Arguments:
- patches: bfloat16 [964, 16, 768], P('seq', 'dp'), may hold values from -6 to 6
- mask: int32 [964, 16], P('seq', 'dp'), may hold values from 0 to 1, as said below
- mask_token: bfloat16 [768], replicated, may hold values from -4 to 4
- ln1_gain: bfloat16 [768], replicated, may hold values from 0.099609375 to 1.8984375
- ln1_bias: bfloat16 [768], replicated, may hold values from -2 to 2
- w_qkv: bfloat16 [768, 2304], replicated, may hold values from -0.21875 to 0.21875
- bias_q: bfloat16 [768], replicated, may hold values from -2 to 2
- bias_v: bfloat16 [768], replicated, may hold values from -2 to 2
- w_proj: bfloat16 [768, 768], replicated, may hold values from -1.75 to 1.75
- bias_proj: bfloat16 [768], replicated, may hold values from -2 to 2
- scale_attn: bfloat16 [768], replicated, may hold values from 0.5 to 2
- ln2_gain: bfloat16 [768], replicated, may hold values from 0.099609375 to 1.8984375
- ln2_bias: bfloat16 [768], replicated, may hold values from -2 to 2
- w_fc1: bfloat16 [768, 3072], replicated, may hold values from -0.21875 to 0.21875
- bias_fc1: bfloat16 [3072], replicated, may hold values from -2 to 2
- w_fc2: bfloat16 [3072, 768], replicated, may hold values from -0.109375 to 0.109375
- bias_fc2: bfloat16 [768], replicated, may hold values from -2 to 2
- scale_ffn: bfloat16 [768], replicated, may hold values from 0.5 to 2
- cotangent: bfloat16 [964, 16, 768], P('seq', 'dp'), may hold values from -6 to 6
Outputs:
- layer_out: bfloat16 [964, 16, 768], P('seq', 'dp')
- input_grad: bfloat16 [964, 16, 768], P('seq', 'dp')
- grad_mask_token: float32 [768], P('seq')
- grad_ln1_gain: float32 [768], P('seq')
- grad_ln1_bias: float32 [768], P('seq')
- grad_w_qkv: float32 [768, 2304], P('seq')
- grad_bias_q: float32 [768], P('seq')
- grad_bias_v: float32 [768], P('seq')
- grad_w_proj: float32 [768, 768], P('seq')
- grad_bias_proj: float32 [768], P('seq')
- grad_scale_attn: float32 [768], P('seq')
- grad_ln2_gain: float32 [768], P('seq')
- grad_ln2_bias: float32 [768], P('seq')
- grad_w_fc1: float32 [768, 3072], P('seq')
- grad_bias_fc1: float32 [3072], P('seq')
- grad_w_fc2: float32 [3072, 768], P('seq')
- grad_bias_fc2: float32 [768], P('seq')
- grad_scale_ffn: float32 [768], P('seq')
The draws below stay inside these ranges and needn't reach their ends.
Inputs may be any that keep to these rules, and one draw needn't show every extreme that they name: `mask`: 1 marks a masked patch; the class row and empty slots are 0; each image masks between two fifths and four fifths of its 900 patches, its own count drawn per image.
All inputs are finite; a program needn't handle non-finite values.
Results may differ from the reference program's by a relative error of at most 0.02.
Values may be sent and summed in bfloat16 or wider, within the bound.
No kernel may reach another device: no remote copies, remote signals or barrier semaphores. Data moves between devices by JAX's collectives and lax.ppermute only.
A program may use at most 192 MiB of HBM per device.

```python
import math
import jax
import jax.numpy as jnp
from jax import lax

D = 768
FF = 3072
HEADS = 12
HEAD_DIM = 64
GRID = 30
IMG_G = 2
PATCHES = 900
SLOT = 241
ROWS = 964
IMAGES = 16
N_DP = 8
N_SEQ = 4


def draw_mask(key, part):
    key = jax.random.fold_in(key, 7)
    image_keys = jax.random.split(key, IMAGES)
    lowest = (2 * PATCHES + 4) // 5
    highest = 4 * PATCHES // 5

    def one_image(image_key):
        order_key, count_key = jax.random.split(image_key)
        ordering = jax.random.permutation(order_key, PATCHES)
        ranking = jnp.argsort(ordering)
        masked_count = jax.random.randint(count_key, (), lowest, highest + 1)
        return (ranking < masked_count).astype(jnp.int32)
    chosen = jax.vmap(one_image)(image_keys)
    slot_index = jnp.arange(ROWS, dtype=jnp.int32)
    owner = slot_index // SLOT
    inside = slot_index % SLOT
    per_part = GRID // N_SEQ
    spare_rows = GRID % N_SEQ
    first_row = owner * per_part + jnp.minimum(owner, spare_rows)
    patch_count = (per_part + (owner < spare_rows).astype(jnp.int32)) * GRID
    leading = (owner == 0).astype(jnp.int32)
    within = inside - leading
    filled = (within >= 0) & (within < patch_count)
    patch_id = jnp.clip(first_row * GRID + within, 0, PATCHES - 1)
    picked = chosen[:, patch_id]
    return jnp.where(filled[None, :], picked, 0).T.astype(jnp.int32)


def level_of(stream_key, shape, cuts, least, high):
    level, own = 1.0, jax.random.fold_in(stream_key, 6)
    for axis_at, blocks in cuts:
        steps = jnp.exp(jax.random.uniform(jax.random.fold_in(own, axis_at), (blocks,), jnp.float32, least / len(cuts), high / len(cuts)))
        level = level * jnp.repeat(steps, shape[axis_at] // blocks).reshape([-1 if axis == axis_at else 1 for axis in range(len(shape))])
    return level


def scatter_about(key, dims, scale, reach, pieces=(), held_as=jnp.bfloat16):
    drawn = scale * jax.random.normal(key, dims, jnp.float32)
    if pieces:
        drawn = drawn * level_of(key, dims, pieces, -0.22, 0.18)
    return jnp.clip(drawn, -reach, reach).astype(held_as)


def setup_inputs(seed: int = 0) -> dict:
    key_list = jax.random.split(jax.random.key(seed), 20)
    patches = scatter_about(key_list[0], (ROWS, IMAGES, D), 1.0, 6.0, ((0, 4), (1, 8)))
    mask = draw_mask(jax.random.fold_in(key_list[19], 71), 0)
    mask_token = scatter_about(key_list[2], (D,), 1.0, 4.0)
    ln1_gain = jnp.clip(1.0 + 0.18 * jax.random.normal(key_list[3], (D,), jnp.float32), 0.099609375, 1.8984375).astype(jnp.bfloat16)
    ln1_bias = scatter_about(key_list[4], (D,), 0.3, 2.0)
    w_qkv = scatter_about(key_list[5], (D, 3 * D), D ** -0.5, 0.21875)
    bias_q = scatter_about(key_list[6], (D,), 0.3, 2.0)
    bias_v = scatter_about(key_list[7], (D,), 0.3, 2.0)
    w_proj = scatter_about(key_list[8], (D, D), (D // 64) ** -0.5, 1.75)
    bias_proj = scatter_about(key_list[9], (D,), 0.3, 2.0)
    scale_attn = jnp.clip(jnp.exp(jax.random.uniform(key_list[10], (D,), jnp.float32, math.log(0.5), math.log(2.0))), 0.5, 2.0).astype(jnp.bfloat16)
    ln2_gain = jnp.clip(1.0 + 0.18 * jax.random.normal(key_list[11], (D,), jnp.float32), 0.099609375, 1.8984375).astype(jnp.bfloat16)
    ln2_bias = scatter_about(key_list[12], (D,), 0.3, 2.0)
    w_fc1 = scatter_about(key_list[13], (D, FF), D ** -0.5, 0.21875)
    bias_fc1 = scatter_about(key_list[14], (FF,), 0.3, 2.0)
    w_fc2 = scatter_about(key_list[15], (FF, D), FF ** -0.5, 0.109375)
    bias_fc2 = scatter_about(key_list[16], (D,), 0.3, 2.0)
    scale_ffn = jnp.clip(jnp.exp(jax.random.uniform(key_list[17], (D,), jnp.float32, math.log(0.5), math.log(2.0))), 0.5, 2.0).astype(jnp.bfloat16)
    cotangent = scatter_about(key_list[18], (ROWS, IMAGES, D), 1.0, 6.0, ((0, 4), (1, 8)))
    return dict(patches=patches, mask=mask, mask_token=mask_token, ln1_gain=ln1_gain, ln1_bias=ln1_bias, w_qkv=w_qkv, bias_q=bias_q, bias_v=bias_v, w_proj=w_proj, bias_proj=bias_proj, scale_attn=scale_attn, ln2_gain=ln2_gain, ln2_bias=ln2_bias, w_fc1=w_fc1, bias_fc1=bias_fc1, w_fc2=w_fc2, bias_fc2=bias_fc2, scale_ffn=scale_ffn, cotangent=cotangent)


@jax.custom_vjp
def low(v):
    return lax.optimization_barrier(v.astype(jnp.bfloat16)).astype(jnp.float32)

@jax.custom_vjp
def low_back(v):
    return v

def low_keep(v):
    return (low(v), None)

def low_pass(kept, grad):
    return (grad,)

def back_keep(v):
    return (v, None)

def back_low(kept, grad):
    return (low(grad),)
low.defvjp(low_keep, low_pass)
low_back.defvjp(back_keep, back_low)

def slot_live(slot_index, slot_rows, parts):
    owner = slot_index // slot_rows
    inside = slot_index % slot_rows
    per_part = GRID // parts
    spare_rows = GRID % parts
    patch_count = (per_part + (owner < spare_rows).astype(jnp.int32)) * GRID
    leading = (owner == 0).astype(jnp.int32)
    within = inside - leading
    return (within >= 0) & (within < patch_count) | (leading == 1) & (inside == 0)

def normalize(values):
    centred = values - lax.optimization_barrier(jnp.mean(values, -1, keepdims=True))
    spread = lax.optimization_barrier(jnp.mean(centred * centred, -1, keepdims=True))
    return centred * lax.rsqrt(spread + 1e-06)

def project(left, weight):
    return jnp.einsum('rbd,de->rbe', left, weight, precision=lax.Precision.HIGHEST)

def forward(params, entries, chosen, live_keys):
    mask_vector, gain_one, shift_one, w_qkv, bias_q, bias_v, w_proj, bias_proj, scale_attn, gain_two, shift_two, w_fc1, bias_fc1, w_fc2, bias_fc2, scale_ffn = params
    rows_here, images_here, width = entries.shape
    entered = jnp.where((chosen == 1)[:, :, None], mask_vector, entries)
    normed = low(normalize(entered) * gain_one + shift_one)
    joined = project(normed, w_qkv)
    query_rows = low_back(low(joined[..., :width] + bias_q))
    key_rows = low_back(low(joined[..., width:2 * width]))
    value_rows = low_back(low(joined[..., 2 * width:] + bias_v))
    split_shape = (rows_here, images_here, HEADS, HEAD_DIM)
    scores = jnp.einsum('rbhe,sbhe->bhrs', query_rows.reshape(split_shape), key_rows.reshape(split_shape), precision=lax.Precision.HIGHEST) * 0.125
    scores = jnp.where(live_keys, low_back(scores), -1e+30)
    weights = low(jax.nn.softmax(scores, axis=-1))
    mixed = jnp.einsum('bhrs,sbhe->rbhe', weights, value_rows.reshape(split_shape), precision=lax.Precision.HIGHEST).reshape(rows_here, images_here, width)
    mixed = low_back(low(mixed))
    branch = low_back(project(mixed, w_proj) + bias_proj)
    middle = entered + scale_attn * branch
    second = low(normalize(middle) * gain_two + shift_two)
    pre_act = low_back(project(second, w_fc1) + bias_fc1)
    hidden = low(jax.nn.gelu(pre_act, approximate=False))
    branch_two = low_back(project(hidden, w_fc2) + bias_fc2)
    return middle + scale_ffn * branch_two

def reference(patches, mask, mask_token, ln1_gain, ln1_bias, w_qkv, bias_q, bias_v, w_proj, bias_proj, scale_attn, ln2_gain, ln2_bias, w_fc1, bias_fc1, w_fc2, bias_fc2, scale_ffn, cotangent):
    params = tuple((item.astype(jnp.float32) for item in (mask_token, ln1_gain, ln1_bias, w_qkv, bias_q, bias_v, w_proj, bias_proj, scale_attn, ln2_gain, ln2_bias, w_fc1, bias_fc1, w_fc2, bias_fc2, scale_ffn)))
    live_keys = slot_live(jnp.arange(ROWS, dtype=jnp.int32), SLOT, N_SEQ)
    entry_blocks = jnp.moveaxis(patches.astype(jnp.float32).reshape(ROWS, N_DP, IMG_G, D), 1, 0)
    mask_blocks = jnp.moveaxis(mask.reshape(ROWS, N_DP, IMG_G), 1, 0)
    cot_blocks = jnp.moveaxis(cotangent.astype(jnp.float32).reshape(ROWS, N_DP, IMG_G, D), 1, 0)

    def one_group(totals, block):
        entries, chosen, cot_rows = block

        def apply_layer(weights_in, rows_in):
            return forward(weights_in, rows_in, chosen, live_keys)
        result, backward = jax.vjp(apply_layer, params, entries)
        d_out = cot_rows * (chosen == 1).astype(jnp.float32)[:, :, None]
        d_params, d_entries = backward(d_out)
        totals = tuple((left + right for left, right in zip(totals, d_params)))
        return (totals, (result.astype(jnp.bfloat16), d_entries.astype(jnp.bfloat16)))
    zeros = tuple((jnp.zeros_like(item) for item in params))
    totals, (outputs, entry_grads) = lax.scan(one_group, zeros, (entry_blocks, mask_blocks, cot_blocks))
    layer_out = jnp.moveaxis(outputs, 0, 1).reshape(ROWS, IMAGES, D)
    input_grad = jnp.moveaxis(entry_grads, 0, 1).reshape(ROWS, IMAGES, D)
    return (layer_out, input_grad, totals[0], totals[1], totals[2], totals[3], totals[4], totals[5], totals[6], totals[7], totals[8], totals[9], totals[10], totals[11], totals[12], totals[13], totals[14], totals[15])
```

```python
import functools

import jax
import jax.numpy as jnp
from jax import lax
from jax.experimental import pallas as pl
from jax.experimental.pallas import tpu as pltpu
from jax.sharding import PartitionSpec as P

HEADS = 12
GRID = 30
WIDTH = 768
FF = 3072
PART = 256
OWN = 512
GROUPS = 3
EPS = 1e-6
LOG2E = 1.4426950408889634
LN2 = 0.6931471805599453
BF16 = jnp.bfloat16
F32 = jnp.float32
SCALARS = 16
ANY = pl.BlockSpec(memory_space=pl.ANY)
SMEM = pl.BlockSpec(memory_space=pltpu.SMEM)
MIB = 1024 * 1024


def params(limit=48):
    return pltpu.CompilerParams(vmem_limit_bytes=limit * MIB)


def cost(flops, moved, trans=0):
    return pl.CostEstimate(flops=int(flops), bytes_accessed=int(moved), transcendentals=int(trans))


def shape_of(dims, dtype):
    return jax.ShapeDtypeStruct(dims, dtype)


def full(dims):
    return pl.BlockSpec(dims, lambda *_: (0,) * len(dims))


def dot(left, right):
    return jnp.dot(left, right, preferred_element_type=F32)


def dot_nt(left, right):
    return lax.dot_general(left, right, (((1,), (1,)), ((), ())), preferred_element_type=F32)


def dot_tn(left, right):
    return lax.dot_general(left, right, (((0,), (0,)), ((), ())), preferred_element_type=F32)


def norm_parts(values):
    centred = values - jnp.mean(values, -1, keepdims=True)
    rho = lax.rsqrt(jnp.mean(centred * centred, -1, keepdims=True) + EPS)
    return centred * rho, rho


def qkv_kernel(own, x_ref, gain_ref, shift_ref, w_ref, bias_ref, *rest):
    if own:
        joined_ref, normed_ref, entered_ref, kept = rest[-4:]
    else:
        joined_ref, kept = rest[-2:]

    @pl.when(pl.program_id(0) == 0)
    def _():
        x = x_ref[...]
        n, _rho = norm_parts(x.astype(F32))
        kept[...] = (n * gain_ref[...] + shift_ref[...]).astype(BF16)
        if own:
            normed_ref[...] = kept[...]
            entered_ref[...] = x

    joined_ref[...] = (dot(kept[...], w_ref[...]) + bias_ref[...]).astype(BF16)


def qkv_part(own, half, x, gain, shift, w_qkv, bias, previous):
    steps, off = (3, 0) if own else (2, 1)
    outs = [shape_of((OWN, steps * WIDTH), BF16)]
    out_specs = [pl.BlockSpec((PART, WIDTH), lambda j: (half, j))]
    if own:
        outs += [shape_of((OWN, WIDTH), BF16)] * 2
        out_specs += [pl.BlockSpec((PART, WIDTH), lambda j: (half, 0))] * 2
    previous = list(previous)
    return pl.pallas_call(
        functools.partial(qkv_kernel, own),
        grid=(steps,),
        in_specs=[
            full((PART, WIDTH)),
            full((1, WIDTH)),
            full((1, WIDTH)),
            pl.BlockSpec((WIDTH, WIDTH), lambda j: (0, j + off)),
            pl.BlockSpec((1, WIDTH), lambda j: (0, j + off)),
        ]
        + [ANY] * len(previous),
        out_shape=outs,
        out_specs=out_specs,
        scratch_shapes=[pltpu.VMEM((PART, WIDTH), BF16)],
        input_output_aliases={5 + i: i for i in range(len(previous))},
        compiler_params=params(),
        cost_estimate=cost(2 * PART * WIDTH * WIDTH * steps, 2 * steps * WIDTH * (WIDTH + PART)),
        name="qkv_own" if own else "qkv_other",
    )(x, gain, shift, w_qkv, bias, *previous)


DEAD_FROM = 208


def lane_half(values, which):
    lane = lax.broadcasted_iota(jnp.int32, values.shape, 1)
    keep = (lane < 64) if which == 0 else (lane >= 64)
    return jnp.where(keep, values.astype(F32), 0.0).astype(BF16)


def live_scores(scores, count):
    tail = scores[DEAD_FROM:]
    row = lax.broadcasted_iota(jnp.int32, tail.shape, 0) + DEAD_FROM
    return jnp.concatenate([scores[:DEAD_FROM], jnp.where(row < count, tail, -1e30)], 0)


def attend_kernel(sv, q_ref, ka_ref, kb_ref, va_ref, vb_ref, mixed_ref, lse_ref):
    scale = 0.125 * LOG2E
    q = q_ref[...]
    keys = [ka_ref[:PART, :], ka_ref[PART:, :], kb_ref[:PART, :], kb_ref[PART:, :]]
    values = [ref[i : i + PART, :].T for ref in (va_ref, vb_ref) for i in (0, PART)]
    heads = []
    for which in range(2):
        qm = lane_half(q, which)
        scores = [live_scores(dot_nt(k, qm), sv[8 + i]) for i, k in enumerate(keys)]
        top = scores[0]
        for block in scores[1:]:
            top = jnp.maximum(top, block)
        top = jnp.max(top, 0, keepdims=True)
        total = jnp.zeros((1, OWN), F32)
        out = jnp.zeros((64, OWN), F32)
        for block, vt in zip(scores, values):
            p = jnp.exp2((block - top) * scale)
            total += jnp.sum(p, 0, keepdims=True)
            out += dot(vt[64 * which : 64 * which + 64], p.astype(BF16))
        lse_ref[0, which : which + 1, :] = top * scale + jnp.log(total) * LOG2E
        heads.append(out / total)
    mixed_ref[...] = jnp.concatenate(heads, 0).T.astype(BF16)


def attend(sv, joined_a, joined_b):
    pairs = HEADS // 2
    wide = lambda off: pl.BlockSpec((OWN, 128), lambda h: (0, off * pairs + h))
    return pl.pallas_call(
        attend_kernel,
        grid=(pairs,),
        in_specs=[SMEM, wide(0), wide(1), wide(0), wide(2), wide(1)],
        out_shape=[shape_of((OWN, WIDTH), BF16), shape_of((pairs, 2, OWN), F32)],
        out_specs=[wide(0), pl.BlockSpec((1, 2, OWN), lambda h: (h, 0, 0))],
        compiler_params=params(),
        cost_estimate=cost(8 * OWN * 4 * PART * 128 * pairs * 4, 6 * OWN * WIDTH * 2, OWN * 1024 * 12),
        name="attend",
    )(sv, joined_a, joined_a, joined_b, joined_a, joined_b)


def attend_back_kernel(
    sv, q_ref, ka_ref, kb_ref, va_ref, vb_ref, mixed_ref, dmix_ref, lse_ref,
    dq_ref, dka_ref, dva_ref, dkb_ref, dvb_ref,
):
    scale = 0.125 * LOG2E
    q, dmix = q_ref[...], dmix_ref[...]
    product = (mixed_ref[...].astype(F32) * dmix.astype(F32)).T
    deltas = [jnp.sum(product[64 * i : 64 * i + 64], 0, keepdims=True) for i in range(2)]
    qs = [lane_half(q, i) for i in range(2)]
    ds = [lane_half(dmix, i) for i in range(2)]
    dq = [jnp.zeros((64, OWN), F32) for _ in range(2)]
    count = 0
    for k_ref, v_ref, dk_ref, dv_ref in (
        (ka_ref, va_ref, dka_ref, dva_ref),
        (kb_ref, vb_ref, dkb_ref, dvb_ref),
    ):
        for at in (0, PART):
            k, v = k_ref[at : at + PART, :], v_ref[at : at + PART, :]
            kt = k.T
            dk = jnp.zeros((PART, 128), F32)
            dv = jnp.zeros((PART, 128), F32)
            for which in range(2):
                scores = live_scores(dot_nt(k, qs[which]), sv[8 + count])
                p = jnp.exp2(scores * scale - lse_ref[0, which : which + 1, :])
                back = (p * (dot_nt(v, ds[which]) - deltas[which])).astype(BF16)
                dv += dot(p.astype(BF16), ds[which])
                dk += dot(back, qs[which])
                dq[which] += dot(kt[64 * which : 64 * which + 64], back)
            dk_ref[at : at + PART, :] = (dk * 0.125).astype(BF16)
            dv_ref[at : at + PART, :] = dv.astype(BF16)
            count += 1
    dq_ref[...] = (jnp.concatenate(dq, 0) * 0.125).T.astype(BF16)


def attend_back(sv, joined_a, joined_b, mixed, d_mixed, lse):
    pairs = HEADS // 2
    wide = lambda off: pl.BlockSpec((OWN, 128), lambda h: (0, off * pairs + h))
    return pl.pallas_call(
        attend_back_kernel,
        grid=(pairs,),
        in_specs=[
            SMEM, wide(0), wide(1), wide(0), wide(2), wide(1), wide(0), wide(0),
            pl.BlockSpec((1, 2, OWN), lambda h: (h, 0, 0)),
        ],
        out_shape=[shape_of((OWN, WIDTH), BF16)] * 5,
        out_specs=[wide(0)] * 5,
        compiler_params=params(),
        cost_estimate=cost(20 * OWN * 4 * PART * 128 * pairs * 4, 12 * OWN * WIDTH * 2, OWN * 1024 * 12),
        name="attend_back",
    )(sv, joined_a, joined_a, joined_b, joined_a, joined_b, mixed, d_mixed, lse)


def head_kernel(
    mixed_ref, entered_ref, dout_ref, w_ref, bias_ref, sattn_ref, gain_ref, shift_ref, sffn_ref,
    branch_ref, second_ref, secondt_ref, dbt_ref,
):
    branch = dot(mixed_ref[...], w_ref[...]) + bias_ref[...]
    branch_ref[...] = branch
    middle = entered_ref[...].astype(F32) + sattn_ref[...] * branch
    n, _rho = norm_parts(middle)
    second = (n * gain_ref[...] + shift_ref[...]).astype(BF16)
    second_ref[...] = second
    secondt_ref[...] = second.T
    dbt_ref[...] = (dout_ref[:, :WIDTH].astype(F32) * sffn_ref[...]).astype(BF16)


def ff_head(mixed, entered, dout, w_proj, bias_proj, sattn, gain, shift, sffn):
    rows = lambda wide: pl.BlockSpec((PART, wide), lambda i: (i, 0))
    vec = full((1, WIDTH))
    return pl.pallas_call(
        head_kernel,
        grid=(2,),
        in_specs=[rows(WIDTH), rows(WIDTH), rows(WIDTH + 128), full((WIDTH, WIDTH)), vec, vec, vec, vec, vec],
        out_shape=[
            shape_of((OWN, WIDTH), F32),
            shape_of((OWN, WIDTH), BF16),
            shape_of((WIDTH, OWN), BF16),
            shape_of((OWN, WIDTH), BF16),
        ],
        out_specs=[rows(WIDTH), rows(WIDTH), pl.BlockSpec((WIDTH, PART), lambda i: (0, i)), rows(WIDTH)],
        compiler_params=params(),
        cost_estimate=cost(2 * OWN * WIDTH * WIDTH, OWN * WIDTH * 16 + WIDTH * WIDTH * 2),
        name="ff_head",
    )(mixed, entered, dout, w_proj, bias_proj, sattn, gain, shift, sffn)


def gelu_pair(u):
    z = jnp.abs(u) * 0.7071067811865476
    t = 1.0 / (1.0 + 0.3275911 * z)
    e = jnp.exp2(u * u * (-0.5 * LOG2E))
    series = t * (
        0.5 * 0.254829592
        + t * (0.5 * -0.284496736 + t * (0.5 * 1.421413741 + t * (0.5 * -1.453152027 + t * (0.5 * 1.061405429))))
    )
    tail = series * e
    below = jnp.where(u >= 0, 1.0 - tail, tail)
    return u * below, below + u * e * 0.3989422804014327


def dest_index(j):
    return 2 * lax.rem(j, 2) + lax.div(j, 2)


def ff_kernel(
    first, second_ref, secondt_ref, dbt_ref, w1_ref, b1_ref, w2_ref, *rest
):
    branch_ref, grad_ref, payload_ref, gb1_ref = rest[-4:]
    j = pl.program_id(0)
    dbt = dbt_ref[...]
    pre = dot(second_ref[...], w1_ref[...]) + b1_ref[...]
    value, slope = gelu_pair(pre)
    hidden = value.astype(BF16)
    d_pre_wide = (dot_nt(dbt, w2_ref[...]) * slope).astype(BF16)
    gb1_ref[...] = jnp.sum(d_pre_wide.astype(F32), 0, keepdims=True)
    branch_add = dot(hidden, w2_ref[...])
    grad_add = dot_nt(d_pre_wide, w1_ref[...])
    if first:

        @pl.when(j == 0)
        def _():
            branch_ref[...] = branch_add
            grad_ref[...] = grad_add

        @pl.when(j > 0)
        def _():
            branch_ref[...] += branch_add
            grad_ref[...] += grad_add
    else:
        branch_in, grad_in = rest[:2]

        @pl.when(j == 0)
        def _():
            branch_ref[...] = branch_in[...] + branch_add
            grad_ref[...] = grad_in[...] + grad_add

        @pl.when(j > 0)
        def _():
            branch_ref[...] += branch_add
            grad_ref[...] += grad_add

    gw1 = dot(secondt_ref[...], d_pre_wide).astype(BF16)
    quarter = WIDTH // 4
    for s in range(4):
        for i in range(2):
            payload_ref[2 * (s % 2) + s // 2, pl.ds(pl.multiple_of((2 * j + i) * quarter, 16), quarter), :] = gw1[
                quarter * s : quarter * (s + 1), 128 * i : 128 * i + 128
            ]
    gw2 = dot_tn(hidden, dbt).astype(BF16)
    for i in range(6):
        payload_ref[dest_index(j), 8 * quarter + 256 * i : 8 * quarter + 256 * i + 256, :] = gw2[:, 128 * i : 128 * i + 128]


def ff_group(group, second, secondt, dbt, w1, b1, w2, carried):
    block = FF // 4 // GROUPS
    first = not carried
    big = full((OWN, WIDTH))
    rows = 8 * (WIDTH // 4) + 6 * block
    return pl.pallas_call(
        functools.partial(ff_kernel, first),
        grid=(4,),
        in_specs=[
            big,
            full((WIDTH, OWN)),
            big,
            pl.BlockSpec((WIDTH, block), lambda j: (0, GROUPS * j + group)),
            pl.BlockSpec((1, block), lambda j: (0, GROUPS * j + group)),
            pl.BlockSpec((block, WIDTH), lambda j: (GROUPS * j + group, 0)),
        ]
        + [big] * len(carried),
        out_shape=[
            shape_of((OWN, WIDTH), F32),
            shape_of((OWN, WIDTH), F32),
            shape_of((4, rows, 128), BF16),
            shape_of((1, 4 * block), F32),
        ],
        out_specs=[big, big, full((4, rows, 128)), pl.BlockSpec((1, block), lambda j: (0, j))],
        compiler_params=params(),
        cost_estimate=cost(12 * OWN * WIDTH * 4 * block, OWN * WIDTH * 22 + WIDTH * block * 32, OWN * block * 8),
        name=f"ff_group_{group}",
    )(second, secondt, dbt, w1, b1, w2, *carried)


def tail_kernel(
    branch2_ref, g_ref, branch_ref, entered_ref, dout_ref, w_ref,
    b2_ref, sffn_ref, sattn_ref, gain_ref,
    out_ref, dmid_ref, dbr_ref, dmix_ref, vec_ref,
):
    branch_two = branch2_ref[...] + b2_ref[...]
    d_out = dout_ref[:, :WIDTH].astype(F32)
    branch = branch_ref[...]
    middle = entered_ref[...].astype(F32) + sattn_ref[...] * branch
    out_ref[...] = (middle + sffn_ref[...] * branch_two).astype(BF16)
    n, rho = norm_parts(middle)
    g = g_ref[...]
    scaled = g * gain_ref[...]
    d_middle = d_out + rho * (
        scaled - jnp.mean(scaled, -1, keepdims=True) - n * jnp.mean(scaled * n, -1, keepdims=True)
    )
    dmid_ref[...] = d_middle
    d_branch = (d_middle * sattn_ref[...]).astype(BF16)
    dbr_ref[...] = d_branch
    dmix_ref[...] = dot_nt(d_branch, w_ref[...]).astype(BF16)
    rounded = (d_out * sffn_ref[...]).astype(BF16).astype(F32)
    total = lambda v: jnp.sum(v, 0, keepdims=True)
    vec = jnp.concatenate(
        [
            total(d_out * branch_two),
            total(rounded),
            total(g * n),
            total(g),
            total(d_middle * branch),
            total(d_branch.astype(F32)),
            jnp.zeros((2, WIDTH), F32),
        ],
        0,
    )

    @pl.when(pl.program_id(0) == 0)
    def _():
        vec_ref[...] = vec

    @pl.when(pl.program_id(0) > 0)
    def _():
        vec_ref[...] += vec


def ff_tail(branch2, g, branch, entered, dout, w_proj, b2, sffn, sattn, gain):
    rows = lambda wide: pl.BlockSpec((PART, wide), lambda i: (i, 0))
    vec = full((1, WIDTH))
    return pl.pallas_call(
        tail_kernel,
        grid=(2,),
        in_specs=[rows(WIDTH), rows(WIDTH), rows(WIDTH), rows(WIDTH), rows(WIDTH + 128), full((WIDTH, WIDTH)), vec, vec, vec, vec],
        out_shape=[
            shape_of((OWN, WIDTH), BF16),
            shape_of((OWN, WIDTH), F32),
            shape_of((OWN, WIDTH), BF16),
            shape_of((OWN, WIDTH), BF16),
            shape_of((8, WIDTH), F32),
        ],
        out_specs=[rows(WIDTH), rows(WIDTH), rows(WIDTH), rows(WIDTH), full((8, WIDTH))],
        compiler_params=params(),
        cost_estimate=cost(2 * OWN * WIDTH * WIDTH, OWN * WIDTH * 26),
        name="ff_tail",
    )(branch2, g, branch, entered, dout, w_proj, b2, sffn, sattn, gain)


def store_slabs(payload_ref, at, grad):
    quarter = WIDTH // 4
    for s in range(4):
        for i in range(6):
            lo = at + i * quarter
            payload_ref[2 * (s % 2) + s // 2, lo : lo + quarter, :] = grad[
                quarter * s : quarter * (s + 1), 128 * i : 128 * i + 128
            ].astype(BF16)


def proj_query_kernel(mixed_ref, dbr_ref, normed_ref, dq_ref, payload_ref):
    store_slabs(payload_ref, 0, dot_tn(mixed_ref[...], dbr_ref[...]))
    store_slabs(payload_ref, 6 * (WIDTH // 4), dot_tn(normed_ref[...], dq_ref[...]))


def proj_query_grads(mixed, d_branch, normed, d_query):
    big, rows = full((OWN, WIDTH)), 12 * (WIDTH // 4)
    return pl.pallas_call(
        proj_query_kernel,
        grid=(1,),
        in_specs=[big] * 4,
        out_shape=shape_of((4, rows, 128), BF16),
        out_specs=full((4, rows, 128)),
        compiler_params=params(),
        cost_estimate=cost(4 * OWN * WIDTH * WIDTH, OWN * WIDTH * 8 + rows * 1024),
        name="proj_query_grads",
    )(mixed, d_branch, normed, d_query)


def key_value_kernel(normed_ref, dk_ref, rk_ref, dv_ref, rv_ref, dkey_ref, dvalue_ref, payload_ref):
    normed_t = normed_ref[...].T
    d_key = (dk_ref[...].astype(F32) + rk_ref[...].astype(F32)).astype(BF16)
    dkey_ref[...] = d_key
    store_slabs(payload_ref, 0, dot(normed_t, d_key))
    d_value = (dv_ref[...].astype(F32) + rv_ref[...].astype(F32)).astype(BF16)
    dvalue_ref[...] = d_value
    store_slabs(payload_ref, 6 * (WIDTH // 4), dot(normed_t, d_value))


def key_value_grads(normed, dk, rk, dv, rv):
    big, rows = full((OWN, WIDTH)), 12 * (WIDTH // 4)
    return pl.pallas_call(
        key_value_kernel,
        grid=(1,),
        in_specs=[big] * 5,
        out_shape=[shape_of((OWN, WIDTH), BF16)] * 2 + [shape_of((4, rows, 128), BF16)],
        out_specs=[big, big, full((4, rows, 128))],
        compiler_params=params(),
        cost_estimate=cost(4 * OWN * WIDTH * WIDTH, OWN * WIDTH * 14 + rows * 1024),
        name="key_value_grads",
    )(normed, dk, rk, dv, rv)


def entry_kernel(
    dq_ref, dk_ref, dv_ref, w_ref, entered_ref, dmid_ref, dout_ref, gain_ref, grad_ref, vec_ref
):
    dq, dk, dv = dq_ref[...], dk_ref[...], dv_ref[...]
    g = (
        dot_nt(dq, w_ref[:, :WIDTH])
        + dot_nt(dk, w_ref[:, WIDTH : 2 * WIDTH])
        + dot_nt(dv, w_ref[:, 2 * WIDTH :])
    )
    n, rho = norm_parts(entered_ref[...].astype(F32))
    scaled = g * gain_ref[...]
    d_entered = dmid_ref[...] + rho * (
        scaled - jnp.mean(scaled, -1, keepdims=True) - n * jnp.mean(scaled * n, -1, keepdims=True)
    )
    chosen = jnp.concatenate([dout_ref[:, WIDTH:].astype(F32)] * 6, 1)
    masked = d_entered * chosen
    grad_ref[...] = (d_entered - masked).astype(BF16)
    total = lambda v: jnp.sum(v, 0, keepdims=True)
    vec = jnp.concatenate(
        [
            total(masked),
            total(g * n),
            total(g),
            total(dq.astype(F32)),
            total(dv.astype(F32)),
            jnp.zeros((3, WIDTH), F32),
        ],
        0,
    )

    @pl.when(pl.program_id(0) == 0)
    def _():
        vec_ref[...] = vec

    @pl.when(pl.program_id(0) > 0)
    def _():
        vec_ref[...] += vec


def entry_back(dq, dk, dv, w_qkv, entered, d_middle, dout, gain):
    rows = lambda wide: pl.BlockSpec((PART, wide), lambda i: (i, 0))
    return pl.pallas_call(
        entry_kernel,
        grid=(2,),
        in_specs=[rows(WIDTH)] * 3
        + [full((WIDTH, 3 * WIDTH)), rows(WIDTH), rows(WIDTH), rows(WIDTH + 128), full((1, WIDTH))],
        out_shape=[shape_of((OWN, WIDTH), BF16), shape_of((8, WIDTH), F32)],
        out_specs=[rows(WIDTH), full((8, WIDTH))],
        compiler_params=params(),
        cost_estimate=cost(6 * OWN * WIDTH * WIDTH, OWN * WIDTH * 16 + WIDTH * WIDTH * 6),
        name="entry_back",
    )(dq, dk, dv, w_qkv, entered, d_middle, dout, gain)


def swap(value, axis, distance):
    count = lax.axis_size(axis)
    return lax.ppermute(value, axis, [(i, i ^ distance) for i in range(count)])


def pick(array, start, size):
    return lax.dynamic_slice_in_dim(array, start, size, 0)


def add_up(*terms):
    total = terms[0].astype(F32)
    for term in terms[1:]:
        total = total + term.astype(F32)
    return total.astype(BF16)


def reduce_payload(payload, place):
    core, y, x, z = place
    rows = payload.shape[1]
    theirs = swap(pick(payload, 2 * (1 - core), 2), "seq", 1)
    mine = pick(payload, 2 * core, 2)
    to_y = add_up(pick(mine, 1 - y, 1)[0], pick(theirs, 1 - y, 1)[0])
    from_y = swap(to_y, "seq", 2)
    mine, theirs = pick(mine, y, 1)[0], pick(theirs, y, 1)[0]
    if lax.axis_size("dp") != 8:
        return [lax.psum(add_up(mine, theirs, from_y), "dp")], [0]
    half, piece = rows // 2, rows // 8
    terms = [mine, theirs, from_y]
    from_x = swap(add_up(*[pick(t, (1 - x) * half, half) for t in terms]), "dp", 1)
    terms = [pick(t, x * half, half) for t in terms] + [from_x]
    own = None
    arrived = []
    for d in (3, 2, 1):
        part = add_up(*[pick(t, (z ^ d) * piece, piece) for t in terms])
        arrived.append(swap(part, "dp", 2 * d))
    own = add_up(*[pick(t, z * piece, piece) for t in terms])
    summed = add_up(own, *arrived)
    pieces, places = [summed], [4 * x + z]
    for d in (3, 2, 1):
        pieces.append(swap(summed, "dp", 2 * d))
        places.append(4 * x + (z ^ d))
    for value, spot in list(zip(pieces, places)):
        pieces.append(swap(value, "dp", 1))
        places.append(spot ^ 4)
    return pieces, places


def gather_pieces(pieces, places):
    if len(pieces) == 1:
        return pieces[0].astype(BF16)
    piece = pieces[0].shape[0]
    out = jnp.zeros((piece * len(pieces), 128), BF16)
    for value, spot in zip(pieces, places):
        out = lax.dynamic_update_slice_in_dim(out, value, spot * piece, 0)
    return out


def unslab(rows_128, slabs):
    r = rows_128.shape[0] // slabs
    return rows_128.reshape(slabs, r, 128).transpose(1, 0, 2).reshape(r, slabs * 128)


def per_device(
    patches, mask, mask_token, ln1_gain, ln1_bias, w_qkv, bias_q, bias_v, w_proj, bias_proj, scale_attn,
    ln2_gain, ln2_bias, w_fc1, bias_fc1, w_fc2, bias_fc2, scale_ffn, cotangent,
):
    slot_rows, images_here, width = patches.shape
    parts = lax.axis_size("seq")
    assert parts == 4 and images_here == 2 and width == WIDTH
    s = lax.axis_index("seq")
    dp = lax.axis_index("dp")
    y, core = s // 2, s % 2
    x, z = dp % 2, dp // 2

    def live_count(part):
        lead = (part == 0).astype(jnp.int32)
        return lead + (GRID // parts + (part < GRID % parts).astype(jnp.int32)) * GRID

    nothing = jnp.int32(0)
    sv = jnp.stack(
        [s, y, core, x, z, nothing, nothing, nothing]
        + [live_count(s), live_count(s ^ 2), live_count(s ^ 1), live_count(s ^ 3)]
    )
    vec = lambda v: v.astype(F32)[None, :]
    gain1, shift1, gain2, shift2 = vec(ln1_gain), vec(ln1_bias), vec(ln2_gain), vec(ln2_bias)
    sattn, sffn, bproj, b2, b1 = vec(scale_attn), vec(scale_ffn), vec(bias_proj), vec(bias_fc2), vec(bias_fc1)
    bias_qkv = jnp.concatenate([bias_q, jnp.zeros_like(bias_q), bias_v]).astype(F32)[None, :]

    chosen = mask[:, :, None] == 1
    entered = jnp.where(chosen, mask_token, patches)
    grow = ((0, PART - slot_rows), (0, 0))
    image = lambda array, i: lax.dynamic_index_in_dim(array, i, 1, keepdims=False)
    x1 = swap(jnp.pad(image(entered, 1 - y), grow), "seq", 2)
    x0 = jnp.pad(image(entered, y), grow)
    xb0 = swap(x0, "seq", 1)
    xb1 = swap(x1, "seq", 1)
    d_rows = jnp.concatenate(
        [
            jnp.where(chosen, cotangent, jnp.zeros_like(cotangent)),
            jnp.broadcast_to(chosen, (slot_rows, images_here, 128)).astype(BF16),
        ],
        -1,
    )
    d1 = swap(jnp.pad(image(d_rows, 1 - y), grow), "seq", 2)
    d0 = jnp.pad(image(d_rows, y), grow)

    own_first = qkv_part(True, 0, x0, gain1, shift1, w_qkv, bias_qkv, [])
    other_first = qkv_part(False, 0, xb0, gain1, shift1, w_qkv, bias_qkv, [])
    joined_a, normed, entered_a = qkv_part(True, 1, x1, gain1, shift1, w_qkv, bias_qkv, own_first)
    (joined_b,) = qkv_part(False, 1, xb1, gain1, shift1, w_qkv, bias_qkv, other_first)
    mixed, lse = attend(sv, joined_a, joined_b)
    dout = jnp.concatenate([d0, d1], 0)
    branch, second, secondt, dbt = ff_head(mixed, entered_a, dout, w_proj, bproj, sattn, gain2, shift2, sffn)
    carried, payloads, gb1 = [], [], []
    for group in range(GROUPS):
        branch2, g, payload, row = ff_group(group, second, secondt, dbt, w_fc1, b1, w_fc2, carried)
        carried = [branch2, g]
        payloads.append(payload)
        gb1.append(row)
    place = (core, y, x, z)
    reduced = [reduce_payload(p, place) for p in payloads]
    out_a, d_middle, d_branch, d_mixed, vec_a = ff_tail(
        carried[0], carried[1], branch, entered_a, dout, w_proj, b2, sffn, sattn, gain2
    )
    out_far = swap(out_a[PART : PART + slot_rows], "seq", 2)
    dq, dka, dva, dkb, dvb = attend_back(sv, joined_a, joined_b, mixed, d_mixed, lse)
    rk, rv = swap(dkb, "seq", 1), swap(dvb, "seq", 1)
    reduced.append(reduce_payload(proj_query_grads(mixed, d_branch, normed, dq), place))
    d_key, d_value, payload = key_value_grads(normed, dka, rk, dva, rv)
    reduced.append(reduce_payload(payload, place))
    grad_a, vec_b = entry_back(dq, d_key, d_value, w_qkv, entered_a, d_middle, dout, gain1)
    grad_far = swap(grad_a[PART : PART + slot_rows], "seq", 2)

    block = FF // 4 // GROUPS
    wide_b1 = jnp.stack([g.reshape(4, block) for g in gb1], 1).reshape(4, WIDTH)
    sums = jnp.concatenate([vec_a, vec_b, wide_b1], 0)
    sums = sums + swap(sums, "seq", 1)
    sums = sums + swap(sums, "seq", 2)
    if lax.axis_size("dp") == 8:
        for bit in (1, 2, 4):
            sums = sums + swap(sums, "dp", bit)
    else:
        sums = lax.psum(sums, "dp")
    quarter = WIDTH // 4
    vectors = lax.dynamic_slice_in_dim(sums, s * quarter, quarter, 1)
    grad_b1 = lax.dynamic_index_in_dim(sums[16:20], s, 0, keepdims=False)

    together = [gather_pieces(*r) for r in reduced]
    gw1, gw2 = [], []
    for t in together[:GROUPS]:
        gw1.append(unslab(t[: 8 * quarter], 8).reshape(quarter, 4, block))
        gw2.append(unslab(t[8 * quarter :], 6))
    grad_w1 = jnp.stack(gw1, 2).reshape(quarter, FF).astype(F32)
    grad_w2 = jnp.concatenate(gw2, 0).astype(F32)
    grad_proj = unslab(together[GROUPS][: 6 * quarter], 6).astype(F32)
    grad_qkv = jnp.concatenate(
        [unslab(together[GROUPS][6 * quarter :], 6), unslab(together[GROUPS + 1], 12)], 1
    ).astype(F32)

    def place_rows(near, far):
        near, far = near[:, None], far[:, None]
        return jnp.where(
            y == 0, jnp.concatenate([near, far], 1), jnp.concatenate([far, near], 1)
        )

    return (
        place_rows(out_a[:slot_rows], out_far),
        place_rows(grad_a[:slot_rows], grad_far),
        vectors[8], vectors[9], vectors[10], grad_qkv, vectors[11], vectors[12], grad_proj,
        vectors[5], vectors[4], vectors[2], vectors[3], grad_w1, grad_b1, grad_w2, vectors[1], vectors[0],
    )


def solution(mesh):
    rows, flat = P("seq", "dp", None), P("seq")
    deep = P("seq", None)
    return jax.shard_map(
        per_device,
        mesh=mesh,
        in_specs=(rows, P("seq", "dp")) + (P(),) * 16 + (rows,),
        out_specs=(
            rows, rows, flat, flat, flat, deep, flat, flat, deep, flat, flat, flat, flat, deep, flat, deep, flat, flat,
        ),
        check_vma=False,
    )
```

```python
import functools

import jax
import jax.numpy as jnp
from jax import lax
from jax.experimental import pallas as pl
from jax.experimental.pallas import tpu as pltpu
from jax.sharding import PartitionSpec as P

HEADS = 12
GRID = 30
WIDTH = 768
FF = 3072
PART = 256
OWN = 512
GROUPS = 3
EPS = 1e-6
LOG2E = 1.4426950408889634
LN2 = 0.6931471805599453
BF16 = jnp.bfloat16
F32 = jnp.float32
ANY = pl.BlockSpec(memory_space=pl.ANY)
SMEM = pl.BlockSpec(memory_space=pltpu.SMEM)
MIB = 1024 * 1024


def params(limit=58):
    return pltpu.CompilerParams(vmem_limit_bytes=limit * MIB)


def launch(kernel, sv, grid, ins, outs, scratch=(), alias=None, after=(), limit=8, micros=0.05, name=None):
    alias = alias or {}
    after = list(after)
    count = len(ins)

    def body(sv_ref, *refs):
        kernel(sv_ref, *refs[:count], *refs[count + len(after) :])

    spec = lambda block, index: ANY if block is None else pl.BlockSpec(block, index)
    return pl.pallas_call(
        body,
        grid_spec=pltpu.PrefetchScalarGridSpec(
            num_scalar_prefetch=1,
            grid=grid,
            in_specs=[spec(b, i) for _, b, i in ins] + [ANY] * len(after),
            out_specs=[spec(b, i) for _, _, b, i in outs],
            scratch_shapes=list(scratch),
        ),
        out_shape=[shape_of(d, t) for d, t, _, _ in outs],
        input_output_aliases={1 + k: v for k, v in alias.items()},
        compiler_params=params(limit),
        cost_estimate=cost(micros),
        name=name,
    )(sv, *[a for a, _, _ in ins], *after)


def whole(array):
    dims = array.shape
    return (array, dims, lambda *_: (0,) * len(dims))


def row_of(table, index):
    return (table, (1, WIDTH), lambda *_: (0, index))


def out_whole(dims, dtype):
    return (dims, dtype, dims, lambda *_: (0,) * len(dims))


def cost(micros):
    return pl.CostEstimate(flops=int(micros * 1.15e9), bytes_accessed=0, transcendentals=0)


def shape_of(dims, dtype):
    return jax.ShapeDtypeStruct(dims, dtype)


def full(dims):
    return pl.BlockSpec(dims, lambda *_: (0,) * len(dims))


def dot(left, right):
    return jnp.dot(left, right, preferred_element_type=F32)


def dot_nt(left, right):
    return lax.dot_general(left, right, (((1,), (1,)), ((), ())), preferred_element_type=F32)


def dot_tn(left, right):
    return lax.dot_general(left, right, (((0,), (0,)), ((), ())), preferred_element_type=F32)


def norm_parts(values):
    centred = values - jnp.mean(values, -1, keepdims=True)
    rho = lax.rsqrt(jnp.mean(centred * centred, -1, keepdims=True) + EPS)
    return centred * rho, rho


def qkv_kernel(own, sv, x_ref, gain_ref, shift_ref, w_ref, bias_ref, *rest):
    if own:
        joined_ref, normed_ref, entered_ref, kept = rest[-4:]
    else:
        joined_ref, kept = rest[-2:]

    @pl.when(pl.program_id(0) == 0)
    def _():
        x = x_ref[...]
        n, _rho = norm_parts(x.astype(F32))
        kept[...] = (n * gain_ref[...] + shift_ref[...]).astype(BF16)
        if own:
            normed_ref[...] = kept[...]
            entered_ref[...] = x

    joined_ref[...] = (dot(kept[...], w_ref[...]) + bias_ref[...]).astype(BF16)


def qkv_part(own, half, x, table, w_qkv, previous, after=()):
    steps, off = (3, 0) if own else (2, 1)
    outs = [((OWN, steps * WIDTH), BF16, (PART, WIDTH), lambda j, sv: (half, j))]
    if own:
        outs += [((OWN, WIDTH), BF16, (PART, WIDTH), lambda j, sv: (half, 0))] * 2
    previous = list(previous)
    return launch(
        functools.partial(qkv_kernel, own),
        jnp.zeros((1,), jnp.int32),
        (steps,),
        [
            whole(x),
            row_of(table, 3),
            row_of(table, 4),
            (w_qkv, (WIDTH, WIDTH), lambda j, sv: (0, j + off)),
            (table, (1, WIDTH), lambda j, sv: (0, j + off)),
        ]
        + [(p, None, None) for p in previous],
        outs,
        scratch=[pltpu.VMEM((PART, WIDTH), BF16)],
        alias={5 + i: i for i in range(len(previous))},
        after=after,
        limit=10,
        micros=4,
        name="qkv_own" if own else "qkv_other",
    )


DEAD_FROM = 208


def lane_half(values, which):
    lane = lax.broadcasted_iota(jnp.int32, values.shape, 1)
    keep = (lane < 64) if which == 0 else (lane >= 64)
    return jnp.where(keep, values.astype(F32), 0.0).astype(BF16)


def live_scores(scores, count):
    tail = scores[DEAD_FROM:]
    row = lax.broadcasted_iota(jnp.int32, tail.shape, 0) + DEAD_FROM
    return jnp.concatenate([scores[:DEAD_FROM], jnp.where(row < count, tail, -1e30)], 0)


PAIRS = 3


class Pair:
    def __init__(self, pair, q_ref, ka_ref, kb_ref, va_ref, vb_ref):
        self.at = slice(128 * pair, 128 * pair + 128)
        self.q = [lane_half(q_ref[:, self.at], i) for i in range(2)]
        self.k = jnp.concatenate([ka_ref[:, self.at], kb_ref[:, self.at]], 0)
        self.v = jnp.concatenate([va_ref[:, self.at], vb_ref[:, self.at]], 0)


def blocks(scores, sv):
    return [live_scores(scores[PART * i : PART * i + PART], sv[COUNTS + i]) for i in range(4)]


def ahead(count, first, then):
    waiting = first(0)
    for i in range(count):
        now, waiting = waiting, first(i + 1) if i + 1 < count else None
        then(i, now)


def attend_kernel(sv, q_ref, ka_ref, kb_ref, va_ref, vb_ref, mixed_ref, lse_ref):
    scale = 0.125 * LOG2E
    pairs, heads = {}, []

    def first(i):
        if i % 2 == 0:
            pairs[i // 2] = Pair(i // 2, q_ref, ka_ref, kb_ref, va_ref, vb_ref)
            pairs[i // 2].vt = pairs[i // 2].v.T
        pair = pairs[i // 2]
        return blocks(dot_nt(pair.k, pair.q[i % 2]), sv)

    def then(i, scores):
        which, pair = i % 2, pairs[i // 2]
        top = scores[0]
        for block in scores[1:]:
            top = jnp.maximum(top, block)
        top = jnp.max(top, 0, keepdims=True)
        total = jnp.zeros((1, OWN), F32)
        out = jnp.zeros((64, OWN), F32)
        for b, block in enumerate(scores):
            p = jnp.exp2((block - top) * scale)
            total += jnp.sum(p, 0, keepdims=True)
            out += dot(pair.vt[64 * which : 64 * which + 64, PART * b : PART * b + PART], p.astype(BF16))
        lse_ref[i // 2, which : which + 1, :] = top * scale + jnp.log(total) * LOG2E
        heads.append(out / total)
        if which == 1:
            mixed_ref[:, pair.at] = jnp.concatenate(heads[-2:], 0).T.astype(BF16)

    ahead(2 * PAIRS, first, then)


def attend(sv, joined_a, joined_b):
    steps = HEADS // 2 // PAIRS
    wide = lambda array, off: (array, (OWN, 128 * PAIRS), lambda h, sv: (0, off * steps + h))
    return launch(
        attend_kernel,
        sv,
        (steps,),
        [wide(joined_a, 0), wide(joined_a, 1), wide(joined_b, 0), wide(joined_a, 2), wide(joined_b, 1)],
        [
            ((OWN, WIDTH), BF16, (OWN, 128 * PAIRS), lambda h, sv: (0, h)),
            ((HEADS // 2, 2, OWN), F32, (PAIRS, 2, OWN), lambda h, sv: (h, 0, 0)),
        ],
        limit=28,
        name="attend",
    )


def attend_back_kernel(
    sv, q_ref, ka_ref, kb_ref, va_ref, vb_ref, mixed_ref, dmix_ref, lse_ref,
    dq_ref, dka_ref, dva_ref, dkb_ref, dvb_ref,
):
    scale = 0.125 * LOG2E
    pairs, held = {}, []

    def first(i):
        if i % 2 == 0:
            pair = pairs[i // 2] = Pair(i // 2, q_ref, ka_ref, kb_ref, va_ref, vb_ref)
            dmix = dmix_ref[:, pair.at]
            product = (mixed_ref[:, pair.at].astype(F32) * dmix.astype(F32)).T
            pair.delta = [jnp.sum(product[64 * w : 64 * w + 64], 0, keepdims=True) for w in range(2)]
            pair.d = [lane_half(dmix, w) for w in range(2)]
            pair.kt = pair.k.T
        pair = pairs[i // 2]
        return dot_nt(pair.k, pair.q[i % 2]), dot_nt(pair.v, pair.d[i % 2])

    def then(i, products):
        which, pair = i % 2, pairs[i // 2]
        weights, backs = [], []
        for b, scores in enumerate(blocks(products[0], sv)):
            p = jnp.exp2(scores * scale - lse_ref[i // 2, which : which + 1, :])
            weights.append(p.astype(BF16))
            backs.append((p * (products[1][PART * b : PART * b + PART] - pair.delta[which])).astype(BF16))
        weights, backs = jnp.concatenate(weights, 0), jnp.concatenate(backs, 0)
        dv, dk = dot(weights, pair.d[which]), dot(backs, pair.q[which])
        dq = dot(pair.kt[64 * which : 64 * which + 64], backs)
        if which == 0:
            held[:] = [dv, dk, dq]
            return
        dv, dk = dv + held[0], (dk + held[1]) * 0.125
        dka_ref[:, pair.at], dkb_ref[:, pair.at] = dk[:OWN].astype(BF16), dk[OWN:].astype(BF16)
        dva_ref[:, pair.at], dvb_ref[:, pair.at] = dv[:OWN].astype(BF16), dv[OWN:].astype(BF16)
        dq_ref[:, pair.at] = (jnp.concatenate([held[2], dq], 0) * 0.125).T.astype(BF16)

    ahead(2 * PAIRS, first, then)


def attend_back(sv, half, joined_a, joined_b, mixed, d_mixed, lse, after):
    steps = HEADS // 2 // PAIRS
    wide = lambda array, off: (array, (OWN, 128 * PAIRS), lambda h, sv: (0, off * steps + half))
    return launch(
        attend_back_kernel,
        sv,
        (1,),
        [
            wide(joined_a, 0), wide(joined_a, 1), wide(joined_b, 0), wide(joined_a, 2), wide(joined_b, 1),
            wide(mixed, 0), wide(d_mixed, 0),
            (lse, (PAIRS, 2, OWN), lambda h, sv: (half, 0, 0)),
        ],
        [out_whole((OWN, WIDTH // 2), BF16)] * 5,
        after=after,
        limit=28,
        name=f"attend_back_{half}",
    )


QUARTER = WIDTH // 4


def rows_of(array):
    return (array, (PART, array.shape[1]), lambda i, sv: (i, 0))


def out_rows(wide, dtype):
    return ((OWN, wide), dtype, (PART, wide), lambda i, sv: (i, 0))


def gelu_pair(u):
    z = jnp.abs(u) * 0.7071067811865476
    t = 1.0 / (1.0 + 0.3275911 * z)
    e = jnp.exp2(u * u * (-0.5 * LOG2E))
    series = t * (
        0.5 * 0.254829592
        + t * (0.5 * -0.284496736 + t * (0.5 * 1.421413741 + t * (0.5 * -1.453152027 + t * (0.5 * 1.061405429))))
    )
    tail = series * e
    below = jnp.where(u >= 0, 1.0 - tail, tail)
    return u * below, below + u * e * 0.3989422804014327


def step_part(j, sv):
    return 2 * jnp.where(lax.rem(j, 2) == 0, sv[FAR_Y], sv[Y]) + jnp.where(j < 2, 1 - sv[CORE], sv[CORE])


BLOCK = FF // 4 // GROUPS
FF_ROWS = 8 * QUARTER + 6 * BLOCK


def ff_kernel(
    sv, mixed_ref, entered_ref, d0_ref, d1_ref, wproj_ref, bias_ref, sattn_ref, gain_ref, shift_ref, sffn_ref, *rest
):
    weights = [rest[3 * i : 3 * i + 3] for i in range(4)]
    branch_ref, branch2_ref, grad_ref, gb1_ref, dout_ref, *rest = rest[12:]
    shares, (second_ref, secondt_ref, dbt_ref) = rest[:4], rest[4:]
    step = pl.program_id(0)

    @pl.when(step == 0)
    def _():
        branch = dot(mixed_ref[...], wproj_ref[...]) + bias_ref[...]
        branch_ref[...] = branch
        n, _rho = norm_parts(entered_ref[...].astype(F32) + sattn_ref[...] * branch)
        second = (n * gain_ref[...] + shift_ref[...]).astype(BF16)
        second_ref[...] = second
        turned = second.T
        for part in range(4):
            place = jnp.where(part % 2 != sv[CORE], 0, 2) + jnp.where(part // 2 != sv[Y], 0, 1)
            secondt_ref[pl.ds(pl.multiple_of(place * QUARTER, 16), QUARTER), :] = turned[
                QUARTER * part : QUARTER * part + QUARTER
            ]
        dout_ref[:PART, :], dout_ref[PART:, :] = d0_ref[...], d1_ref[...]
        dbt_ref[...] = (dout_ref[:, :WIDTH].astype(F32) * sffn_ref[...]).astype(BF16)
        branch2_ref[...] = jnp.zeros((OWN, WIDTH), F32)
        grad_ref[...] = jnp.zeros((OWN, WIDTH), F32)

    hidden, d_pre = [], []

    def first(i):
        w1_ref, b1_ref, w2_ref = weights[i]
        return dot(second_ref[...], w1_ref[...]) + b1_ref[...], dot_nt(dbt_ref[...], w2_ref[...])

    def then(i, products):
        value, slope = gelu_pair(products[0])
        hidden.append(value.astype(BF16))
        d_pre.append((products[1] * slope).astype(BF16))
        spot = pl.ds(pl.multiple_of(step_part(i, sv) * BLOCK, BLOCK), BLOCK)
        gb1_ref[:, spot] = jnp.sum(d_pre[-1].astype(F32), 0, keepdims=True)

    ahead(4, first, then)
    hidden, d_pre = jnp.concatenate(hidden, 1), jnp.concatenate(d_pre, 1)
    gw1 = dot(secondt_ref[...], d_pre).astype(BF16)
    for i in range(4):
        for k in range(2):
            spot = pl.ds(pl.multiple_of((2 * step_part(i, sv) + k) * QUARTER, 16), QUARTER)
            at = BLOCK * i + 128 * k
            for ref, row in zip(shares, range(0, WIDTH, QUARTER)):
                ref[spot, :] = gw1[row : row + QUARTER, at : at + 128]
    gw2 = dot_tn(hidden, dbt_ref[...]).astype(BF16)
    for i in range(4):
        for k in range(6):
            low = 8 * QUARTER + BLOCK * k
            shares[i][low : low + BLOCK, :] = gw2[BLOCK * i : BLOCK * i + BLOCK, 128 * k : 128 * k + 128]
    branch2_ref[...] += dot(hidden, jnp.concatenate([w[2][...] for w in weights], 0))
    grad_ref[...] += dot_nt(d_pre, jnp.concatenate([w[0][...] for w in weights], 1))


def feed_forward(sv, mixed, entered, d0, d1, w_proj, vectors, w1, table, w2):
    streamed = []
    for i in range(4):
        at = lambda g, sv, i=i: GROUPS * step_part(i, sv) + g
        streamed += [
            (w1, (WIDTH, BLOCK), lambda g, sv, at=at: (0, at(g, sv))),
            (table, (1, BLOCK), lambda g, sv, at=at: (0, 11 * GROUPS + at(g, sv))),
            (w2, (BLOCK, WIDTH), lambda g, sv, at=at: (at(g, sv), 0)),
        ]
    return launch(
        ff_kernel,
        sv,
        (GROUPS,),
        [whole(mixed), whole(entered), whole(d0), whole(d1), whole(w_proj)] + vectors + streamed,
        [
            out_whole((OWN, WIDTH), F32),
            out_whole((OWN, WIDTH), F32),
            out_whole((OWN, WIDTH), F32),
            ((1, FF), F32, (1, 4 * BLOCK), lambda g, sv: (0, g)),
            out_whole((OWN, WIDTH + 128), BF16),
            *[((GROUPS * FF_ROWS, 128), BF16, (FF_ROWS, 128), lambda g, sv: (g, 0))] * 4,
        ],
        scratch=[pltpu.VMEM((OWN, WIDTH), BF16), pltpu.VMEM((WIDTH, OWN), BF16), pltpu.VMEM((OWN, WIDTH), BF16)],
        limit=56,
        name="feed_forward",
    )


def tail_kernel(
    sv, branch2_ref, g_ref, branch_ref, entered_ref, dout_ref, w_ref, b2_ref, sffn_ref, sattn_ref, gain_ref,
    out_ref, dmid_ref, dbr_ref, dmix_ref, vec_ref,
):
    branch_two = branch2_ref[...] + b2_ref[...]
    d_out = dout_ref[:, :WIDTH].astype(F32)
    branch = branch_ref[...]
    middle = entered_ref[...].astype(F32) + sattn_ref[...] * branch
    out_ref[...] = (middle + sffn_ref[...] * branch_two).astype(BF16)
    n, rho = norm_parts(middle)
    g = g_ref[...]
    scaled = g * gain_ref[...]
    d_middle = d_out + rho * (
        scaled - jnp.mean(scaled, -1, keepdims=True) - n * jnp.mean(scaled * n, -1, keepdims=True)
    )
    dmid_ref[...] = d_middle
    d_branch = (d_middle * sattn_ref[...]).astype(BF16)
    dbr_ref[...] = d_branch
    dmix_ref[...] = dot_nt(d_branch, w_ref[...]).astype(BF16)
    rounded = (d_out * sffn_ref[...]).astype(BF16).astype(F32)
    add_vectors(
        vec_ref,
        [d_out * branch_two, rounded, g * n, g, d_middle * branch, d_branch.astype(F32)],
    )


def add_vectors(vec_ref, values):
    rows = [jnp.sum(v, 0, keepdims=True) for v in values]
    vec = jnp.concatenate(rows + [jnp.zeros((8 - len(rows), WIDTH), F32)], 0)

    @pl.when(pl.program_id(0) == 0)
    def _():
        vec_ref[...] = vec

    @pl.when(pl.program_id(0) > 0)
    def _():
        vec_ref[...] += vec


def ff_tail(sv, branch2, g, branch, entered, dout, w_proj, vectors, after):
    return launch(
        tail_kernel,
        sv,
        (2,),
        [rows_of(a) for a in (branch2, g, branch, entered, dout)] + [whole(w_proj)] + list(vectors),
        [out_rows(WIDTH, BF16), out_rows(WIDTH, F32), out_rows(WIDTH, BF16), out_rows(WIDTH, BF16), out_whole((8, WIDTH), F32)],
        after=after,
        limit=16,
        name="ff_tail",
    )


def store_slabs(sv, kept, slabs, at, shares):
    for step, ref in enumerate(shares):
        rows = pl.ds(pl.multiple_of(step_part(step, sv) * QUARTER, 16), QUARTER)
        for i in range(slabs):
            lo = at + i * QUARTER
            ref[lo : lo + QUARTER, :] = kept[rows, 128 * i : 128 * i + 128].astype(BF16)


def first_grads_kernel(
    sv, mixed_ref, dbr_ref, normed_ref, dq_ref, dk_ref, rk_ref, dv_ref, rv_ref,
    *rest,
):
    *shares, dkey_ref, dvalue_ref, kept = rest
    kept[:, :WIDTH] = dot_tn(mixed_ref[...], dbr_ref[...])
    store_slabs(sv, kept, 6, 0, shares)
    d_key = (dk_ref[...].astype(F32) + rk_ref[...].astype(F32)).astype(BF16)
    d_value = (dv_ref[...].astype(F32) + rv_ref[...].astype(F32)).astype(BF16)
    dkey_ref[...] = d_key
    dvalue_ref[...] = d_value
    kept[...] = dot_tn(normed_ref[...], jnp.concatenate([dq_ref[...], d_key, d_value], 1))
    store_slabs(sv, kept, 9, 6 * QUARTER, shares)


def first_grads(sv, mixed, d_branch, normed, parts, after):
    rows = 15 * QUARTER
    return launch(
        first_grads_kernel,
        sv,
        (1,),
        [whole(a) for a in (mixed, d_branch, normed, *parts)],
        [out_whole((rows, 128), BF16)] * 4 + [out_whole((OWN, WIDTH // 2), BF16)] * 2,
        scratch=[pltpu.VMEM((WIDTH, 9 * 128), F32)],
        after=after,
        limit=24,
        name="first_grads",
    )


VEC_ROWS = 128


def second_grads_kernel(
    sv, normed_ref, dq_ref, dk_ref, rk_ref, dv_ref, rv_ref, va_ref, vb_ref, b1_ref,
    *rest,
):
    *shares, kept, spread = rest
    d_key = (dk_ref[...].astype(F32) + rk_ref[...].astype(F32)).astype(BF16)
    d_value = (dv_ref[...].astype(F32) + rv_ref[...].astype(F32)).astype(BF16)
    kept[...] = dot_tn(normed_ref[...], jnp.concatenate([dq_ref[...], d_key, d_value], 1))
    store_slabs(sv, kept, 9, 0, shares)
    vec = jnp.concatenate([va_ref[...], vb_ref[...]], 0)
    for part in range(4):
        at = QUARTER * part
        spots = [4 * BLOCK * g + BLOCK * part + 128 * i for g in range(GROUPS) for i in range(2)]
        b1 = [b1_ref[:, spot : spot + 128] for spot in spots]
        spread[part] = jnp.concatenate(
            [
                vec[:, at : at + 128],
                jnp.concatenate([vec[:, at + 128 : at + 192], jnp.zeros((16, 64), F32)], 1),
                *b1,
                jnp.zeros((VEC_ROWS - 38, 128), F32),
            ],
            0,
        )
    for step, ref in enumerate(shares):
        ref[9 * QUARTER :, :] = spread[step_part(step, sv)].astype(BF16)


def second_grads(sv, normed, parts, vectors, after):
    rows = 9 * QUARTER + VEC_ROWS
    return launch(
        second_grads_kernel,
        sv,
        (1,),
        [whole(a) for a in (normed, *parts, *vectors)],
        [out_whole((rows, 128), BF16)] * 4,
        scratch=[pltpu.VMEM((WIDTH, 9 * 128), F32), pltpu.VMEM((4, VEC_ROWS, 128), F32)],
        after=after,
        limit=20,
        name="second_grads",
    )


def entry_kernel(
    sv, dq1_ref, dk1_ref, dv1_ref, dq2_ref, dk2_ref, rk2_ref, dv2_ref, rv2_ref, w_ref, entered_ref, dmid_ref, dout_ref,
    gain_ref, grad_ref, vec_ref,
):
    both = lambda a, b: (a[...].astype(F32) + b[...].astype(F32)).astype(BF16)
    dq = jnp.concatenate([dq1_ref[...], dq2_ref[...]], 1)
    dk = jnp.concatenate([dk1_ref[...], both(dk2_ref, rk2_ref)], 1)
    dv = jnp.concatenate([dv1_ref[...], both(dv2_ref, rv2_ref)], 1)
    g = dot_nt(jnp.concatenate([dq, dk, dv], 1), w_ref[...])
    n, rho = norm_parts(entered_ref[...].astype(F32))
    scaled = g * gain_ref[...]
    d_entered = dmid_ref[...] + rho * (
        scaled - jnp.mean(scaled, -1, keepdims=True) - n * jnp.mean(scaled * n, -1, keepdims=True)
    )
    chosen = jnp.concatenate([dout_ref[:, WIDTH:].astype(F32)] * 6, 1)
    masked = d_entered * chosen
    grad_ref[...] = (d_entered - masked).astype(BF16)
    add_vectors(vec_ref, [masked, g * n, g, dq.astype(F32), dv.astype(F32)])


def entry_back(sv, parts, w_qkv, entered, d_middle, dout, gain, after):
    return launch(
        entry_kernel,
        sv,
        (2,),
        [rows_of(p) for p in parts]
        + [whole(w_qkv), rows_of(entered), rows_of(d_middle), rows_of(dout), gain],
        [out_rows(WIDTH, BF16), out_whole((8, WIDTH), F32)],
        after=after,
        limit=20,
        micros=10,
        name="entry_back",
    )


CORE, Y, FAR_Y, X, FAR_X, Z, FAR_Z, QUARTER_MINE, QUARTER_FAR, TURNED_MINE, TURNED_FAR, COUNTS = range(12)


def swap(value, axis, distance):
    count = lax.axis_size(axis)
    return lax.ppermute(value, axis, [(i, i ^ distance) for i in range(count)])


def sums_kernel(plan, sv, *refs):
    count = sum(terms for _, _, parts in plan for _, terms in parts)
    ins, outs = list(refs[:count]), refs[count:]
    for (_, _, parts), out_ref in zip(plan, outs):
        low = 0
        for rows, terms in parts:
            total = ins.pop(0)[...].astype(F32)
            for _ in range(terms - 1):
                total += ins.pop(0)[...].astype(F32)
            out_ref[low : low + rows, :] = total.astype(BF16)
            low += rows


def add_up(sv, outs, after, name, micros=0.05):
    ins, plan, results = [], [], []
    for parts in outs:
        for rows, terms in parts:
            for array, block, skip in terms:
                at = lambda i, sv, block=block, skip=skip: (skip if block is None else sv[block] + skip, 0)
                ins.append((array, (rows, 128), at))
        total = sum(rows for rows, _ in parts)
        plan.append((None, None, [(rows, len(terms)) for rows, terms in parts]))
        results.append(out_whole((total, 128), BF16))
    return list(launch(functools.partial(sums_kernel, plan), sv, (1,), ins, results, after=after, limit=16, micros=micros, name=name))


class Piece:
    def __init__(self, order, kept, rows, skip=0):
        self.order, self.rows, self.skip = order, rows, skip
        self.far, self.near, self.core_far, self.core = kept

    def two(self, share, block, far):
        a, b = (self.far, self.core_far) if far else (self.near, self.core)
        return [(a, block, share * self.skip), (b, block, share * self.skip)]

    def first(self):
        n = self.rows
        if self.order == "yxz":
            return [(n, self.two(1, None, True))]
        block = FAR_X if self.order[0] == "x" else FAR_Z
        return [(n // 2, self.two(2, block, True)), (n // 2, self.two(2, block, False))]

    def second(self):
        n, one = self.rows, self.arrived[0]
        if self.order == "yxz":
            return [(n // 2, self.two(2, FAR_X, False) + [(one, FAR_X, 0)])]
        if self.order == "xzy":
            return [
                (n // 4, self.two(4, QUARTER_FAR, True) + [(one, FAR_Z, 0)]),
                (n // 4, self.two(4, QUARTER_FAR, False) + [(one, FAR_Z, 2)]),
            ]
        if self.order == "xyz":
            return [(n // 2, self.two(2, X, True) + [(one, None, 0)])]
        return [(n // 2, self.two(2, Z, True) + [(one, None, 0)])]

    def third(self):
        n, (one, two) = self.rows, self.arrived
        if self.order == "yxz":
            return [(n // 4, self.two(4, QUARTER_FAR, False) + [(one, QUARTER_FAR, 0), (two, FAR_Z, 0)])]
        if self.order == "xzy":
            return [(n // 4, self.two(4, QUARTER_MINE, True) + [(one, Z, 0), (two, None, 0)])]
        if self.order == "xyz":
            return [(n // 4, self.two(4, QUARTER_FAR, False) + [(one, FAR_Z, 2), (two, FAR_Z, 0)])]
        return [(n // 4, self.two(4, TURNED_FAR, False) + [(one, FAR_X, 2), (two, FAR_X, 0)])]

    def fourth(self):
        n, (one, two, three) = self.rows, self.arrived
        if self.order == "yxz":
            return (n // 4, self.two(4, QUARTER_MINE, False) + [(one, QUARTER_MINE, 0), (two, Z, 0), (three, None, 0)])
        if self.order == "xzy":
            return (n // 4, self.two(4, QUARTER_MINE, False) + [(one, Z, 2), (two, None, 1), (three, None, 0)])
        if self.order == "xyz":
            return (n // 4, self.two(4, QUARTER_MINE, False) + [(one, Z, 2), (two, Z, 0), (three, None, 0)])
        return (n // 4, self.two(4, TURNED_MINE, False) + [(one, X, 2), (two, X, 0), (three, None, 0)])

    def send(self, value, step):
        axis = self.order[step]
        arrived = swap(value, "seq", 2) if axis == "y" else swap(value, "dp", 1 if axis == "x" else 2)
        self.arrived = (self.arrived if step else []) + [arrived]
        return arrived


class Payload:
    def __init__(self, sv, name, *pieces, micros=0.05):
        self.sv, self.name, self.pieces, self.micros = sv, name, list(pieces), micros

    def step(self, number, after):
        outs = [(p.first, p.second, p.third)[number]() for p in self.pieces]
        sent = add_up(self.sv, outs, after, f"{self.name}_{number + 1}", self.micros)
        return sent, [p.send(value, number) for p, value in zip(self.pieces, sent)]

    def far_z(self, after):
        (self.sum,) = add_up(self.sv, [[p.fourth() for p in self.pieces]], after, self.name + "_4", self.micros)
        self.arrived = swap(self.sum, "dp", 4)
        return [self.sum], [self.arrived]

    def back(self, after):
        rows = self.sum.shape[0]
        (own,) = add_up(self.sv, [[(rows, [(self.sum, None, 0), (self.arrived, None, 0)])]], after, self.name + "_5")
        across = swap(own, "dp", 2)
        self.gathered = [own, across, swap(own, "dp", 1), swap(across, "dp", 1)]
        return [own], self.gathered[1:]

    def psum(self):
        gathered = []
        for p in self.pieces:
            terms = p.two(1, None, False) + [(p.arrived[0], None, 0)]
            (out,) = add_up(self.sv, [[(p.rows, terms)]], [], self.name + "_all")
            out, quarter = lax.psum(out, "dp"), p.rows // 4
            places = [self.sv[QUARTER_MINE] ^ d for d in range(4)]
            gathered.append([lax.dynamic_slice_in_dim(out, place * quarter, quarter, 0) for place in places])
        self.gathered = [jnp.concatenate(parts, 0) for parts in zip(*gathered)]

    def layout(self):
        return [(p.order, p.rows) for p in self.pieces]


def share(arrays):
    return [arrays[2], arrays[3], swap(arrays[0], "seq", 1), swap(arrays[1], "seq", 1)]


def copy_kernel(sv, in_ref, out_ref):
    out_ref[...] = in_ref[...]


def copy_rows(sv, array, part, after, name):
    ins = [(array, (PART, WIDTH), lambda i, sv: (part, 0))]
    return launch(copy_kernel, sv, (1,), ins, [out_whole((PART, WIDTH), array.dtype)], after=after, name=name)[0]


def order_pieces(sv, layout, refs, whole_ref):
    low = 0
    for order, rows in layout:
        quarter = rows // 4
        for d, ref in enumerate(refs):
            place = (sv[TURNED_MINE] ^ (0, 2, 1, 3)[d]) if order == "zyx" else (sv[QUARTER_MINE] ^ d)
            at = pl.multiple_of(low + place * quarter, 16)
            whole_ref[pl.ds(at, quarter), :] = ref[low // 4 : low // 4 + quarter, :]
        low += rows


def slab(whole_ref, at, rows):
    return whole_ref[at : at + rows, :].astype(F32)


def finish_ff_kernel(layout, sv, *refs):
    w1_ref, w2_ref, whole_ref = refs[-3:]
    order_pieces(sv, layout, refs[:4], whole_ref)
    for g in range(GROUPS):
        low = FF_ROWS * g
        for i in range(6):
            w2_ref[BLOCK * g : BLOCK * g + BLOCK, 128 * i : 128 * i + 128] = slab(whole_ref, low + 8 * QUARTER + BLOCK * i, BLOCK)
        for i in range(8):
            at = BLOCK * (GROUPS * (i // 2) + g) + 128 * (i % 2)
            w1_ref[:, at : at + 128] = slab(whole_ref, low + QUARTER * i, QUARTER)


def finish_ff(sv, payload, after):
    return launch(
        functools.partial(finish_ff_kernel, payload.layout()),
        sv,
        (1,),
        [whole(part) for part in payload.gathered],
        [out_whole((QUARTER, FF), F32), out_whole((FF // 4, WIDTH), F32)],
        scratch=[pltpu.VMEM((GROUPS * FF_ROWS, 128), BF16)],
        after=after,
        limit=20,
        name="finish_ff",
    )


def finish_rest_kernel(layout, sv, *refs):
    proj_ref, qkv_ref, vec_ref, b1_ref, whole_ref = refs[-5:]
    order_pieces(sv, layout, refs[:4], whole_ref)
    for i in range(6):
        proj_ref[:, 128 * i : 128 * i + 128] = slab(whole_ref, i * QUARTER, QUARTER)
    for i in range(9):
        at = WIDTH * (i // 3) + 128 * (i % 3)
        qkv_ref[:, at : at + 128] = slab(whole_ref, (6 + i) * QUARTER, QUARTER)
        at += WIDTH // 2
        qkv_ref[:, at : at + 128] = slab(whole_ref, (15 + i) * QUARTER, QUARTER)
    rows = slab(whole_ref, 24 * QUARTER, VEC_ROWS)
    vec_ref[...] = jnp.concatenate([rows[:16], rows[16:32, :64]], 1)
    b1_ref[...] = rows[32:40]


def finish_rest(sv, payload):
    return launch(
        functools.partial(finish_rest_kernel, payload.layout()),
        sv,
        (1,),
        [whole(part) for part in payload.gathered],
        [
            out_whole((QUARTER, WIDTH), F32),
            out_whole((QUARTER, 3 * WIDTH), F32),
            out_whole((16, QUARTER), F32),
            out_whole((8, 128), F32),
        ],
        scratch=[pltpu.VMEM((24 * QUARTER + VEC_ROWS, 128), BF16)],
        limit=16,
        name="finish_rest",
    )


def per_device(
    patches, mask, mask_token, ln1_gain, ln1_bias, w_qkv, bias_q, bias_v, w_proj, bias_proj, scale_attn,
    ln2_gain, ln2_bias, w_fc1, bias_fc1, w_fc2, bias_fc2, scale_ffn, cotangent,
):
    slot_rows, images_here, width = patches.shape
    parts = lax.axis_size("seq")
    assert parts == 4 and images_here == 2 and width == WIDTH
    s = lax.axis_index("seq")
    dp = lax.axis_index("dp")
    y, core = s // 2, s % 2
    x, z = dp % 2, dp // 2 % 2

    def live_count(part):
        lead = (part == 0).astype(jnp.int32)
        return lead + (GRID // parts + (part < GRID % parts).astype(jnp.int32)) * GRID

    sv = jnp.stack(
        [core, y, 1 - y, x, 1 - x, z, 1 - z, 2 * x + z, 2 * x + 1 - z, 2 * z + x, 2 * z + 1 - x]
        + [live_count(s), live_count(s ^ 2), live_count(s ^ 1), live_count(s ^ 3)]
    ).astype(jnp.int32)
    table = jnp.concatenate(
        [
            bias_q, jnp.zeros_like(bias_q), bias_v, ln1_gain, ln1_bias, ln2_gain, ln2_bias, scale_attn, scale_ffn,
            bias_proj, bias_fc2, bias_fc1,
        ]
    ).astype(F32)[None, :]
    gain1, _shift1, gain2, shift2, sattn, sffn, bproj, b2 = [row_of(table, i) for i in range(3, 11)]

    chosen = mask[:, :, None] == 1
    entered = jnp.where(chosen, mask_token, patches)
    grow = ((0, PART - slot_rows), (0, 0))
    image = lambda array, i: lax.dynamic_index_in_dim(array, i, 1, keepdims=False)
    x1 = swap(jnp.pad(image(entered, 1 - y), grow), "seq", 2)
    x0 = jnp.pad(image(entered, y), grow)
    xb0 = swap(x0, "seq", 1)
    xb1 = swap(x1, "seq", 1)
    d_rows = jnp.concatenate(
        [
            jnp.where(chosen, cotangent, jnp.zeros_like(cotangent)),
            jnp.broadcast_to(chosen, (slot_rows, images_here, 128)).astype(BF16),
        ],
        -1,
    )
    d1 = swap(jnp.pad(image(d_rows, 1 - y), grow), "seq", 2)
    d0 = jnp.pad(image(d_rows, y), grow)

    own_first = qkv_part(True, 0, x0, table, w_qkv, [])
    other_first = qkv_part(False, 0, xb0, table, w_qkv, [])
    joined_a, normed, entered_a = qkv_part(True, 1, x1, table, w_qkv, own_first)
    (joined_b,) = qkv_part(False, 1, xb1, table, w_qkv, other_first)
    mixed, lse = attend(sv, joined_a, joined_b)
    fused = lax.axis_size("dp") == 8
    branch, branch2, g, gb1, dout, *shares = feed_forward(
        sv, mixed, entered_a, d0, d1, w_proj, [bproj, sattn, gain2, shift2, sffn], w_fc1, table, w_fc2
    )
    shares = share(shares)
    orders = ("yxz", "xzy", "zyx") if fused else ("yxz",) * 3
    ff = Payload(sv, "ff", *[Piece(orders[i], shares, FF_ROWS, i) for i in range(GROUPS)], micros=10)

    def far_rows(array, after, name):
        return swap(copy_rows(sv, array, 1, after, name), "seq", 2)

    def place_rows(array, far):
        near, far = array[:slot_rows, None], far[:slot_rows, None]
        return jnp.where(y == 0, jnp.concatenate([near, far], 1), jnp.concatenate([far, near], 1))

    out_a, d_middle, d_branch, d_mixed, vec_a = ff_tail(
        sv, branch2, g, branch, entered_a, dout, w_proj, [b2, sffn, sattn, gain2], []
    )
    sent, arrived = ff.step(0, [d_mixed])
    dq1, dka1, dva1, dkb1, dvb1 = attend_back(sv, 0, joined_a, joined_b, mixed, d_mixed, lse, sent)
    rk1, rv1 = swap(dkb1, "seq", 1), swap(dvb1, "seq", 1)
    dq2, dka2, dva2, dkb2, dvb2 = attend_back(sv, 1, joined_a, joined_b, mixed, d_mixed, lse, [dq1])
    rk2, rv2 = swap(dkb2, "seq", 1), swap(dvb2, "seq", 1)
    sent = [dq2]
    if fused:
        sent, arrived = ff.step(1, [dq2] + arrived)
    *shares, dkey1, dvalue1 = first_grads(sv, mixed, d_branch, normed, [dq1, dka1, rk1, dva1, rv1], sent)
    pd = Payload(sv, "first", Piece("yxz", share(shares), shares[0].shape[0]))
    second_parts = [dq2, dka2, rk2, dva2, rv2]
    grad_a, vec_b = entry_back(
        sv, [dq1, dkey1, dvalue1] + second_parts, w_qkv, entered_a, d_middle, dout, gain1, [dkey1]
    )
    sent, arrived_d = pd.step(0, [vec_b])
    if fused:
        sent, arrived = ff.step(2, sent + arrived)
    shares = second_grads(sv, normed, second_parts, [vec_a, vec_b, gb1], sent)
    pe = Payload(sv, "second", Piece("xyz" if fused else "yxz", share(shares), shares[0].shape[0]))
    if fused:
        sent, arrived = ff.far_z([shares[3]] + arrived)
        sent, arrived_e = pe.step(0, sent)
        out_far = far_rows(out_a, sent, "layer_out_far")
        both = Payload(sv, "both", *pd.pieces, *pe.pieces)
        sent, more = both.step(1, sent + arrived_d + arrived_e)
        grad_far = far_rows(grad_a, sent, "input_grad_far")
        layer_out = place_rows(out_a, out_far)
        sent, more = both.step(2, sent + more + [layer_out])
        sent, arrived = ff.back(sent + arrived)
        both.micros = 10
        sent, more = both.far_z(sent + more)
        input_grad = place_rows(grad_a, grad_far)
        sent, more = both.back(sent + more + [input_grad])
        grad_w1, grad_w2 = finish_ff(sv, ff, sent + arrived)
    else:
        pe.step(0, [])
        both = Payload(sv, "both", *pd.pieces, *pe.pieces)
        ff.psum()
        both.psum()
        grad_w1, grad_w2 = finish_ff(sv, ff, [])
        layer_out = place_rows(out_a, far_rows(out_a, [], "layer_out_far"))
        input_grad = place_rows(grad_a, far_rows(grad_a, [], "input_grad_far"))
    grad_proj, grad_qkv, vectors, wide_b1 = finish_rest(sv, both)
    grad_b1 = wide_b1[:6].reshape(WIDTH)

    return (
        layer_out, input_grad,
        vectors[8], vectors[9], vectors[10], grad_qkv, vectors[11], vectors[12], grad_proj,
        vectors[5], vectors[4], vectors[2], vectors[3], grad_w1, grad_b1, grad_w2, vectors[1], vectors[0],
    )


def solution(mesh):
    rows, flat = P("seq", "dp", None), P("seq")
    deep = P("seq", None)
    return jax.shard_map(
        per_device,
        mesh=mesh,
        in_specs=(rows, P("seq", "dp")) + (P(),) * 16 + (rows,),
        out_specs=(
            rows, rows, flat, flat, flat, deep, flat, flat, deep, flat, flat, flat, flat, deep, flat, deep, flat, flat,
        ),
        check_vma=False,
    )
```

```python
import functools

import jax
import jax.numpy as jnp
from jax import lax
from jax.experimental import pallas as pl
from jax.experimental.pallas import tpu as pltpu
from jax.sharding import PartitionSpec as P

HEADS = 12
GRID = 30
WIDTH = 768
FF = 3072
PART = 256
OWN = 512
GROUPS = 3
EPS = 1e-6
LOG2E = 1.4426950408889634
LN2 = 0.6931471805599453
BF16 = jnp.bfloat16
F32 = jnp.float32
ANY = pl.BlockSpec(memory_space=pl.ANY)
SMEM = pl.BlockSpec(memory_space=pltpu.SMEM)
MIB = 1024 * 1024


def params(limit=58):
    return pltpu.CompilerParams(vmem_limit_bytes=limit * MIB)


def launch(kernel, sv, grid, ins, outs, scratch=(), alias=None, after=(), limit=8, micros=0.05, name=None):
    alias = alias or {}
    after = list(after)
    count = len(ins)

    def body(sv_ref, *refs):
        kernel(sv_ref, *refs[:count], *refs[count + len(after) :])

    spec = lambda block, index: ANY if block is None else pl.BlockSpec(block, index)
    return pl.pallas_call(
        body,
        grid_spec=pltpu.PrefetchScalarGridSpec(
            num_scalar_prefetch=1,
            grid=grid,
            in_specs=[spec(b, i) for _, b, i in ins] + [ANY] * len(after),
            out_specs=[spec(b, i) for _, _, b, i in outs],
            scratch_shapes=list(scratch),
        ),
        out_shape=[shape_of(d, t) for d, t, _, _ in outs],
        input_output_aliases={1 + k: v for k, v in alias.items()},
        compiler_params=params(limit),
        cost_estimate=cost(micros),
        name=name,
    )(sv, *[a for a, _, _ in ins], *after)


def whole(array):
    dims = array.shape
    return (array, dims, lambda *_: (0,) * len(dims))


def row_of(table, index):
    return (table, (1, WIDTH), lambda *_: (0, index))


def out_whole(dims, dtype):
    return (dims, dtype, dims, lambda *_: (0,) * len(dims))


def cost(micros):
    return pl.CostEstimate(flops=int(micros * 1.15e9), bytes_accessed=0, transcendentals=0)


def shape_of(dims, dtype):
    return jax.ShapeDtypeStruct(dims, dtype)


def full(dims):
    return pl.BlockSpec(dims, lambda *_: (0,) * len(dims))


def dot(left, right):
    return jnp.dot(left, right, preferred_element_type=F32)


def dot_nt(left, right):
    return lax.dot_general(left, right, (((1,), (1,)), ((), ())), preferred_element_type=F32)


def dot_tn(left, right):
    return lax.dot_general(left, right, (((0,), (0,)), ((), ())), preferred_element_type=F32)


def norm_parts(values):
    centred = values - jnp.mean(values, -1, keepdims=True)
    rho = lax.rsqrt(jnp.mean(centred * centred, -1, keepdims=True) + EPS)
    return centred * rho, rho


def qkv_kernel(own, sv, x_ref, gain_ref, shift_ref, w_ref, bias_ref, *rest):
    if own:
        joined_ref, normed_ref, entered_ref, kept = rest[-4:]
    else:
        joined_ref, kept = rest[-2:]

    @pl.when(pl.program_id(0) == 0)
    def _():
        x = x_ref[...]
        n, _rho = norm_parts(x.astype(F32))
        kept[...] = (n * gain_ref[...] + shift_ref[...]).astype(BF16)
        if own:
            normed_ref[...] = kept[...]
            entered_ref[...] = x

    joined_ref[...] = (dot(kept[...], w_ref[...]) + bias_ref[...]).astype(BF16)


def qkv_part(own, half, x, table, w_qkv, previous, after=()):
    steps, off = (3, 0) if own else (2, 1)
    outs = [((OWN, steps * WIDTH), BF16, (PART, WIDTH), lambda j, sv: (half, j))]
    if own:
        outs += [((OWN, WIDTH), BF16, (PART, WIDTH), lambda j, sv: (half, 0))] * 2
    previous = list(previous)
    return launch(
        functools.partial(qkv_kernel, own),
        jnp.zeros((1,), jnp.int32),
        (steps,),
        [
            whole(x),
            row_of(table, 3),
            row_of(table, 4),
            (w_qkv, (WIDTH, WIDTH), lambda j, sv: (0, j + off)),
            (table, (1, WIDTH), lambda j, sv: (0, j + off)),
        ]
        + [(p, None, None) for p in previous],
        outs,
        scratch=[pltpu.VMEM((PART, WIDTH), BF16)],
        alias={5 + i: i for i in range(len(previous))},
        after=after,
        limit=10,
        micros=4,
        name="qkv_own" if own else "qkv_other",
    )


DEAD_FROM = 208


def lane_half(values, which):
    lane = lax.broadcasted_iota(jnp.int32, values.shape, 1)
    keep = (lane < 64) if which == 0 else (lane >= 64)
    return jnp.where(keep, values.astype(F32), 0.0).astype(BF16)


def live_scores(scores, count):
    tail = scores[DEAD_FROM:]
    row = lax.broadcasted_iota(jnp.int32, tail.shape, 0) + DEAD_FROM
    return jnp.concatenate([scores[:DEAD_FROM], jnp.where(row < count, tail, -1e30)], 0)


PAIRS = 3


class Pair:
    def __init__(self, pair, q_ref, ka_ref, kb_ref, va_ref, vb_ref):
        self.at = slice(128 * pair, 128 * pair + 128)
        self.q = [lane_half(q_ref[:, self.at], i) for i in range(2)]
        self.k = jnp.concatenate([ka_ref[:, self.at], kb_ref[:, self.at]], 0)
        self.v = jnp.concatenate([va_ref[:, self.at], vb_ref[:, self.at]], 0)


def blocks(scores, sv):
    return [live_scores(scores[PART * i : PART * i + PART], sv[COUNTS + i]) for i in range(4)]


def ahead(count, first, then):
    waiting = first(0)
    for i in range(count):
        now, waiting = waiting, first(i + 1) if i + 1 < count else None
        then(i, now)


def attend_kernel(sv, q_ref, ka_ref, kb_ref, va_ref, vb_ref, mixed_ref, lse_ref):
    scale = 0.125 * LOG2E
    pairs, heads = {}, []

    def first(i):
        if i % 2 == 0:
            pairs[i // 2] = Pair(i // 2, q_ref, ka_ref, kb_ref, va_ref, vb_ref)
            pairs[i // 2].vt = pairs[i // 2].v.T
        pair = pairs[i // 2]
        return blocks(dot_nt(pair.k, pair.q[i % 2]), sv)

    def then(i, scores):
        which, pair = i % 2, pairs[i // 2]
        top = scores[0]
        for block in scores[1:]:
            top = jnp.maximum(top, block)
        top = jnp.max(top, 0, keepdims=True)
        total = jnp.zeros((1, OWN), F32)
        out = jnp.zeros((64, OWN), F32)
        for b, block in enumerate(scores):
            p = jnp.exp2((block - top) * scale)
            total += jnp.sum(p, 0, keepdims=True)
            out += dot(pair.vt[64 * which : 64 * which + 64, PART * b : PART * b + PART], p.astype(BF16))
        lse_ref[i // 2, which : which + 1, :] = top * scale + jnp.log(total) * LOG2E
        heads.append(out / total)
        if which == 1:
            mixed_ref[:, pair.at] = jnp.concatenate(heads[-2:], 0).T.astype(BF16)

    ahead(2 * PAIRS, first, then)


def attend(sv, joined_a, joined_b):
    steps = HEADS // 2 // PAIRS
    wide = lambda array, off: (array, (OWN, 128 * PAIRS), lambda h, sv: (0, off * steps + h))
    return launch(
        attend_kernel,
        sv,
        (steps,),
        [wide(joined_a, 0), wide(joined_a, 1), wide(joined_b, 0), wide(joined_a, 2), wide(joined_b, 1)],
        [
            ((OWN, WIDTH), BF16, (OWN, 128 * PAIRS), lambda h, sv: (0, h)),
            ((HEADS // 2, 2, OWN), F32, (PAIRS, 2, OWN), lambda h, sv: (h, 0, 0)),
        ],
        limit=18,
        name="attend",
    )


def attend_back_kernel(
    sv, q_ref, ka_ref, kb_ref, va_ref, vb_ref, mixed_ref, dmix_ref, lse_ref,
    dq_ref, dka_ref, dva_ref, dkb_ref, dvb_ref,
):
    scale = 0.125 * LOG2E
    pairs, held = {}, []

    def first(i):
        if i % 2 == 0:
            pair = pairs[i // 2] = Pair(i // 2, q_ref, ka_ref, kb_ref, va_ref, vb_ref)
            dmix = dmix_ref[:, pair.at]
            product = (mixed_ref[:, pair.at].astype(F32) * dmix.astype(F32)).T
            pair.delta = [jnp.sum(product[64 * w : 64 * w + 64], 0, keepdims=True) for w in range(2)]
            pair.d = [lane_half(dmix, w) for w in range(2)]
            pair.kt = pair.k.T
        pair = pairs[i // 2]
        return dot_nt(pair.k, pair.q[i % 2]), dot_nt(pair.v, pair.d[i % 2])

    def then(i, products):
        which, pair = i % 2, pairs[i // 2]
        weights, backs = [], []
        for b, scores in enumerate(blocks(products[0], sv)):
            p = jnp.exp2(scores * scale - lse_ref[i // 2, which : which + 1, :])
            weights.append(p.astype(BF16))
            backs.append((p * (products[1][PART * b : PART * b + PART] - pair.delta[which])).astype(BF16))
        weights, backs = jnp.concatenate(weights, 0), jnp.concatenate(backs, 0)
        dv, dk = dot(weights, pair.d[which]), dot(backs, pair.q[which])
        dq = dot(pair.kt[64 * which : 64 * which + 64], backs)
        if which == 0:
            held[:] = [dv, dk, dq]
            return
        dv, dk = dv + held[0], (dk + held[1]) * 0.125
        dka_ref[:, pair.at], dkb_ref[:, pair.at] = dk[:OWN].astype(BF16), dk[OWN:].astype(BF16)
        dva_ref[:, pair.at], dvb_ref[:, pair.at] = dv[:OWN].astype(BF16), dv[OWN:].astype(BF16)
        dq_ref[:, pair.at] = (jnp.concatenate([held[2], dq], 0) * 0.125).T.astype(BF16)

    ahead(2 * PAIRS, first, then)


def attend_back(sv, half, joined_a, joined_b, mixed, d_mixed, lse, after):
    steps = HEADS // 2 // PAIRS
    wide = lambda array, off: (array, (OWN, 128 * PAIRS), lambda h, sv: (0, off * steps + half))
    return launch(
        attend_back_kernel,
        sv,
        (1,),
        [
            wide(joined_a, 0), wide(joined_a, 1), wide(joined_b, 0), wide(joined_a, 2), wide(joined_b, 1),
            wide(mixed, 0), wide(d_mixed, 0),
            (lse, (PAIRS, 2, OWN), lambda h, sv: (half, 0, 0)),
        ],
        [out_whole((OWN, WIDTH // 2), BF16)] * 5,
        after=after,
        limit=18,
        name=f"attend_back_{half}",
    )


QUARTER = WIDTH // 4


def rows_of(array):
    return (array, (PART, array.shape[1]), lambda i, sv: (i, 0))


def out_rows(wide, dtype):
    return ((OWN, wide), dtype, (PART, wide), lambda i, sv: (i, 0))


def gelu_pair(u):
    z = jnp.abs(u) * 0.7071067811865476
    t = 1.0 / (1.0 + 0.3275911 * z)
    e = jnp.exp2(u * u * (-0.5 * LOG2E))
    series = t * (
        0.5 * 0.254829592
        + t * (0.5 * -0.284496736 + t * (0.5 * 1.421413741 + t * (0.5 * -1.453152027 + t * (0.5 * 1.061405429))))
    )
    tail = series * e
    below = jnp.where(u >= 0, 1.0 - tail, tail)
    return u * below, below + u * e * 0.3989422804014327


def step_part(j, sv):
    return 2 * jnp.where(lax.rem(j, 2) == 0, sv[FAR_Y], sv[Y]) + jnp.where(j < 2, 1 - sv[CORE], sv[CORE])


BLOCK = FF // 4 // GROUPS
FF_ROWS = 8 * QUARTER + 6 * BLOCK


def ff_head(sv, ins, branch_ref, dout_ref, second_ref, secondt_ref, dbt_ref):
    mixed_ref, entered_ref, d0_ref, d1_ref, wproj_ref, bias_ref, sattn_ref, gain_ref, shift_ref, sffn_ref = ins
    branch = dot(mixed_ref[...], wproj_ref[...]) + bias_ref[...]
    branch_ref[...] = branch
    n, _rho = norm_parts(entered_ref[...].astype(F32) + sattn_ref[...] * branch)
    second = (n * gain_ref[...] + shift_ref[...]).astype(BF16)
    second_ref[...] = second
    turned = second.T
    for part in range(4):
        place = jnp.where(part % 2 != sv[CORE], 0, 2) + jnp.where(part // 2 != sv[Y], 0, 1)
        secondt_ref[pl.ds(pl.multiple_of(place * QUARTER, 16), QUARTER), :] = turned[
            QUARTER * part : QUARTER * part + QUARTER
        ]
    dout_ref[:PART, :], dout_ref[PART:, :] = d0_ref[...], d1_ref[...]
    dbt_ref[...] = (dout_ref[:, :WIDTH].astype(F32) * sffn_ref[...]).astype(BF16)


def ff_kernel(opens, sv, *refs):
    weights = [refs[3 * i : 3 * i + 3] for i in range(4)]
    branch2_ref, grad_ref, gb1_ref, *shares = refs[-7:]
    if opens:
        head = refs[22:27]
        second_ref, secondt_ref, dbt_ref = head[2:]
    else:
        second_ref, secondt_ref, dbt_ref = refs[12:15]

    @pl.when(pl.program_id(0) == 0)
    def _():
        if opens:
            ff_head(sv, refs[12:22], *head)
            branch2_ref[...] = jnp.zeros((OWN, WIDTH), F32)
            grad_ref[...] = jnp.zeros((OWN, WIDTH), F32)
        else:
            branch2_ref[...] = refs[15][...]
            grad_ref[...] = refs[16][...]

    hidden, d_pre = [], []

    def first(i):
        w1_ref, b1_ref, w2_ref = weights[i]
        return dot(second_ref[...], w1_ref[...]) + b1_ref[...], dot_nt(dbt_ref[...], w2_ref[...])

    def then(i, products):
        value, slope = gelu_pair(products[0])
        hidden.append(value.astype(BF16))
        d_pre.append((products[1] * slope).astype(BF16))
        spot = pl.ds(pl.multiple_of(step_part(i, sv) * BLOCK, BLOCK), BLOCK)
        gb1_ref[:, spot] = jnp.sum(d_pre[-1].astype(F32), 0, keepdims=True)

    ahead(4, first, then)
    hidden, d_pre = jnp.concatenate(hidden, 1), jnp.concatenate(d_pre, 1)
    gw1 = dot(secondt_ref[...], d_pre).astype(BF16)
    for i in range(4):
        for k in range(2):
            spot = pl.ds(pl.multiple_of((2 * step_part(i, sv) + k) * QUARTER, 16), QUARTER)
            at = BLOCK * i + 128 * k
            for ref, row in zip(shares, range(0, WIDTH, QUARTER)):
                ref[spot, :] = gw1[row : row + QUARTER, at : at + 128]
    gw2 = dot_tn(hidden, dbt_ref[...]).astype(BF16)
    for i in range(4):
        for k in range(6):
            low = 8 * QUARTER + BLOCK * k
            shares[i][low : low + BLOCK, :] = gw2[BLOCK * i : BLOCK * i + BLOCK, 128 * k : 128 * k + 128]
    branch2_ref[...] += dot(hidden, jnp.concatenate([w[2][...] for w in weights], 0))
    grad_ref[...] += dot_nt(d_pre, jnp.concatenate([w[0][...] for w in weights], 1))


def feed_forward(sv, groups, others, w1, table, w2, opens):
    streamed = []
    for i in range(4):
        at = lambda g, sv, i=i: GROUPS * step_part(i, sv) + g + groups[0]
        streamed += [
            (w1, (WIDTH, BLOCK), lambda g, sv, at=at: (0, at(g, sv))),
            (table, (1, BLOCK), lambda g, sv, at=at: (0, 11 * GROUPS + at(g, sv))),
            (w2, (BLOCK, WIDTH), lambda g, sv, at=at: (at(g, sv), 0)),
        ]
    count = len(groups)
    head = [
        out_whole((OWN, WIDTH), F32),
        out_whole((OWN, WIDTH + 128), BF16),
        out_whole((OWN, WIDTH), BF16),
        out_whole((WIDTH, OWN), BF16),
        out_whole((OWN, WIDTH), BF16),
    ]
    return launch(
        functools.partial(ff_kernel, opens),
        sv,
        (count,),
        streamed + [o if isinstance(o, tuple) else whole(o) for o in others],
        (head if opens else [])
        + [
            out_whole((OWN, WIDTH), F32),
            out_whole((OWN, WIDTH), F32),
            ((1, 4 * BLOCK * count), F32, (1, 4 * BLOCK), lambda g, sv: (0, g)),
            *[((count * FF_ROWS, 128), BF16, (FF_ROWS, 128), lambda g, sv: (g, 0))] * 4,
        ],
        limit=20,
        name=f"feed_forward_{groups[0]}",
    )


def tail_kernel(
    sv, branch2_ref, g_ref, branch_ref, entered_ref, dout_ref, w_ref, b2_ref, sffn_ref, sattn_ref, gain_ref,
    out_ref, dmid_ref, dbr_ref, dmix_ref, vec_ref,
):
    branch_two = branch2_ref[...] + b2_ref[...]
    d_out = dout_ref[:, :WIDTH].astype(F32)
    branch = branch_ref[...]
    middle = entered_ref[...].astype(F32) + sattn_ref[...] * branch
    out_ref[...] = (middle + sffn_ref[...] * branch_two).astype(BF16)
    n, rho = norm_parts(middle)
    g = g_ref[...]
    scaled = g * gain_ref[...]
    d_middle = d_out + rho * (
        scaled - jnp.mean(scaled, -1, keepdims=True) - n * jnp.mean(scaled * n, -1, keepdims=True)
    )
    dmid_ref[...] = d_middle
    d_branch = (d_middle * sattn_ref[...]).astype(BF16)
    dbr_ref[...] = d_branch
    dmix_ref[...] = dot_nt(d_branch, w_ref[...]).astype(BF16)
    rounded = (d_out * sffn_ref[...]).astype(BF16).astype(F32)
    add_vectors(
        vec_ref,
        [d_out * branch_two, rounded, g * n, g, d_middle * branch, d_branch.astype(F32)],
    )


def add_vectors(vec_ref, values):
    rows = [jnp.sum(v, 0, keepdims=True) for v in values]
    vec = jnp.concatenate(rows + [jnp.zeros((8 - len(rows), WIDTH), F32)], 0)

    @pl.when(pl.program_id(0) == 0)
    def _():
        vec_ref[...] = vec

    @pl.when(pl.program_id(0) > 0)
    def _():
        vec_ref[...] += vec


def ff_tail(sv, branch2, g, branch, entered, dout, w_proj, vectors, after):
    return launch(
        tail_kernel,
        sv,
        (2,),
        [rows_of(a) for a in (branch2, g, branch, entered, dout)] + [whole(w_proj)] + list(vectors),
        [out_rows(WIDTH, BF16), out_rows(WIDTH, F32), out_rows(WIDTH, BF16), out_rows(WIDTH, BF16), out_whole((8, WIDTH), F32)],
        after=after,
        limit=16,
        name="ff_tail",
    )


def store_slabs(sv, kept, slabs, at, shares):
    for step, ref in enumerate(shares):
        rows = pl.ds(pl.multiple_of(step_part(step, sv) * QUARTER, 16), QUARTER)
        for i in range(slabs):
            lo = at + i * QUARTER
            ref[lo : lo + QUARTER, :] = kept[rows, 128 * i : 128 * i + 128].astype(BF16)


def first_grads_kernel(
    sv, mixed_ref, dbr_ref, normed_ref, dq_ref, dk_ref, rk_ref, dv_ref, rv_ref,
    *rest,
):
    *shares, dkey_ref, dvalue_ref, kept = rest
    kept[:, :WIDTH] = dot_tn(mixed_ref[...], dbr_ref[...])
    store_slabs(sv, kept, 6, 0, shares)
    d_key = (dk_ref[...].astype(F32) + rk_ref[...].astype(F32)).astype(BF16)
    d_value = (dv_ref[...].astype(F32) + rv_ref[...].astype(F32)).astype(BF16)
    dkey_ref[...] = d_key
    dvalue_ref[...] = d_value
    kept[...] = dot_tn(normed_ref[...], jnp.concatenate([dq_ref[...], d_key, d_value], 1))
    store_slabs(sv, kept, 9, 6 * QUARTER, shares)


def first_grads(sv, mixed, d_branch, normed, parts, after):
    rows = 15 * QUARTER
    return launch(
        first_grads_kernel,
        sv,
        (1,),
        [whole(a) for a in (mixed, d_branch, normed, *parts)],
        [out_whole((rows, 128), BF16)] * 4 + [out_whole((OWN, WIDTH // 2), BF16)] * 2,
        scratch=[pltpu.VMEM((WIDTH, 9 * 128), F32)],
        after=after,
        limit=18,
        name="first_grads",
    )


def second_grads_kernel(sv, normed_ref, dq_ref, dk_ref, rk_ref, dv_ref, rv_ref, *rest):
    *shares, dkey_ref, dvalue_ref, kept = rest
    d_key = (dk_ref[...].astype(F32) + rk_ref[...].astype(F32)).astype(BF16)
    d_value = (dv_ref[...].astype(F32) + rv_ref[...].astype(F32)).astype(BF16)
    dkey_ref[...] = d_key
    dvalue_ref[...] = d_value
    kept[...] = dot_tn(normed_ref[...], jnp.concatenate([dq_ref[...], d_key, d_value], 1))
    store_slabs(sv, kept, 9, 0, shares)


def second_grads(sv, normed, parts, after):
    rows = 9 * QUARTER
    return launch(
        second_grads_kernel,
        sv,
        (1,),
        [whole(a) for a in (normed, *parts)],
        [out_whole((rows, 128), BF16)] * 4 + [out_whole((OWN, WIDTH // 2), BF16)] * 2,
        scratch=[pltpu.VMEM((WIDTH, 9 * 128), F32)],
        after=after,
        limit=20,
        name="second_grads",
    )


VEC_ROWS = 128


def entry_kernel(
    sv, dq1_ref, dk1_ref, dv1_ref, dq2_ref, dk2_ref, dv2_ref, w_ref, entered_ref, dmid_ref, dout_ref, gain_ref,
    va_ref, b1a_ref, b1b_ref, grad_ref, *rest,
):
    *shares, vec_ref, spread = rest
    dq = jnp.concatenate([dq1_ref[...], dq2_ref[...]], 1)
    dk = jnp.concatenate([dk1_ref[...], dk2_ref[...]], 1)
    dv = jnp.concatenate([dv1_ref[...], dv2_ref[...]], 1)
    g = dot_nt(jnp.concatenate([dq, dk, dv], 1), w_ref[...])
    n, rho = norm_parts(entered_ref[...].astype(F32))
    scaled = g * gain_ref[...]
    d_entered = dmid_ref[...] + rho * (
        scaled - jnp.mean(scaled, -1, keepdims=True) - n * jnp.mean(scaled * n, -1, keepdims=True)
    )
    chosen = jnp.concatenate([dout_ref[:, WIDTH:].astype(F32)] * 6, 1)
    masked = d_entered * chosen
    grad_ref[...] = (d_entered - masked).astype(BF16)
    add_vectors(vec_ref, [masked, g * n, g, dq.astype(F32), dv.astype(F32)])

    @pl.when(pl.program_id(0) == 1)
    def _():
        vec = jnp.concatenate([va_ref[...], vec_ref[...]], 0)
        split = b1a_ref.shape[1]
        for part in range(4):
            at = QUARTER * part
            spots = [4 * BLOCK * g + BLOCK * part + 128 * i for g in range(GROUPS) for i in range(2)]
            b1 = [
                b1a_ref[:, spot : spot + 128] if spot < split else b1b_ref[:, spot - split : spot - split + 128]
                for spot in spots
            ]
            spread[part] = jnp.concatenate(
                [
                    vec[:, at : at + 128],
                    jnp.concatenate([vec[:, at + 128 : at + 192], jnp.zeros((16, 64), F32)], 1),
                    *b1,
                    jnp.zeros((VEC_ROWS - 38, 128), F32),
                ],
                0,
            )
        for step, ref in enumerate(shares):
            ref[...] = spread[step_part(step, sv)].astype(BF16)


def entry_back(sv, parts, w_qkv, entered, d_middle, dout, gain, vectors, after):
    return launch(
        entry_kernel,
        sv,
        (2,),
        [rows_of(p) for p in parts]
        + [whole(w_qkv), rows_of(entered), rows_of(d_middle), rows_of(dout), gain]
        + [whole(v) for v in vectors],
        [out_rows(WIDTH, BF16)] + [out_whole((VEC_ROWS, 128), BF16)] * 4,
        scratch=[pltpu.VMEM((8, WIDTH), F32), pltpu.VMEM((4, VEC_ROWS, 128), F32)],
        after=after,
        limit=20,
        micros=10,
        name="entry_back",
    )


CORE, Y, FAR_Y, X, FAR_X, Z, FAR_Z, QUARTER_MINE, QUARTER_FAR, TURNED_MINE, TURNED_FAR, COUNTS = range(12)


def swap(value, axis, distance):
    count = lax.axis_size(axis)
    return lax.ppermute(value, axis, [(i, i ^ distance) for i in range(count)])


def sums_kernel(plan, sv, *refs):
    count = sum(terms for _, _, parts in plan for _, terms in parts)
    ins, outs = list(refs[:count]), refs[count:]
    for (_, _, parts), out_ref in zip(plan, outs):
        low = 0
        for rows, terms in parts:
            total = ins.pop(0)[...].astype(F32)
            for _ in range(terms - 1):
                total += ins.pop(0)[...].astype(F32)
            out_ref[low : low + rows, :] = total.astype(BF16)
            low += rows


def add_up(sv, outs, after, name, micros=0.05):
    ins, plan, results = [], [], []
    for parts in outs:
        for rows, terms in parts:
            for array, block, skip in terms:
                at = lambda i, sv, block=block, skip=skip: (skip if block is None else sv[block] + skip, 0)
                ins.append((array, (rows, 128), at))
        total = sum(rows for rows, _ in parts)
        plan.append((None, None, [(rows, len(terms)) for rows, terms in parts]))
        results.append(out_whole((total, 128), BF16))
    return list(launch(functools.partial(sums_kernel, plan), sv, (1,), ins, results, after=after, limit=8, micros=micros, name=name))


class Piece:
    def __init__(self, order, kept, rows, skip=0):
        self.order, self.rows, self.skip = order, rows, skip
        self.far, self.near, self.core_far, self.core = kept

    def two(self, share, block, far):
        a, b = (self.far, self.core_far) if far else (self.near, self.core)
        return [(a, block, share * self.skip), (b, block, share * self.skip)]

    def first(self):
        n = self.rows
        if self.order == "yxz":
            return [(n, self.two(1, None, True))]
        block = FAR_X if self.order[0] == "x" else FAR_Z
        return [(n // 2, self.two(2, block, True)), (n // 2, self.two(2, block, False))]

    def second(self):
        n, one = self.rows, self.arrived[0]
        if self.order == "yxz":
            return [(n // 2, self.two(2, FAR_X, False) + [(one, FAR_X, 0)])]
        if self.order == "xzy":
            return [
                (n // 4, self.two(4, QUARTER_FAR, True) + [(one, FAR_Z, 0)]),
                (n // 4, self.two(4, QUARTER_FAR, False) + [(one, FAR_Z, 2)]),
            ]
        if self.order == "xyz":
            return [(n // 2, self.two(2, X, True) + [(one, None, 0)])]
        return [(n // 2, self.two(2, Z, True) + [(one, None, 0)])]

    def third(self):
        n, (one, two) = self.rows, self.arrived
        if self.order == "yxz":
            return [(n // 4, self.two(4, QUARTER_FAR, False) + [(one, QUARTER_FAR, 0), (two, FAR_Z, 0)])]
        if self.order == "xzy":
            return [(n // 4, self.two(4, QUARTER_MINE, True) + [(one, Z, 0), (two, None, 0)])]
        if self.order == "xyz":
            return [(n // 4, self.two(4, QUARTER_FAR, False) + [(one, FAR_Z, 2), (two, FAR_Z, 0)])]
        return [(n // 4, self.two(4, TURNED_FAR, False) + [(one, FAR_X, 2), (two, FAR_X, 0)])]

    def fourth(self):
        n, (one, two, three) = self.rows, self.arrived
        if self.order == "yxz":
            return (n // 4, self.two(4, QUARTER_MINE, False) + [(one, QUARTER_MINE, 0), (two, Z, 0), (three, None, 0)])
        if self.order == "xzy":
            return (n // 4, self.two(4, QUARTER_MINE, False) + [(one, Z, 2), (two, None, 1), (three, None, 0)])
        if self.order == "xyz":
            return (n // 4, self.two(4, QUARTER_MINE, False) + [(one, Z, 2), (two, Z, 0), (three, None, 0)])
        return (n // 4, self.two(4, TURNED_MINE, False) + [(one, X, 2), (two, X, 0), (three, None, 0)])

    def send(self, value, step):
        axis = self.order[step]
        arrived = swap(value, "seq", 2) if axis == "y" else swap(value, "dp", 1 if axis == "x" else 2)
        self.arrived = (self.arrived if step else []) + [arrived]
        return arrived


class Payload:
    def __init__(self, sv, name, *pieces, micros=0.05):
        self.sv, self.name, self.pieces, self.micros = sv, name, list(pieces), micros

    def step(self, number, after):
        outs = [(p.first, p.second, p.third)[number]() for p in self.pieces]
        sent = add_up(self.sv, outs, after, f"{self.name}_{number + 1}", self.micros)
        return sent, [p.send(value, number) for p, value in zip(self.pieces, sent)]

    def far_z(self, after):
        (self.sum,) = add_up(self.sv, [[p.fourth() for p in self.pieces]], after, self.name + "_4", self.micros)
        self.arrived = swap(self.sum, "dp", 4)
        return [self.sum], [self.arrived]

    def back(self, after):
        rows = self.sum.shape[0]
        (own,) = add_up(self.sv, [[(rows, [(self.sum, None, 0), (self.arrived, None, 0)])]], after, self.name + "_5")
        across = swap(own, "dp", 2)
        self.gathered = [own, across, swap(own, "dp", 1), swap(across, "dp", 1)]
        return [own], self.gathered[1:]

    def psum(self):
        gathered = []
        for p in self.pieces:
            terms = p.two(1, None, False) + [(p.arrived[0], None, 0)]
            (out,) = add_up(self.sv, [[(p.rows, terms)]], [], self.name + "_all")
            out, quarter = lax.psum(out, "dp"), p.rows // 4
            places = [self.sv[QUARTER_MINE] ^ d for d in range(4)]
            gathered.append([lax.dynamic_slice_in_dim(out, place * quarter, quarter, 0) for place in places])
        self.gathered = [jnp.concatenate(parts, 0) for parts in zip(*gathered)]

    def layout(self):
        return [(p.order, p.rows) for p in self.pieces]


def share(arrays):
    return [arrays[2], arrays[3], swap(arrays[0], "seq", 1), swap(arrays[1], "seq", 1)]


def copy_kernel(sv, in_ref, out_ref):
    out_ref[...] = in_ref[...]


def copy_rows(sv, array, part, after, name):
    ins = [(array, (PART, WIDTH), lambda i, sv: (part, 0))]
    return launch(copy_kernel, sv, (1,), ins, [out_whole((PART, WIDTH), array.dtype)], after=after, name=name)[0]


def order_pieces(sv, layout, refs, whole_ref):
    low = 0
    for order, rows in layout:
        quarter = rows // 4
        for d, ref in enumerate(refs):
            place = (sv[TURNED_MINE] ^ (0, 2, 1, 3)[d]) if order == "zyx" else (sv[QUARTER_MINE] ^ d)
            at = pl.multiple_of(low + place * quarter, 16)
            whole_ref[pl.ds(at, quarter), :] = ref[low // 4 : low // 4 + quarter, :]
        low += rows


def slab(whole_ref, at, rows):
    return whole_ref[at : at + rows, :].astype(F32)


def finish_ff_kernel(layout, sv, *refs):
    w1_ref, w2_ref, whole_ref = refs[-3:]
    order_pieces(sv, layout, refs[:4], whole_ref)
    for g in range(GROUPS):
        low = FF_ROWS * g
        for i in range(6):
            w2_ref[BLOCK * g : BLOCK * g + BLOCK, 128 * i : 128 * i + 128] = slab(whole_ref, low + 8 * QUARTER + BLOCK * i, BLOCK)
        for i in range(8):
            at = BLOCK * (GROUPS * (i // 2) + g) + 128 * (i % 2)
            w1_ref[:, at : at + 128] = slab(whole_ref, low + QUARTER * i, QUARTER)


def finish_ff(sv, payload, after):
    return launch(
        functools.partial(finish_ff_kernel, payload.layout()),
        sv,
        (1,),
        [whole(part) for part in payload.gathered],
        [out_whole((QUARTER, FF), F32), out_whole((FF // 4, WIDTH), F32)],
        scratch=[pltpu.VMEM((GROUPS * FF_ROWS, 128), BF16)],
        after=after,
        limit=20,
        micros=5,
        name="finish_ff",
    )


def finish_rest_kernel(layout, sv, *refs):
    proj_ref, qkv_ref, vec_ref, b1_ref, whole_ref = refs[-5:]
    order_pieces(sv, layout, refs[:4], whole_ref)
    for i in range(6):
        proj_ref[:, 128 * i : 128 * i + 128] = slab(whole_ref, i * QUARTER, QUARTER)
    for i in range(9):
        at = WIDTH * (i // 3) + 128 * (i % 3)
        qkv_ref[:, at : at + 128] = slab(whole_ref, (6 + i) * QUARTER, QUARTER)
        at += WIDTH // 2
        qkv_ref[:, at : at + 128] = slab(whole_ref, (15 + i) * QUARTER, QUARTER)
    rows = slab(whole_ref, 24 * QUARTER, VEC_ROWS)
    vec_ref[...] = jnp.concatenate([rows[:16], rows[16:32, :64]], 1)
    b1_ref[...] = rows[32:40]


def finish_rest(sv, payload, after):
    return launch(
        functools.partial(finish_rest_kernel, payload.layout()),
        sv,
        (1,),
        [whole(part) for part in payload.gathered],
        [
            out_whole((QUARTER, WIDTH), F32),
            out_whole((QUARTER, 3 * WIDTH), F32),
            out_whole((16, QUARTER), F32),
            out_whole((8, 128), F32),
        ],
        scratch=[pltpu.VMEM((24 * QUARTER + VEC_ROWS, 128), BF16)],
        after=after,
        limit=16,
        name="finish_rest",
    )


def per_device(
    patches, mask, mask_token, ln1_gain, ln1_bias, w_qkv, bias_q, bias_v, w_proj, bias_proj, scale_attn,
    ln2_gain, ln2_bias, w_fc1, bias_fc1, w_fc2, bias_fc2, scale_ffn, cotangent,
):
    slot_rows, images_here, width = patches.shape
    parts = lax.axis_size("seq")
    assert parts == 4 and images_here == 2 and width == WIDTH
    s = lax.axis_index("seq")
    dp = lax.axis_index("dp")
    y, core = s // 2, s % 2
    x, z = dp % 2, dp // 2 % 2

    def live_count(part):
        lead = (part == 0).astype(jnp.int32)
        return lead + (GRID // parts + (part < GRID % parts).astype(jnp.int32)) * GRID

    sv = jnp.stack(
        [core, y, 1 - y, x, 1 - x, z, 1 - z, 2 * x + z, 2 * x + 1 - z, 2 * z + x, 2 * z + 1 - x]
        + [live_count(s), live_count(s ^ 2), live_count(s ^ 1), live_count(s ^ 3)]
    ).astype(jnp.int32)
    table = jnp.concatenate(
        [
            bias_q, jnp.zeros_like(bias_q), bias_v, ln1_gain, ln1_bias, ln2_gain, ln2_bias, scale_attn, scale_ffn,
            bias_proj, bias_fc2, bias_fc1,
        ]
    ).astype(F32)[None, :]
    gain1, _shift1, gain2, shift2, sattn, sffn, bproj, b2 = [row_of(table, i) for i in range(3, 11)]

    chosen = mask[:, :, None] == 1
    entered = jnp.where(chosen, mask_token, patches)
    grow = ((0, PART - slot_rows), (0, 0))
    image = lambda array, i: lax.dynamic_index_in_dim(array, i, 1, keepdims=False)
    x1 = swap(jnp.pad(image(entered, 1 - y), grow), "seq", 2)
    x0 = jnp.pad(image(entered, y), grow)
    xb0 = swap(x0, "seq", 1)
    xb1 = swap(x1, "seq", 1)
    d_rows = jnp.concatenate(
        [
            jnp.where(chosen, cotangent, jnp.zeros_like(cotangent)),
            jnp.broadcast_to(chosen, (slot_rows, images_here, 128)).astype(BF16),
        ],
        -1,
    )
    d1 = swap(jnp.pad(image(d_rows, 1 - y), grow), "seq", 2)
    d0 = jnp.pad(image(d_rows, y), grow)

    own_first = qkv_part(True, 0, x0, table, w_qkv, [])
    other_first = qkv_part(False, 0, xb0, table, w_qkv, [])
    joined_a, normed, entered_a = qkv_part(True, 1, x1, table, w_qkv, own_first)
    (joined_b,) = qkv_part(False, 1, xb1, table, w_qkv, other_first)
    mixed, lse = attend(sv, joined_a, joined_b)
    fused = lax.axis_size("dp") == 8
    orders = ("yxz", "xzy", "zyx") if fused else ("yxz",) * 3
    branch, dout, second, secondt, dbt, branch2, g, gb1a, *shares = feed_forward(
        sv, (0, 1), [mixed, entered_a, d0, d1, w_proj, bproj, sattn, gain2, shift2, sffn], w_fc1, table, w_fc2, True
    )
    shares = share(shares)
    ff01 = Payload(sv, "ff01", *[Piece(orders[i], shares, FF_ROWS, i) for i in range(2)])
    branch2, g, gb1b, *shares = feed_forward(
        sv, (2,), [second, secondt, dbt, branch2, g], w_fc1, table, w_fc2, False
    )
    ff2 = Payload(sv, "ff2", Piece(orders[2], share(shares), FF_ROWS), micros=2)
    ff = Payload(sv, "ff", *ff01.pieces, *ff2.pieces, micros=10)

    def far_rows(array, after, name):
        return swap(copy_rows(sv, array, 1, after, name), "seq", 2)

    def place_rows(array, far):
        near, far = array[:slot_rows, None], far[:slot_rows, None]
        return jnp.where(y == 0, jnp.concatenate([near, far], 1), jnp.concatenate([far, near], 1))

    sent, arrived = ff01.step(0, [gb1b])
    out_a, d_middle, d_branch, d_mixed, vec_a = ff_tail(
        sv, branch2, g, branch, entered_a, dout, w_proj, [b2, sffn, sattn, gain2], sent
    )
    sent, more = ff2.step(0, [d_mixed])
    dq1, dka1, dva1, dkb1, dvb1 = attend_back(sv, 0, joined_a, joined_b, mixed, d_mixed, lse, sent)
    rk1, rv1 = swap(dkb1, "seq", 1), swap(dvb1, "seq", 1)
    dq2, dka2, dva2, dkb2, dvb2 = attend_back(sv, 1, joined_a, joined_b, mixed, d_mixed, lse, [dq1])
    rk2, rv2 = swap(dkb2, "seq", 1), swap(dvb2, "seq", 1)
    sent = [dq2]
    if fused:
        sent, arrived = ff01.step(1, sent + arrived)
        sent, more = ff2.step(1, sent + more)
    *shares, dkey1, dvalue1 = first_grads(sv, mixed, d_branch, normed, [dq1, dka1, rk1, dva1, rv1], sent)
    pd = Payload(sv, "first", Piece("yxz", share(shares), shares[0].shape[0]))
    *shares, dkey2, dvalue2 = second_grads(sv, normed, [dq2, dka2, rk2, dva2, rv2], [dkey1])
    pe = Payload(sv, "second", Piece("xyz" if fused else "yxz", share(shares), shares[0].shape[0]))
    sent = [dkey2]
    if fused:
        sent, arrived = ff.step(2, sent + arrived + more)
    sent, arrived_d = pd.step(0, sent)
    sent, arrived_e = pe.step(0, sent)
    grad_a, *shares = entry_back(
        sv, [dq1, dkey1, dvalue1, dq2, dkey2, dvalue2], w_qkv, entered_a, d_middle, dout, gain1, [vec_a, gb1a, gb1b], sent
    )
    pf = Payload(sv, "vec", Piece("yxz", share(shares), VEC_ROWS))
    sent = [grad_a]
    if fused:
        sent, arrived = ff.far_z(sent + arrived)
    sent, arrived_f = pf.step(0, sent)
    both = Payload(sv, "both", *pd.pieces, *pe.pieces, *pf.pieces)
    if fused:
        sent, more = both.step(1, sent + arrived_d + arrived_e + arrived_f)
        sent, arrived = ff.back(sent + arrived)
        sent, more = both.step(2, sent + more)
        both.micros = 10
        sent, more = both.far_z(sent + more)
        out_far = far_rows(out_a, sent, "layer_out_far")
        grad_far = far_rows(grad_a, [out_far], "input_grad_far")
        sent, more = both.back(sent + more + [arrived[1]])
        layer_out = place_rows(out_a, out_far)
        input_grad = place_rows(grad_a, grad_far)
        grad_w1, grad_w2 = finish_ff(sv, ff, sent + arrived)
    else:
        ff.psum()
        both.psum()
        grad_w1, grad_w2 = finish_ff(sv, ff, [])
        layer_out = place_rows(out_a, far_rows(out_a, [], "layer_out_far"))
        input_grad = place_rows(grad_a, far_rows(grad_a, [], "input_grad_far"))
    grad_proj, grad_qkv, vectors, wide_b1 = finish_rest(sv, both, [grad_w1, layer_out, input_grad])
    grad_b1 = wide_b1[:6].reshape(WIDTH)

    return (
        layer_out, input_grad,
        vectors[8], vectors[9], vectors[10], grad_qkv, vectors[11], vectors[12], grad_proj,
        vectors[5], vectors[4], vectors[2], vectors[3], grad_w1, grad_b1, grad_w2, vectors[1], vectors[0],
    )


def solution(mesh):
    rows, flat = P("seq", "dp", None), P("seq")
    deep = P("seq", None)
    return jax.shard_map(
        per_device,
        mesh=mesh,
        in_specs=(rows, P("seq", "dp")) + (P(),) * 16 + (rows,),
        out_specs=(
            rows, rows, flat, flat, flat, deep, flat, flat, deep, flat, flat, flat, flat, deep, flat, deep, flat, flat,
        ),
        check_vma=False,
    )
```

```python
import functools

import jax
import jax.numpy as jnp
from jax import lax
from jax.experimental import pallas as pl
from jax.experimental.pallas import tpu as pltpu
from jax.sharding import PartitionSpec as P

HEADS = 12
GRID = 30
WIDTH = 768
FF = 3072
PART = 256
OWN = 512
GROUPS = 3
EPS = 1e-6
LOG2E = 1.4426950408889634
LN2 = 0.6931471805599453
BF16 = jnp.bfloat16
F32 = jnp.float32
ANY = pl.BlockSpec(memory_space=pl.ANY)
SMEM = pl.BlockSpec(memory_space=pltpu.SMEM)
MIB = 1024 * 1024


def params(limit=58):
    return pltpu.CompilerParams(vmem_limit_bytes=limit * MIB)


def launch(kernel, sv, grid, ins, outs, scratch=(), alias=None, after=(), limit=8, micros=0.05, name=None):
    alias = alias or {}
    after = list(after)
    count = len(ins)

    def body(sv_ref, *refs):
        kernel(sv_ref, *refs[:count], *refs[count + len(after) :])

    spec = lambda block, index: ANY if block is None else pl.BlockSpec(block, index)
    return pl.pallas_call(
        body,
        grid_spec=pltpu.PrefetchScalarGridSpec(
            num_scalar_prefetch=1,
            grid=grid,
            in_specs=[spec(b, i) for _, b, i in ins] + [ANY] * len(after),
            out_specs=[spec(b, i) for _, _, b, i in outs],
            scratch_shapes=list(scratch),
        ),
        out_shape=[shape_of(d, t) for d, t, _, _ in outs],
        input_output_aliases={1 + k: v for k, v in alias.items()},
        compiler_params=params(limit),
        cost_estimate=cost(micros),
        name=name,
    )(sv, *[a for a, _, _ in ins], *after)


def whole(array):
    dims = array.shape
    return (array, dims, lambda *_: (0,) * len(dims))


def row_of(table, index):
    return (table, (1, WIDTH), lambda *_: (0, index))


def out_whole(dims, dtype):
    return (dims, dtype, dims, lambda *_: (0,) * len(dims))


def cost(micros):
    return pl.CostEstimate(flops=int(micros * 1.15e9), bytes_accessed=0, transcendentals=0)


def shape_of(dims, dtype):
    return jax.ShapeDtypeStruct(dims, dtype)


def full(dims):
    return pl.BlockSpec(dims, lambda *_: (0,) * len(dims))


def dot(left, right):
    return jnp.dot(left, right, preferred_element_type=F32)


def dot_nt(left, right):
    return lax.dot_general(left, right, (((1,), (1,)), ((), ())), preferred_element_type=F32)


def dot_tn(left, right):
    return lax.dot_general(left, right, (((0,), (0,)), ((), ())), preferred_element_type=F32)


def norm_parts(values):
    centred = values - jnp.mean(values, -1, keepdims=True)
    rho = lax.rsqrt(jnp.mean(centred * centred, -1, keepdims=True) + EPS)
    return centred * rho, rho


def qkv_kernel(own, sv, x_ref, gain_ref, shift_ref, w_ref, bias_ref, *rest):
    if own:
        joined_ref, normed_ref, entered_ref, kept = rest[-4:]
    else:
        joined_ref, kept = rest[-2:]

    @pl.when(pl.program_id(0) == 0)
    def _():
        x = x_ref[...]
        n, _rho = norm_parts(x.astype(F32))
        kept[...] = (n * gain_ref[...] + shift_ref[...]).astype(BF16)
        if own:
            normed_ref[...] = kept[...]
            entered_ref[...] = x

    joined_ref[...] = (dot(kept[...], w_ref[...]) + bias_ref[...]).astype(BF16)


def qkv_part(own, half, x, table, w_qkv, previous, after=()):
    steps, off = (3, 0) if own else (2, 1)
    outs = [((OWN, steps * WIDTH), BF16, (PART, WIDTH), lambda j, sv: (half, j))]
    if own:
        outs += [((OWN, WIDTH), BF16, (PART, WIDTH), lambda j, sv: (half, 0))] * 2
    previous = list(previous)
    return launch(
        functools.partial(qkv_kernel, own),
        jnp.zeros((1,), jnp.int32),
        (steps,),
        [
            whole(x),
            row_of(table, 3),
            row_of(table, 4),
            (w_qkv, (WIDTH, WIDTH), lambda j, sv: (0, j + off)),
            (table, (1, WIDTH), lambda j, sv: (0, j + off)),
        ]
        + [(p, None, None) for p in previous],
        outs,
        scratch=[pltpu.VMEM((PART, WIDTH), BF16)],
        alias={5 + i: i for i in range(len(previous))},
        after=after,
        limit=10,
        micros=4,
        name="qkv_own" if own else "qkv_other",
    )


DEAD_FROM = 208


def lane_half(values, which):
    lane = lax.broadcasted_iota(jnp.int32, values.shape, 1)
    keep = (lane < 64) if which == 0 else (lane >= 64)
    return jnp.where(keep, values.astype(F32), 0.0).astype(BF16)


def live_scores(scores, count):
    tail = scores[DEAD_FROM:]
    row = lax.broadcasted_iota(jnp.int32, tail.shape, 0) + DEAD_FROM
    return jnp.concatenate([scores[:DEAD_FROM], jnp.where(row < count, tail, -1e30)], 0)


PAIRS = 3


class Pair:
    def __init__(self, pair, q_ref, ka_ref, kb_ref, va_ref, vb_ref):
        self.at = slice(128 * pair, 128 * pair + 128)
        self.q = [lane_half(q_ref[:, self.at], i) for i in range(2)]
        self.k = jnp.concatenate([ka_ref[:, self.at], kb_ref[:, self.at]], 0)
        self.v = jnp.concatenate([va_ref[:, self.at], vb_ref[:, self.at]], 0)


def blocks(scores, sv):
    return [live_scores(scores[PART * i : PART * i + PART], sv[COUNTS + i]) for i in range(4)]


def ahead(count, first, then):
    waiting = first(0)
    for i in range(count):
        now, waiting = waiting, first(i + 1) if i + 1 < count else None
        then(i, now)


def attend_kernel(sv, q_ref, ka_ref, kb_ref, va_ref, vb_ref, mixed_ref, lse_ref):
    scale = 0.125 * LOG2E
    pairs, heads = {}, []

    def first(i):
        if i % 2 == 0:
            pairs[i // 2] = Pair(i // 2, q_ref, ka_ref, kb_ref, va_ref, vb_ref)
            pairs[i // 2].vt = pairs[i // 2].v.T
        pair = pairs[i // 2]
        return blocks(dot_nt(pair.k, pair.q[i % 2]), sv)

    def then(i, scores):
        which, pair = i % 2, pairs[i // 2]
        top = scores[0]
        for block in scores[1:]:
            top = jnp.maximum(top, block)
        top = jnp.max(top, 0, keepdims=True)
        total = jnp.zeros((1, OWN), F32)
        out = jnp.zeros((64, OWN), F32)
        for b, block in enumerate(scores):
            p = jnp.exp2((block - top) * scale)
            total += jnp.sum(p, 0, keepdims=True)
            out += dot(pair.vt[64 * which : 64 * which + 64, PART * b : PART * b + PART], p.astype(BF16))
        lse_ref[i // 2, which : which + 1, :] = top * scale + jnp.log(total) * LOG2E
        heads.append(out / total)
        if which == 1:
            mixed_ref[:, pair.at] = jnp.concatenate(heads[-2:], 0).T.astype(BF16)

    ahead(2 * PAIRS, first, then)


def attend(sv, joined_a, joined_b):
    steps = HEADS // 2 // PAIRS
    wide = lambda array, off: (array, (OWN, 128 * PAIRS), lambda h, sv: (0, off * steps + h))
    return launch(
        attend_kernel,
        sv,
        (steps,),
        [wide(joined_a, 0), wide(joined_a, 1), wide(joined_b, 0), wide(joined_a, 2), wide(joined_b, 1)],
        [
            ((OWN, WIDTH), BF16, (OWN, 128 * PAIRS), lambda h, sv: (0, h)),
            ((HEADS // 2, 2, OWN), F32, (PAIRS, 2, OWN), lambda h, sv: (h, 0, 0)),
        ],
        limit=18,
        name="attend",
    )


UNIT = 256


def attend_back_kernel(units, sv, *refs):
    scale = 0.125 * LOG2E
    ins = [refs[8 * u : 8 * u + 8] for u in range(units)]
    dq_ref, dka_ref, dva_ref, dkb_ref, dvb_ref = refs[8 * units :]
    pairs, held = {}, []

    def first(i):
        number = i // 2
        *unit, mixed_ref, dmix_ref, lse_ref = ins[number // 2]
        if i % 2 == 0:
            pair = pairs[number] = Pair(number % 2, *unit)
            dmix = dmix_ref[:, pair.at]
            product = (mixed_ref[:, pair.at].astype(F32) * dmix.astype(F32)).T
            pair.delta = [jnp.sum(product[64 * w : 64 * w + 64], 0, keepdims=True) for w in range(2)]
            pair.d = [lane_half(dmix, w) for w in range(2)]
            pair.kt = pair.k.T
            pair.lse = [lse_ref[number % 2, w : w + 1, :] for w in range(2)]
            pair.out = slice(128 * number, 128 * number + 128)
        pair = pairs[number]
        return dot_nt(pair.k, pair.q[i % 2]), dot_nt(pair.v, pair.d[i % 2])

    def then(i, products):
        which, pair = i % 2, pairs[i // 2]
        weights, backs = [], []
        for b, scores in enumerate(blocks(products[0], sv)):
            p = jnp.exp2(scores * scale - pair.lse[which])
            weights.append(p.astype(BF16))
            backs.append((p * (products[1][PART * b : PART * b + PART] - pair.delta[which])).astype(BF16))
        weights, backs = jnp.concatenate(weights, 0), jnp.concatenate(backs, 0)
        dv, dk = dot(weights, pair.d[which]), dot(backs, pair.q[which])
        dq = dot(pair.kt[64 * which : 64 * which + 64], backs)
        if which == 0:
            held[:] = [dv, dk, dq]
            return
        dv, dk = dv + held[0], (dk + held[1]) * 0.125
        dka_ref[:, pair.out], dkb_ref[:, pair.out] = dk[:OWN].astype(BF16), dk[OWN:].astype(BF16)
        dva_ref[:, pair.out], dvb_ref[:, pair.out] = dv[:OWN].astype(BF16), dv[OWN:].astype(BF16)
        dq_ref[:, pair.out] = (jnp.concatenate([held[2], dq], 0) * 0.125).T.astype(BF16)

    ahead(4 * units, first, then)


def attend_back(sv, joined_a, joined_b, mixed, d_mixed, lse, after):
    span = WIDTH // UNIT
    units = range(span)
    ins = []
    for unit in units:
        wide = lambda array, off, unit=unit: (array, (OWN, UNIT), lambda h, sv: (0, off * span + unit))
        ins += [wide(joined_a, 0), wide(joined_a, 1), wide(joined_b, 0), wide(joined_a, 2), wide(joined_b, 1)]
        ins += [wide(mixed, 0), wide(d_mixed, 0), (lse, (2, 2, OWN), lambda h, sv, unit=unit: (unit, 0, 0))]
    return launch(
        functools.partial(attend_back_kernel, len(units)),
        sv,
        (1,),
        ins,
        [out_whole((OWN, UNIT * len(units)), BF16)] * 5,
        after=after,
        limit=24,
        name="attend_back",
    )


QUARTER = WIDTH // 4


def rows_of(array):
    return (array, (PART, array.shape[1]), lambda i, sv: (i, 0))


def out_rows(wide, dtype):
    return ((OWN, wide), dtype, (PART, wide), lambda i, sv: (i, 0))


def gelu_pair(u):
    z = jnp.abs(u) * 0.7071067811865476
    t = 1.0 / (1.0 + 0.3275911 * z)
    e = jnp.exp2(u * u * (-0.5 * LOG2E))
    series = t * (
        0.5 * 0.254829592
        + t * (0.5 * -0.284496736 + t * (0.5 * 1.421413741 + t * (0.5 * -1.453152027 + t * (0.5 * 1.061405429))))
    )
    tail = series * e
    below = jnp.where(u >= 0, 1.0 - tail, tail)
    return u * below, below + u * e * 0.3989422804014327


def step_part(j, sv):
    return 2 * jnp.where(lax.rem(j, 2) == 0, sv[FAR_Y], sv[Y]) + jnp.where(j < 2, 1 - sv[CORE], sv[CORE])


BLOCK = FF // 4 // GROUPS
FF_ROWS = 8 * QUARTER + 6 * BLOCK


def ff_head(sv, ins, branch_ref, dout_ref, second_ref, secondt_ref, dbt_ref):
    mixed_ref, entered_ref, d0_ref, d1_ref, wproj_ref, bias_ref, sattn_ref, gain_ref, shift_ref, sffn_ref = ins
    branch = dot(mixed_ref[...], wproj_ref[...]) + bias_ref[...]
    branch_ref[...] = branch
    n, _rho = norm_parts(entered_ref[...].astype(F32) + sattn_ref[...] * branch)
    second = (n * gain_ref[...] + shift_ref[...]).astype(BF16)
    second_ref[...] = second
    turned = second.T
    for part in range(4):
        place = jnp.where(part % 2 != sv[CORE], 0, 2) + jnp.where(part // 2 != sv[Y], 0, 1)
        secondt_ref[pl.ds(pl.multiple_of(place * QUARTER, 16), QUARTER), :] = turned[
            QUARTER * part : QUARTER * part + QUARTER
        ]
    dout_ref[:PART, :], dout_ref[PART:, :] = d0_ref[...], d1_ref[...]
    dbt_ref[...] = (dout_ref[:, :WIDTH].astype(F32) * sffn_ref[...]).astype(BF16)


def ff_kernel(opens, sv, *refs):
    weights = [refs[3 * i : 3 * i + 3] for i in range(4)]
    branch2_ref, grad_ref, gb1_ref, *shares = refs[-7:]
    if opens:
        head = refs[22:27]
        second_ref, secondt_ref, dbt_ref = head[2:]
    else:
        second_ref, secondt_ref, dbt_ref = refs[12:15]

    @pl.when(pl.program_id(0) == 0)
    def _():
        if opens:
            ff_head(sv, refs[12:22], *head)
            branch2_ref[...] = jnp.zeros((OWN, WIDTH), F32)
            grad_ref[...] = jnp.zeros((OWN, WIDTH), F32)
        else:
            branch2_ref[...] = refs[15][...]
            grad_ref[...] = refs[16][...]

    hidden, d_pre = [], []

    def first(i):
        w1_ref, b1_ref, w2_ref = weights[i]
        return dot(second_ref[...], w1_ref[...]) + b1_ref[...], dot_nt(dbt_ref[...], w2_ref[...])

    def then(i, products):
        value, slope = gelu_pair(products[0])
        hidden.append(value.astype(BF16))
        d_pre.append((products[1] * slope).astype(BF16))
        spot = pl.ds(pl.multiple_of(step_part(i, sv) * BLOCK, BLOCK), BLOCK)
        gb1_ref[:, spot] = jnp.sum(d_pre[-1].astype(F32), 0, keepdims=True)

    ahead(4, first, then)
    hidden, d_pre = jnp.concatenate(hidden, 1), jnp.concatenate(d_pre, 1)
    gw1 = dot(secondt_ref[...], d_pre).astype(BF16)
    for i in range(4):
        for k in range(2):
            spot = pl.ds(pl.multiple_of((2 * step_part(i, sv) + k) * QUARTER, 16), QUARTER)
            at = BLOCK * i + 128 * k
            for ref, row in zip(shares, range(0, WIDTH, QUARTER)):
                ref[spot, :] = gw1[row : row + QUARTER, at : at + 128]
    gw2 = dot_tn(hidden, dbt_ref[...]).astype(BF16)
    for i in range(4):
        for k in range(6):
            low = 8 * QUARTER + BLOCK * k
            shares[i][low : low + BLOCK, :] = gw2[BLOCK * i : BLOCK * i + BLOCK, 128 * k : 128 * k + 128]
    branch2_ref[...] += dot(hidden, jnp.concatenate([w[2][...] for w in weights], 0))
    grad_ref[...] += dot_nt(d_pre, jnp.concatenate([w[0][...] for w in weights], 1))


def feed_forward(sv, groups, others, w1, table, w2, opens):
    streamed = []
    for i in range(4):
        at = lambda g, sv, i=i: GROUPS * step_part(i, sv) + g + groups[0]
        streamed += [
            (w1, (WIDTH, BLOCK), lambda g, sv, at=at: (0, at(g, sv))),
            (table, (1, BLOCK), lambda g, sv, at=at: (0, 11 * GROUPS + at(g, sv))),
            (w2, (BLOCK, WIDTH), lambda g, sv, at=at: (at(g, sv), 0)),
        ]
    count = len(groups)
    head = [
        out_whole((OWN, WIDTH), F32),
        out_whole((OWN, WIDTH + 128), BF16),
        out_whole((OWN, WIDTH), BF16),
        out_whole((WIDTH, OWN), BF16),
        out_whole((OWN, WIDTH), BF16),
    ]
    return launch(
        functools.partial(ff_kernel, opens),
        sv,
        (count,),
        streamed + [o if isinstance(o, tuple) else whole(o) for o in others],
        (head if opens else [])
        + [
            out_whole((OWN, WIDTH), F32),
            out_whole((OWN, WIDTH), F32),
            ((1, 4 * BLOCK * count), F32, (1, 4 * BLOCK), lambda g, sv: (0, g)),
            *[((count * FF_ROWS, 128), BF16, (FF_ROWS, 128), lambda g, sv: (g, 0))] * 4,
        ],
        limit=16,
        name=f"feed_forward_{groups[0]}",
    )


def tail_kernel(
    sv, branch2_ref, g_ref, branch_ref, entered_ref, dout_ref, w_ref, b2_ref, sffn_ref, sattn_ref, gain_ref,
    out_ref, dmid_ref, dbr_ref, dmix_ref, vec_ref,
):
    branch_two = branch2_ref[...] + b2_ref[...]
    d_out = dout_ref[:, :WIDTH].astype(F32)
    branch = branch_ref[...]
    middle = entered_ref[...].astype(F32) + sattn_ref[...] * branch
    out_ref[...] = (middle + sffn_ref[...] * branch_two).astype(BF16)
    n, rho = norm_parts(middle)
    g = g_ref[...]
    scaled = g * gain_ref[...]
    d_middle = d_out + rho * (
        scaled - jnp.mean(scaled, -1, keepdims=True) - n * jnp.mean(scaled * n, -1, keepdims=True)
    )
    dmid_ref[...] = d_middle
    d_branch = (d_middle * sattn_ref[...]).astype(BF16)
    dbr_ref[...] = d_branch
    dmix_ref[...] = dot_nt(d_branch, w_ref[...]).astype(BF16)
    rounded = (d_out * sffn_ref[...]).astype(BF16).astype(F32)
    add_vectors(
        vec_ref,
        [d_out * branch_two, rounded, g * n, g, d_middle * branch, d_branch.astype(F32)],
    )


def add_vectors(vec_ref, values):
    rows = [jnp.sum(v, 0, keepdims=True) for v in values]
    vec = jnp.concatenate(rows + [jnp.zeros((8 - len(rows), WIDTH), F32)], 0)

    @pl.when(pl.program_id(0) == 0)
    def _():
        vec_ref[...] = vec

    @pl.when(pl.program_id(0) > 0)
    def _():
        vec_ref[...] += vec


def ff_tail(sv, branch2, g, branch, entered, dout, w_proj, vectors, after):
    return launch(
        tail_kernel,
        sv,
        (2,),
        [rows_of(a) for a in (branch2, g, branch, entered, dout)] + [whole(w_proj)] + list(vectors),
        [out_rows(WIDTH, BF16), out_rows(WIDTH, F32), out_rows(WIDTH, BF16), out_rows(WIDTH, BF16), out_whole((8, WIDTH), F32)],
        after=after,
        limit=16,
        name="ff_tail",
    )


def store_slabs(sv, kept, slabs, low, shares):
    for step, ref in enumerate(shares):
        rows = pl.ds(pl.multiple_of(step_part(step, sv) * QUARTER, 16), QUARTER)
        for i in range(slabs):
            at = (low + i) * QUARTER
            ref[at : at + QUARTER, :] = kept[rows, 128 * i : 128 * i + 128].astype(BF16)


def grads_kernel(
    sv, mixed_ref, dbr_ref, normed_ref, dq_ref, dk_ref, rk_ref, dv_ref, rv_ref, *rest
):
    *shares, dkey_ref, dvalue_ref, kept = rest
    kept[:, :WIDTH] = dot_tn(mixed_ref[...], dbr_ref[...])
    store_slabs(sv, kept, 6, 0, shares)
    d_key = (dk_ref[...].astype(F32) + rk_ref[...].astype(F32)).astype(BF16)
    d_value = (dv_ref[...].astype(F32) + rv_ref[...].astype(F32)).astype(BF16)
    dkey_ref[...] = d_key
    dvalue_ref[...] = d_value
    kept[...] = dot_tn(normed_ref[...], jnp.concatenate([dq_ref[...], d_key, d_value], 1))
    store_slabs(sv, kept, 18, 6, shares)


def projection_grads(sv, mixed, d_branch, normed, parts, after):
    rows = 24 * QUARTER
    return launch(
        grads_kernel,
        sv,
        (1,),
        [whole(a) for a in (mixed, d_branch, normed, *parts)],
        [out_whole((rows, 128), BF16)] * 4 + [out_whole((OWN, WIDTH), BF16)] * 2,
        scratch=[pltpu.VMEM((WIDTH, 3 * WIDTH), F32)],
        after=after,
        limit=24,
        name="projection_grads",
    )


VECTORS = 32


def entry_kernel(
    sv, dq_ref, dk_ref, dv_ref, w_ref, entered_ref, dmid_ref, dout_ref, gain_ref,
    va_ref, b1a_ref, b1b_ref, grad_ref, sums_ref, vec_ref,
):
    dq, dk, dv = dq_ref[...], dk_ref[...], dv_ref[...]
    g = dot_nt(jnp.concatenate([dq, dk, dv], 1), w_ref[...])
    n, rho = norm_parts(entered_ref[...].astype(F32))
    scaled = g * gain_ref[...]
    d_entered = dmid_ref[...] + rho * (
        scaled - jnp.mean(scaled, -1, keepdims=True) - n * jnp.mean(scaled * n, -1, keepdims=True)
    )
    chosen = jnp.concatenate([dout_ref[:, WIDTH:].astype(F32)] * 6, 1)
    masked = d_entered * chosen
    grad_ref[...] = (d_entered - masked).astype(BF16)
    add_vectors(vec_ref, [masked, g * n, g, dq.astype(F32), dv.astype(F32)])

    @pl.when(pl.program_id(0) == 1)
    def _():
        b1 = jnp.concatenate([b1a_ref[...], b1b_ref[...]], 1)
        parts = [
            jnp.concatenate([b1[:, 4 * BLOCK * g + BLOCK * p : 4 * BLOCK * g + BLOCK * (p + 1)] for g in range(GROUPS)], 1)
            for p in range(4)
        ]
        rows = [va_ref[...], vec_ref[...], *parts, jnp.zeros((VECTORS - 20, WIDTH), F32)]
        rows = jnp.concatenate(rows, 0)
        for i in range(WIDTH // 128):
            sums_ref[VECTORS * i : VECTORS * i + VECTORS, :] = rows[:, 128 * i : 128 * i + 128]


def entry_back(sv, parts, w_qkv, entered, d_middle, dout, gain, vectors, after):
    return launch(
        entry_kernel,
        sv,
        (2,),
        [rows_of(p) for p in parts]
        + [whole(w_qkv), rows_of(entered), rows_of(d_middle), rows_of(dout), gain]
        + [whole(v) for v in vectors],
        [out_rows(WIDTH, BF16), out_whole((VECTORS * WIDTH // 128, 128), F32)],
        scratch=[pltpu.VMEM((8, WIDTH), F32)],
        after=after,
        limit=20,
        micros=10,
        name="entry_back",
    )


CORE, Y, FAR_Y, X, FAR_X, Z, FAR_Z, QUARTER_MINE, QUARTER_FAR, TURNED_MINE, TURNED_FAR, COUNTS = range(12)


def swap(value, axis, distance):
    count = lax.axis_size(axis)
    return lax.ppermute(value, axis, [(i, i ^ distance) for i in range(count)])


def sums_kernel(plan, sv, *refs):
    count = sum(terms for _, _, parts in plan for _, terms in parts)
    ins, outs = list(refs[:count]), refs[count:]
    for (_, _, parts), out_ref in zip(plan, outs):
        low = 0
        for rows, terms in parts:
            total = ins.pop(0)[...].astype(F32)
            for _ in range(terms - 1):
                total += ins.pop(0)[...].astype(F32)
            out_ref[low : low + rows, :] = total.astype(out_ref.dtype)
            low += rows


def add_up(sv, outs, after, name, micros=0.05):
    ins, plan, results = [], [], []
    for dtype, parts in outs:
        for rows, terms in parts:
            for array, block, skip in terms:
                at = lambda i, sv, block=block, skip=skip: (skip if block is None else sv[block] + skip, 0)
                ins.append((array, (rows, 128), at))
        total = sum(rows for rows, _ in parts)
        plan.append((None, None, [(rows, len(terms)) for rows, terms in parts]))
        results.append(out_whole((total, 128), dtype))
    return list(launch(functools.partial(sums_kernel, plan), sv, (1,), ins, results, after=after, limit=8, micros=micros, name=name))


class Piece:
    def __init__(self, order, kept, rows, skip=0):
        self.order, self.rows, self.skip = order, rows, skip
        self.far, self.near, self.core_far, self.core = kept

    def two(self, share, block, far):
        a, b = (self.far, self.core_far) if far else (self.near, self.core)
        return [(a, block, share * self.skip), (b, block, share * self.skip)]

    def first(self):
        n = self.rows
        if self.order == "yxz":
            return [(n, self.two(1, None, True))], None
        far, mine = (FAR_X, X) if self.order[0] == "x" else (FAR_Z, Z)
        return tuple([(n // 2, self.two(2, block, True)), (n // 2, self.two(2, block, False))] for block in (far, mine))

    def both(self, rows, block, skip):
        assert self.kept[1] % rows == 0 and self.arrived[1] % rows == 0
        return [(array, block, skip + offset // rows) for array, offset in (self.kept, self.arrived)]

    def second(self):
        n = self.rows
        if self.order == "yxz":
            array, offset = self.arrived
            assert offset % (n // 2) == 0
            skip = offset // (n // 2)
            return tuple([(n // 2, self.two(2, at, False) + [(array, at, skip)])] for at in (FAR_X, X))
        if self.order == "xzy":
            return tuple([(n // 4, self.both(n // 4, at, skip)) for skip in (0, 2)] for at in (FAR_Z, Z))
        return tuple([(n // 2, self.both(n // 2, None, skip))] for skip in (0, 1))

    def third(self):
        n = self.rows
        if self.order == "xzy":
            return tuple([(n // 4, self.both(n // 4, None, skip))] for skip in (0, 1))
        far, mine = (FAR_X, X) if self.order[2] == "x" else (FAR_Z, Z)
        return tuple([(n // 4, self.both(n // 4, at, 0))] for at in (far, mine))

    def fourth(self):
        return (self.rows // 4, self.both(self.rows // 4, None, 0))


class Payload:
    def __init__(self, sv, name, *pieces, micros=0.05, vectors=None):
        self.sv, self.name, self.pieces, self.micros = sv, name, list(pieces), micros
        self.vectors = vectors
        if vectors is not None:
            self.more = [swap(vectors, "seq", d) for d in (1, 2, 3)]

    def ride(self, outs):
        if self.vectors is None:
            return outs
        terms = [(v, None, 0) for v in (self.vectors, *self.more)]
        return outs + [(F32, [(self.vectors.shape[0], terms)])]

    def rode(self, sums, distance):
        if self.vectors is not None:
            self.vectors = sums.pop()
            self.more = [swap(self.vectors, "dp", distance)]

    def step(self, number, after):
        plans = [(p, *(p.first, p.second, p.third)[number]()) for p in self.pieces]
        axes = sorted({p.order[number] for p in self.pieces})
        packs = {axis: [] for axis in axes}
        places, kept, keepers = [], [], []

        def put(pack, parts):
            at = sum(rows for rows, _ in pack)
            pack += parts
            return at

        for p, send, keep in plans:
            places.append((p, p.order[number], put(packs[p.order[number]], send)))
            if keep:
                keepers.append((p, put(kept, keep)))
        outs = [(BF16, packs[axis]) for axis in axes] + ([(F32, kept)] if kept else [])
        outs = self.ride(outs) if number == 2 else outs
        sums = add_up(self.sv, outs, after, f"{self.name}_{number + 1}", self.micros)
        if number == 2:
            self.rode(sums, 1)
        for p, at in keepers:
            p.kept = (sums[len(axes)], at)
        sent = sums[: len(axes)]
        where = {"y": ("seq", 2), "x": ("dp", 1), "z": ("dp", 2)}
        arrived = {axis: swap(value, *where[axis]) for axis, value in zip(axes, sent)}
        for p, axis, at in places:
            p.arrived = (arrived[axis], at)
        return sent, list(arrived.values())

    def far_z(self, after):
        outs = self.ride([(BF16, [p.fourth() for p in self.pieces])])
        sums = add_up(self.sv, outs, after, self.name + "_4", self.micros)
        self.rode(sums, 2)
        self.sums, self.arrived = sums, [swap(sums[0], "dp", 4)]
        return sums, self.arrived

    def far_z_halves(self, after):
        first, middle, last = self.pieces
        rows = middle.rows // 8
        low, high = [(rows, middle.both(rows, None, i)) for i in range(2)]
        self.sums = add_up(self.sv, [(BF16, [first.fourth(), low]), (BF16, [high, last.fourth()])], after, self.name + "_4")
        self.arrived = [swap(value, "dp", 4) for value in self.sums]
        return self.sums, self.arrived

    def back(self, after, micros=0.05):
        parts = [(mine.shape[0], [(mine, None, 0), (other, None, 0)]) for mine, other in zip(self.sums, self.arrived)]
        sums = add_up(self.sv, self.ride([(BF16, parts)]), after, self.name + "_5", micros)
        self.rode(sums, 4)
        (own,) = sums
        across = swap(own, "dp", 2)
        self.gathered = [own, across, swap(own, "dp", 1), swap(across, "dp", 1)]
        return [own], self.gathered[1:]

    def psum(self):
        gathered = []
        for p in self.pieces:
            terms = p.two(1, None, False) + [(p.arrived[0], None, p.arrived[1] // p.rows)]
            (out,) = add_up(self.sv, [(BF16, [(p.rows, terms)])], [], self.name + "_all")
            out, quarter = lax.psum(out, "dp"), p.rows // 4
            places = [self.sv[QUARTER_MINE] ^ d for d in range(4)]
            gathered.append([lax.dynamic_slice_in_dim(out, place * quarter, quarter, 0) for place in places])
        self.gathered = [jnp.concatenate(parts, 0) for parts in zip(*gathered)]

    def layout(self):
        return [(p.order, p.rows) for p in self.pieces]


def share(arrays):
    return [arrays[2], arrays[3], swap(arrays[0], "seq", 1), swap(arrays[1], "seq", 1)]


def copy_kernel(sv, in_ref, out_ref):
    out_ref[...] = in_ref[...]


def copy_rows(sv, array, part, after, name):
    ins = [(array, (PART, WIDTH), lambda i, sv: (part, 0))]
    return launch(copy_kernel, sv, (1,), ins, [out_whole((PART, WIDTH), array.dtype)], after=after, name=name)[0]


def order_pieces(sv, layout, refs, whole_ref):
    low = 0
    for order, rows in layout:
        quarter = rows // 4
        for d, ref in enumerate(refs):
            place = (sv[TURNED_MINE] ^ (0, 2, 1, 3)[d]) if order == "zyx" else (sv[QUARTER_MINE] ^ d)
            at = pl.multiple_of(low + place * quarter, 16)
            whole_ref[pl.ds(at, quarter), :] = ref[low // 4 : low // 4 + quarter, :]
        low += rows


def slab(whole_ref, at, rows):
    return whole_ref[at : at + rows, :].astype(F32)


def finish_ff_kernel(layout, sv, *refs):
    w1_ref, w2_ref, whole_ref = refs[-3:]
    order_pieces(sv, layout, refs[:4], whole_ref)
    for g in range(GROUPS):
        low = FF_ROWS * g
        for i in range(6):
            w2_ref[BLOCK * g : BLOCK * g + BLOCK, 128 * i : 128 * i + 128] = slab(whole_ref, low + 8 * QUARTER + BLOCK * i, BLOCK)
        for i in range(8):
            at = BLOCK * (GROUPS * (i // 2) + g) + 128 * (i % 2)
            w1_ref[:, at : at + 128] = slab(whole_ref, low + QUARTER * i, QUARTER)


def finish_ff(sv, payload, after):
    return launch(
        functools.partial(finish_ff_kernel, payload.layout()),
        sv,
        (1,),
        [whole(part) for part in payload.gathered],
        [out_whole((QUARTER, FF), F32), out_whole((FF // 4, WIDTH), F32)],
        scratch=[pltpu.VMEM((GROUPS * FF_ROWS, 128), BF16)],
        after=after,
        limit=20,
        micros=5,
        name="finish_ff",
    )


def finish_rest_kernel(layout, sv, *refs):
    proj_ref, qkv_ref, vec_ref, whole_ref = refs[-4:]
    vec = refs[4][...] + refs[5][...]
    for i in range(WIDTH // 128):
        vec_ref[:, 128 * i : 128 * i + 128] = vec[VECTORS * i : VECTORS * i + VECTORS]
    order_pieces(sv, layout, refs[:4], whole_ref)
    for i in range(6):
        proj_ref[:, 128 * i : 128 * i + 128] = slab(whole_ref, i * QUARTER, QUARTER)
    for i in range(18):
        qkv_ref[:, 128 * i : 128 * i + 128] = slab(whole_ref, (6 + i) * QUARTER, QUARTER)


def finish_rest(sv, payload, after):
    return launch(
        functools.partial(finish_rest_kernel, payload.layout()),
        sv,
        (1,),
        [whole(part) for part in (*payload.gathered, payload.vectors, *payload.more)],
        [
            out_whole((QUARTER, WIDTH), F32),
            out_whole((QUARTER, 3 * WIDTH), F32),
            out_whole((VECTORS, WIDTH), F32),
        ],
        scratch=[pltpu.VMEM((24 * QUARTER, 128), BF16)],
        after=after,
        limit=16,
        name="finish_rest",
    )


def per_device(
    patches, mask, mask_token, ln1_gain, ln1_bias, w_qkv, bias_q, bias_v, w_proj, bias_proj, scale_attn,
    ln2_gain, ln2_bias, w_fc1, bias_fc1, w_fc2, bias_fc2, scale_ffn, cotangent,
):
    slot_rows, images_here, width = patches.shape
    parts = lax.axis_size("seq")
    assert parts == 4 and images_here == 2 and width == WIDTH
    s = lax.axis_index("seq")
    dp = lax.axis_index("dp")
    y, core = s // 2, s % 2
    x, z = dp % 2, dp // 2 % 2

    def live_count(part):
        lead = (part == 0).astype(jnp.int32)
        return lead + (GRID // parts + (part < GRID % parts).astype(jnp.int32)) * GRID

    sv = jnp.stack(
        [core, y, 1 - y, x, 1 - x, z, 1 - z, 2 * x + z, 2 * x + 1 - z, 2 * z + x, 2 * z + 1 - x]
        + [live_count(s), live_count(s ^ 2), live_count(s ^ 1), live_count(s ^ 3)]
    ).astype(jnp.int32)
    table = jnp.concatenate(
        [
            bias_q, jnp.zeros_like(bias_q), bias_v, ln1_gain, ln1_bias, ln2_gain, ln2_bias, scale_attn, scale_ffn,
            bias_proj, bias_fc2, bias_fc1,
        ]
    ).astype(F32)[None, :]
    gain1, _shift1, gain2, shift2, sattn, sffn, bproj, b2 = [row_of(table, i) for i in range(3, 11)]

    chosen = mask[:, :, None] == 1
    entered = jnp.where(chosen, mask_token, patches)
    grow = ((0, PART - slot_rows), (0, 0))
    image = lambda array, i: lax.dynamic_index_in_dim(array, i, 1, keepdims=False)
    x1 = swap(jnp.pad(image(entered, 1 - y), grow), "seq", 2)
    x0 = jnp.pad(image(entered, y), grow)
    xb0 = swap(x0, "seq", 1)
    d_rows = jnp.concatenate(
        [
            jnp.where(chosen, cotangent, jnp.zeros_like(cotangent)),
            jnp.broadcast_to(chosen, (slot_rows, images_here, 128)).astype(BF16),
        ],
        -1,
    )
    d1 = swap(jnp.pad(image(d_rows, 1 - y), grow), "seq", 2)
    d0 = jnp.pad(image(d_rows, y), grow)

    own_first = qkv_part(True, 0, x0, table, w_qkv, [])
    other_first = qkv_part(False, 0, xb0, table, w_qkv, [])
    x1 = copy_rows(sv, x1, 0, other_first, "entered_far")
    xb1 = swap(x1, "seq", 1)
    joined_a, normed, entered_a = qkv_part(True, 1, x1, table, w_qkv, own_first)
    (joined_b,) = qkv_part(False, 1, xb1, table, w_qkv, other_first)
    mixed, lse = attend(sv, joined_a, joined_b)
    fused = lax.axis_size("dp") == 8
    orders = ("yxz", "xzy", "zyx") if fused else ("yxz",) * 3
    branch, dout, second, secondt, dbt, branch2, g, gb1a, *shares = feed_forward(
        sv, (0, 1), [mixed, entered_a, d0, d1, w_proj, bproj, sattn, gain2, shift2, sffn], w_fc1, table, w_fc2, True
    )
    shares = share(shares)
    ff01 = Payload(sv, "ff01", *[Piece(orders[i], shares, FF_ROWS, i) for i in range(2)])
    branch2, g, gb1b, *shares = feed_forward(
        sv, (2,), [second, secondt, dbt, branch2, g], w_fc1, table, w_fc2, False
    )
    ff2 = Payload(sv, "ff2", Piece(orders[2], share(shares), FF_ROWS), micros=2)
    ff = Payload(sv, "ff", *ff01.pieces, *ff2.pieces)

    def halves(kept):
        rows = kept[0].shape[0] // 2
        return [Piece("yxz", kept, rows, 0), Piece("xyz" if fused else "yxz", kept, rows, 1)]

    def far_rows(array, after, name):
        return swap(copy_rows(sv, array, 1, after, name), "seq", 2)

    def place_rows(array, far):
        near, far = array[:slot_rows, None], far[:slot_rows, None]
        return jnp.where(y == 0, jnp.concatenate([near, far], 1), jnp.concatenate([far, near], 1))

    sent, arrived = ff01.step(0, [gb1b])
    sent, more = ff2.step(0, sent)
    out_a, d_middle, d_branch, d_mixed, vec_a = ff_tail(
        sv, branch2, g, branch, entered_a, dout, w_proj, [b2, sffn, sattn, gain2], sent
    )
    dq, dka, dva, dkb, dvb = attend_back(sv, joined_a, joined_b, mixed, d_mixed, lse, sent)
    rk, rv = swap(dkb, "seq", 1), swap(dvb, "seq", 1)
    sent = [dq]
    if fused:
        sent, arrived = ff01.step(1, sent + arrived)
        sent, more = ff2.step(1, sent + more)
    *shares, d_key, d_value = projection_grads(sv, mixed, d_branch, normed, [dq, dka, rk, dva, rv], sent)
    shares = share(shares)
    grad_a, vectors = entry_back(
        sv, [dq, d_key, d_value], w_qkv, entered_a, d_middle, dout, gain1, [vec_a, gb1a, gb1b], []
    )
    both = Payload(sv, "both", *halves(shares), vectors=vectors if fused else None)
    sent = [grad_a]
    if fused:
        sent, arrived = ff.step(2, sent + arrived + more)
    sent, more = both.step(0, sent)
    if fused:
        ff.micros = 3
        sent, arrived = ff.far_z(sent + arrived)
        sent, more = both.step(1, sent + more)
        sent, more = both.step(2, arrived + sent + more)
        sent, arrived = ff.back(sent + arrived)
        sent, more = both.far_z(sent + more)
        out_far = far_rows(out_a, sent, "layer_out_far")
        grad_far = far_rows(grad_a, sent, "input_grad_far")
        sent, more = both.back(sent + more + [arrived[1]], 10)
        layer_out = place_rows(out_a, out_far)
        input_grad = place_rows(grad_a, grad_far)
        grad_w1, grad_w2 = finish_ff(sv, ff, sent + arrived)
    else:
        ff.psum()
        both.psum()
        both.vectors, both.more = lax.psum(vectors, ("dp", "seq")), [jnp.zeros_like(vectors)]
        grad_w1, grad_w2 = finish_ff(sv, ff, [])
        layer_out = place_rows(out_a, far_rows(out_a, [], "layer_out_far"))
        input_grad = place_rows(grad_a, far_rows(grad_a, [], "input_grad_far"))
    grad_proj, grad_qkv, vectors = finish_rest(sv, both, [grad_w1, layer_out, input_grad])
    grad_b1 = lax.dynamic_index_in_dim(vectors[16:20], s, 0, keepdims=False)
    vectors = lax.dynamic_slice_in_dim(vectors[:16], s * QUARTER, QUARTER, 1)

    return (
        layer_out, input_grad,
        vectors[8], vectors[9], vectors[10], grad_qkv, vectors[11], vectors[12], grad_proj,
        vectors[5], vectors[4], vectors[2], vectors[3], grad_w1, grad_b1, grad_w2, vectors[1], vectors[0],
    )


def solution(mesh):
    rows, flat = P("seq", "dp", None), P("seq")
    deep = P("seq", None)
    return jax.shard_map(
        per_device,
        mesh=mesh,
        in_specs=(rows, P("seq", "dp")) + (P(),) * 16 + (rows,),
        out_specs=(
            rows, rows, flat, flat, flat, deep, flat, flat, deep, flat, flat, flat, flat, deep, flat, deep, flat, flat,
        ),
        check_vma=False,
    )
```

```python
import functools

import jax
import jax.numpy as jnp
from jax import lax
from jax.experimental import pallas as pl
from jax.experimental.pallas import tpu as pltpu
from jax.sharding import PartitionSpec as P

HEADS = 12
GRID = 30
WIDTH = 768
FF = 3072
PART = 256
OWN = 512
GROUPS = 3
EPS = 1e-6
LOG2E = 1.4426950408889634
LN2 = 0.6931471805599453
BF16 = jnp.bfloat16
F32 = jnp.float32
ANY = pl.BlockSpec(memory_space=pl.ANY)
SMEM = pl.BlockSpec(memory_space=pltpu.SMEM)
MIB = 1024 * 1024


def params(limit=58):
    return pltpu.CompilerParams(vmem_limit_bytes=limit * MIB)


def launch(kernel, sv, grid, ins, outs, scratch=(), alias=None, after=(), limit=8, micros=0.05, name=None):
    alias = alias or {}
    after = list(after)
    count = len(ins)

    def body(sv_ref, *refs):
        kernel(sv_ref, *refs[:count], *refs[count + len(after) :])

    spec = lambda block, index: ANY if block is None else pl.BlockSpec(block, index)
    return pl.pallas_call(
        body,
        grid_spec=pltpu.PrefetchScalarGridSpec(
            num_scalar_prefetch=1,
            grid=grid,
            in_specs=[spec(b, i) for _, b, i in ins] + [ANY] * len(after),
            out_specs=[spec(b, i) for _, _, b, i in outs],
            scratch_shapes=list(scratch),
        ),
        out_shape=[shape_of(d, t) for d, t, _, _ in outs],
        input_output_aliases={1 + k: v for k, v in alias.items()},
        compiler_params=params(limit),
        cost_estimate=cost(micros),
        name=name,
    )(sv, *[a for a, _, _ in ins], *after)


def whole(array):
    dims = array.shape
    return (array, dims, lambda *_: (0,) * len(dims))


def row_of(table, index):
    return (table, (1, WIDTH), lambda *_: (0, index))


def out_whole(dims, dtype):
    return (dims, dtype, dims, lambda *_: (0,) * len(dims))


def cost(micros):
    return pl.CostEstimate(flops=int(micros * 1.15e9), bytes_accessed=0, transcendentals=0)


def shape_of(dims, dtype):
    return jax.ShapeDtypeStruct(dims, dtype)


def full(dims):
    return pl.BlockSpec(dims, lambda *_: (0,) * len(dims))


def dot(left, right):
    return jnp.dot(left, right, preferred_element_type=F32)


def dot_nt(left, right):
    return lax.dot_general(left, right, (((1,), (1,)), ((), ())), preferred_element_type=F32)


def dot_tn(left, right):
    return lax.dot_general(left, right, (((0,), (0,)), ((), ())), preferred_element_type=F32)


def norm_parts(values):
    centred = values - jnp.mean(values, -1, keepdims=True)
    rho = lax.rsqrt(jnp.mean(centred * centred, -1, keepdims=True) + EPS)
    return centred * rho, rho


def qkv_kernel(own, sv, x_ref, gain_ref, shift_ref, w_ref, bias_ref, *rest):
    if own:
        joined_ref, normed_ref, entered_ref, kept = rest[-4:]
    else:
        joined_ref, kept = rest[-2:]

    @pl.when(pl.program_id(0) == 0)
    def _():
        x = x_ref[...]
        n, _rho = norm_parts(x.astype(F32))
        kept[...] = (n * gain_ref[...] + shift_ref[...]).astype(BF16)
        if own:
            normed_ref[...] = kept[...]
            entered_ref[...] = x

    joined_ref[...] = (dot(kept[...], w_ref[...]) + bias_ref[...]).astype(BF16)


def qkv_part(own, half, x, table, w_qkv, previous, after=()):
    steps, off = (3, 0) if own else (2, 1)
    outs = [((OWN, steps * WIDTH), BF16, (PART, WIDTH), lambda j, sv: (half, j))]
    if own:
        outs += [((OWN, WIDTH), BF16, (PART, WIDTH), lambda j, sv: (half, 0))] * 2
    previous = list(previous)
    return launch(
        functools.partial(qkv_kernel, own),
        jnp.zeros((1,), jnp.int32),
        (steps,),
        [
            whole(x),
            row_of(table, 3),
            row_of(table, 4),
            (w_qkv, (WIDTH, WIDTH), lambda j, sv: (0, j + off)),
            (table, (1, WIDTH), lambda j, sv: (0, j + off)),
        ]
        + [(p, None, None) for p in previous],
        outs,
        scratch=[pltpu.VMEM((PART, WIDTH), BF16)],
        alias={5 + i: i for i in range(len(previous))},
        after=after,
        limit=10,
        micros=4,
        name="qkv_own" if own else "qkv_other",
    )


DEAD_FROM = 208


def lane_half(values, which):
    lane = lax.broadcasted_iota(jnp.int32, values.shape, 1)
    keep = (lane < 64) if which == 0 else (lane >= 64)
    return jnp.where(keep, values.astype(F32), 0.0).astype(BF16)


def live_scores(scores, count):
    tail = scores[DEAD_FROM:]
    row = lax.broadcasted_iota(jnp.int32, tail.shape, 0) + DEAD_FROM
    return jnp.concatenate([scores[:DEAD_FROM], jnp.where(row < count, tail, -1e30)], 0)


PAIRS = 3


class Pair:
    def __init__(self, pair, q_ref, ka_ref, kb_ref, va_ref, vb_ref):
        self.at = slice(128 * pair, 128 * pair + 128)
        self.q = [lane_half(q_ref[:, self.at], i) for i in range(2)]
        self.k = jnp.concatenate([ka_ref[:, self.at], kb_ref[:, self.at]], 0)
        self.v = jnp.concatenate([va_ref[:, self.at], vb_ref[:, self.at]], 0)


def blocks(scores, sv):
    return [live_scores(scores[PART * i : PART * i + PART], sv[COUNTS + i]) for i in range(4)]


def ahead(count, first, then):
    waiting = first(0)
    for i in range(count):
        now, waiting = waiting, first(i + 1) if i + 1 < count else None
        then(i, now)


def attend_kernel(sv, q_ref, ka_ref, kb_ref, va_ref, vb_ref, mixed_ref, lse_ref):
    scale = 0.125 * LOG2E
    pairs, heads = {}, []

    def first(i):
        if i % 2 == 0:
            pairs[i // 2] = Pair(i // 2, q_ref, ka_ref, kb_ref, va_ref, vb_ref)
            pairs[i // 2].vt = pairs[i // 2].v.T
        pair = pairs[i // 2]
        return blocks(dot_nt(pair.k, pair.q[i % 2]), sv)

    def then(i, scores):
        which, pair = i % 2, pairs[i // 2]
        top = scores[0]
        for block in scores[1:]:
            top = jnp.maximum(top, block)
        top = jnp.max(top, 0, keepdims=True)
        total = jnp.zeros((1, OWN), F32)
        out = jnp.zeros((64, OWN), F32)
        for b, block in enumerate(scores):
            p = jnp.exp2((block - top) * scale)
            total += jnp.sum(p, 0, keepdims=True)
            out += dot(pair.vt[64 * which : 64 * which + 64, PART * b : PART * b + PART], p.astype(BF16))
        lse_ref[i // 2, which : which + 1, :] = top * scale + jnp.log(total) * LOG2E
        heads.append(out / total)
        if which == 1:
            mixed_ref[:, pair.at] = jnp.concatenate(heads[-2:], 0).T.astype(BF16)

    ahead(2 * PAIRS, first, then)


def attend(sv, joined_a, joined_b):
    steps = HEADS // 2 // PAIRS
    wide = lambda array, off: (array, (OWN, 128 * PAIRS), lambda h, sv: (0, off * steps + h))
    return launch(
        attend_kernel,
        sv,
        (steps,),
        [wide(joined_a, 0), wide(joined_a, 1), wide(joined_b, 0), wide(joined_a, 2), wide(joined_b, 1)],
        [
            ((OWN, WIDTH), BF16, (OWN, 128 * PAIRS), lambda h, sv: (0, h)),
            ((HEADS // 2, 2, OWN), F32, (PAIRS, 2, OWN), lambda h, sv: (h, 0, 0)),
        ],
        limit=18,
        name="attend",
    )


UNIT = 256


def attend_back_kernel(units, sv, *refs):
    scale = 0.125 * LOG2E
    ins = [refs[8 * u : 8 * u + 8] for u in range(units)]
    dq_ref, dka_ref, dva_ref, dkb_ref, dvb_ref = refs[8 * units :]
    pairs, held = {}, []

    def first(i):
        number = i // 2
        *unit, mixed_ref, dmix_ref, lse_ref = ins[number // 2]
        if i % 2 == 0:
            pair = pairs[number] = Pair(number % 2, *unit)
            dmix = dmix_ref[:, pair.at]
            product = (mixed_ref[:, pair.at].astype(F32) * dmix.astype(F32)).T
            pair.delta = [jnp.sum(product[64 * w : 64 * w + 64], 0, keepdims=True) for w in range(2)]
            pair.d = [lane_half(dmix, w) for w in range(2)]
            pair.kt = pair.k.T
            pair.lse = [lse_ref[number % 2, w : w + 1, :] for w in range(2)]
            pair.out = slice(128 * number, 128 * number + 128)
        pair = pairs[number]
        return dot_nt(pair.k, pair.q[i % 2]), dot_nt(pair.v, pair.d[i % 2])

    def then(i, products):
        which, pair = i % 2, pairs[i // 2]
        weights, backs = [], []
        for b, scores in enumerate(blocks(products[0], sv)):
            p = jnp.exp2(scores * scale - pair.lse[which])
            weights.append(p.astype(BF16))
            backs.append((p * (products[1][PART * b : PART * b + PART] - pair.delta[which])).astype(BF16))
        weights, backs = jnp.concatenate(weights, 0), jnp.concatenate(backs, 0)
        dv, dk = dot(weights, pair.d[which]), dot(backs, pair.q[which])
        dq = dot(pair.kt[64 * which : 64 * which + 64], backs)
        if which == 0:
            held[:] = [dv, dk, dq]
            return
        dv, dk = dv + held[0], (dk + held[1]) * 0.125
        dka_ref[:, pair.out], dkb_ref[:, pair.out] = dk[:OWN].astype(BF16), dk[OWN:].astype(BF16)
        dva_ref[:, pair.out], dvb_ref[:, pair.out] = dv[:OWN].astype(BF16), dv[OWN:].astype(BF16)
        dq_ref[:, pair.out] = (jnp.concatenate([held[2], dq], 0) * 0.125).T.astype(BF16)

    ahead(4 * units, first, then)


def attend_back(sv, joined_a, joined_b, mixed, d_mixed, lse, after):
    span = WIDTH // UNIT
    units = range(span)
    ins = []
    for unit in units:
        wide = lambda array, off, unit=unit: (array, (OWN, UNIT), lambda h, sv: (0, off * span + unit))
        ins += [wide(joined_a, 0), wide(joined_a, 1), wide(joined_b, 0), wide(joined_a, 2), wide(joined_b, 1)]
        ins += [wide(mixed, 0), wide(d_mixed, 0), (lse, (2, 2, OWN), lambda h, sv, unit=unit: (unit, 0, 0))]
    return launch(
        functools.partial(attend_back_kernel, len(units)),
        sv,
        (1,),
        ins,
        [out_whole((OWN, UNIT * len(units)), BF16)] * 5,
        after=after,
        limit=24,
        name="attend_back",
    )


QUARTER = WIDTH // 4


def rows_of(array):
    return (array, (PART, array.shape[1]), lambda i, sv: (i, 0))


def out_rows(wide, dtype):
    return ((OWN, wide), dtype, (PART, wide), lambda i, sv: (i, 0))


def gelu_pair(u):
    z = jnp.abs(u) * 0.7071067811865476
    t = 1.0 / (1.0 + 0.3275911 * z)
    e = jnp.exp2(u * u * (-0.5 * LOG2E))
    series = t * (
        0.5 * 0.254829592
        + t * (0.5 * -0.284496736 + t * (0.5 * 1.421413741 + t * (0.5 * -1.453152027 + t * (0.5 * 1.061405429))))
    )
    tail = series * e
    below = jnp.where(u >= 0, 1.0 - tail, tail)
    return u * below, below + u * e * 0.3989422804014327


def step_part(j, sv):
    return 2 * jnp.where(lax.rem(j, 2) == 0, sv[FAR_Y], sv[Y]) + jnp.where(j < 2, 1 - sv[CORE], sv[CORE])


BLOCK = FF // 4 // GROUPS
FF_ROWS = 8 * QUARTER + 6 * BLOCK


def ff_head(sv, ins, branch_ref, dout_ref, second_ref, secondt_ref, dbt_ref):
    mixed_ref, entered_ref, d0_ref, d1_ref, wproj_ref, bias_ref, sattn_ref, gain_ref, shift_ref, sffn_ref = ins
    branch = dot(mixed_ref[...], wproj_ref[...]) + bias_ref[...]
    branch_ref[...] = branch
    n, _rho = norm_parts(entered_ref[...].astype(F32) + sattn_ref[...] * branch)
    second = (n * gain_ref[...] + shift_ref[...]).astype(BF16)
    second_ref[...] = second
    turned = second.T
    for part in range(4):
        place = jnp.where(part % 2 != sv[CORE], 0, 2) + jnp.where(part // 2 != sv[Y], 0, 1)
        secondt_ref[pl.ds(pl.multiple_of(place * QUARTER, 16), QUARTER), :] = turned[
            QUARTER * part : QUARTER * part + QUARTER
        ]
    dout_ref[:PART, :], dout_ref[PART:, :] = d0_ref[...], d1_ref[...]
    dbt_ref[...] = (dout_ref[:, :WIDTH].astype(F32) * sffn_ref[...]).astype(BF16)


def ff_kernel(opens, sv, *refs):
    weights = [refs[3 * i : 3 * i + 3] for i in range(4)]
    branch2_ref, grad_ref, gb1_ref, *shares = refs[-7:]
    if opens:
        head = refs[22:27]
        second_ref, secondt_ref, dbt_ref = head[2:]
    else:
        second_ref, secondt_ref, dbt_ref = refs[12:15]

    @pl.when(pl.program_id(0) == 0)
    def _():
        if opens:
            ff_head(sv, refs[12:22], *head)
            branch2_ref[...] = jnp.zeros((OWN, WIDTH), F32)
            grad_ref[...] = jnp.zeros((OWN, WIDTH), F32)
        else:
            branch2_ref[...] = refs[15][...]
            grad_ref[...] = refs[16][...]

    hidden, d_pre = [], []

    def first(i):
        w1_ref, b1_ref, w2_ref = weights[i]
        return dot(second_ref[...], w1_ref[...]) + b1_ref[...], dot_nt(dbt_ref[...], w2_ref[...])

    def then(i, products):
        value, slope = gelu_pair(products[0])
        hidden.append(value.astype(BF16))
        d_pre.append((products[1] * slope).astype(BF16))
        spot = pl.ds(pl.multiple_of(step_part(i, sv) * BLOCK, BLOCK), BLOCK)
        gb1_ref[:, spot] = jnp.sum(d_pre[-1].astype(F32), 0, keepdims=True)

    ahead(4, first, then)
    hidden, d_pre = jnp.concatenate(hidden, 1), jnp.concatenate(d_pre, 1)
    gw1 = dot(secondt_ref[...], d_pre).astype(BF16)
    for i in range(4):
        for k in range(2):
            spot = pl.ds(pl.multiple_of((2 * step_part(i, sv) + k) * QUARTER, 16), QUARTER)
            at = BLOCK * i + 128 * k
            for ref, row in zip(shares, range(0, WIDTH, QUARTER)):
                ref[spot, :] = gw1[row : row + QUARTER, at : at + 128]
    gw2 = dot_tn(hidden, dbt_ref[...]).astype(BF16)
    for i in range(4):
        for k in range(6):
            low = 8 * QUARTER + BLOCK * k
            shares[i][low : low + BLOCK, :] = gw2[BLOCK * i : BLOCK * i + BLOCK, 128 * k : 128 * k + 128]
    branch2_ref[...] += dot(hidden, jnp.concatenate([w[2][...] for w in weights], 0))
    grad_ref[...] += dot_nt(d_pre, jnp.concatenate([w[0][...] for w in weights], 1))


def feed_forward(sv, groups, others, w1, table, w2, opens):
    streamed = []
    for i in range(4):
        at = lambda g, sv, i=i: GROUPS * step_part(i, sv) + g + groups[0]
        streamed += [
            (w1, (WIDTH, BLOCK), lambda g, sv, at=at: (0, at(g, sv))),
            (table, (1, BLOCK), lambda g, sv, at=at: (0, 11 * GROUPS + at(g, sv))),
            (w2, (BLOCK, WIDTH), lambda g, sv, at=at: (at(g, sv), 0)),
        ]
    count = len(groups)
    head = [
        out_whole((OWN, WIDTH), F32),
        out_whole((OWN, WIDTH + 128), BF16),
        out_whole((OWN, WIDTH), BF16),
        out_whole((WIDTH, OWN), BF16),
        out_whole((OWN, WIDTH), BF16),
    ]
    return launch(
        functools.partial(ff_kernel, opens),
        sv,
        (count,),
        streamed + [o if isinstance(o, tuple) else whole(o) for o in others],
        (head if opens else [])
        + [
            out_whole((OWN, WIDTH), F32),
            out_whole((OWN, WIDTH), F32),
            ((1, 4 * BLOCK * count), F32, (1, 4 * BLOCK), lambda g, sv: (0, g)),
            *[((count * FF_ROWS, 128), BF16, (FF_ROWS, 128), lambda g, sv: (g, 0))] * 4,
        ],
        limit=16,
        name=f"feed_forward_{groups[0]}",
    )


def tail_kernel(
    sv, branch2_ref, g_ref, branch_ref, entered_ref, dout_ref, w_ref, b2_ref, sffn_ref, sattn_ref, gain_ref,
    out_ref, dmid_ref, dbr_ref, dmix_ref, vec_ref,
):
    branch_two = branch2_ref[...] + b2_ref[...]
    d_out = dout_ref[:, :WIDTH].astype(F32)
    branch = branch_ref[...]
    middle = entered_ref[...].astype(F32) + sattn_ref[...] * branch
    out_ref[...] = (middle + sffn_ref[...] * branch_two).astype(BF16)
    n, rho = norm_parts(middle)
    g = g_ref[...]
    scaled = g * gain_ref[...]
    d_middle = d_out + rho * (
        scaled - jnp.mean(scaled, -1, keepdims=True) - n * jnp.mean(scaled * n, -1, keepdims=True)
    )
    dmid_ref[...] = d_middle
    d_branch = (d_middle * sattn_ref[...]).astype(BF16)
    dbr_ref[...] = d_branch
    dmix_ref[...] = dot_nt(d_branch, w_ref[...]).astype(BF16)
    rounded = (d_out * sffn_ref[...]).astype(BF16).astype(F32)
    add_vectors(
        vec_ref,
        [d_out * branch_two, rounded, g * n, g, d_middle * branch, d_branch.astype(F32)],
    )


def add_vectors(vec_ref, values):
    rows = [jnp.sum(v, 0, keepdims=True) for v in values]
    vec = jnp.concatenate(rows + [jnp.zeros((8 - len(rows), WIDTH), F32)], 0)

    @pl.when(pl.program_id(0) == 0)
    def _():
        vec_ref[...] = vec

    @pl.when(pl.program_id(0) > 0)
    def _():
        vec_ref[...] += vec


def ff_tail(sv, branch2, g, branch, entered, dout, w_proj, vectors, after):
    return launch(
        tail_kernel,
        sv,
        (2,),
        [rows_of(a) for a in (branch2, g, branch, entered, dout)] + [whole(w_proj)] + list(vectors),
        [out_rows(WIDTH, BF16), out_rows(WIDTH, F32), out_rows(WIDTH, BF16), out_rows(WIDTH, BF16), out_whole((8, WIDTH), F32)],
        after=after,
        limit=16,
        name="ff_tail",
    )


def store_slabs(sv, kept, slabs, low, shares):
    for step, ref in enumerate(shares):
        rows = pl.ds(pl.multiple_of(step_part(step, sv) * QUARTER, 16), QUARTER)
        for i in range(slabs):
            at = (low + i) * QUARTER
            ref[at : at + QUARTER, :] = kept[rows, 128 * i : 128 * i + 128].astype(BF16)


def grads_kernel(
    sv, mixed_ref, dbr_ref, normed_ref, dq_ref, dk_ref, rk_ref, dv_ref, rv_ref, *rest
):
    *shares, dkey_ref, dvalue_ref, kept = rest
    kept[:, :WIDTH] = dot_tn(mixed_ref[...], dbr_ref[...])
    store_slabs(sv, kept, 6, 0, shares)
    d_key = (dk_ref[...].astype(F32) + rk_ref[...].astype(F32)).astype(BF16)
    d_value = (dv_ref[...].astype(F32) + rv_ref[...].astype(F32)).astype(BF16)
    dkey_ref[...] = d_key
    dvalue_ref[...] = d_value
    kept[...] = dot_tn(normed_ref[...], jnp.concatenate([dq_ref[...], d_key, d_value], 1))
    store_slabs(sv, kept, 18, 6, shares)


def projection_grads(sv, mixed, d_branch, normed, parts, after):
    rows = 24 * QUARTER
    return launch(
        grads_kernel,
        sv,
        (1,),
        [whole(a) for a in (mixed, d_branch, normed, *parts)],
        [out_whole((rows, 128), BF16)] * 4 + [out_whole((OWN, WIDTH), BF16)] * 2,
        scratch=[pltpu.VMEM((WIDTH, 3 * WIDTH), F32)],
        after=after,
        limit=24,
        name="projection_grads",
    )


VECTORS = 32


def entry_kernel(
    sv, dq_ref, dk_ref, dv_ref, w_ref, entered_ref, dmid_ref, dout_ref, gain_ref,
    va_ref, b1a_ref, b1b_ref, grad_ref, sums_ref, vec_ref,
):
    dq, dk, dv = dq_ref[...], dk_ref[...], dv_ref[...]
    g = dot_nt(jnp.concatenate([dq, dk, dv], 1), w_ref[...])
    n, rho = norm_parts(entered_ref[...].astype(F32))
    scaled = g * gain_ref[...]
    d_entered = dmid_ref[...] + rho * (
        scaled - jnp.mean(scaled, -1, keepdims=True) - n * jnp.mean(scaled * n, -1, keepdims=True)
    )
    chosen = jnp.concatenate([dout_ref[:, WIDTH:].astype(F32)] * 6, 1)
    masked = d_entered * chosen
    grad_ref[...] = (d_entered - masked).astype(BF16)
    add_vectors(vec_ref, [masked, g * n, g, dq.astype(F32), dv.astype(F32)])

    @pl.when(pl.program_id(0) == 1)
    def _():
        b1 = jnp.concatenate([b1a_ref[...], b1b_ref[...]], 1)
        parts = [
            jnp.concatenate([b1[:, 4 * BLOCK * g + BLOCK * p : 4 * BLOCK * g + BLOCK * (p + 1)] for g in range(GROUPS)], 1)
            for p in range(4)
        ]
        rows = [va_ref[...], vec_ref[...], *parts, jnp.zeros((VECTORS - 20, WIDTH), F32)]
        rows = jnp.concatenate(rows, 0)
        for i in range(WIDTH // 128):
            sums_ref[VECTORS * i : VECTORS * i + VECTORS, :] = rows[:, 128 * i : 128 * i + 128]


def entry_back(sv, parts, w_qkv, entered, d_middle, dout, gain, vectors, after):
    return launch(
        entry_kernel,
        sv,
        (2,),
        [rows_of(p) for p in parts]
        + [whole(w_qkv), rows_of(entered), rows_of(d_middle), rows_of(dout), gain]
        + [whole(v) for v in vectors],
        [out_rows(WIDTH, BF16), out_whole((VECTORS * WIDTH // 128, 128), F32)],
        scratch=[pltpu.VMEM((8, WIDTH), F32)],
        after=after,
        limit=20,
        micros=10,
        name="entry_back",
    )


CORE, Y, FAR_Y, X, FAR_X, Z, FAR_Z, QUARTER_MINE, QUARTER_FAR, TURNED_MINE, TURNED_FAR, COUNTS = range(12)


def swap(value, axis, distance):
    count = lax.axis_size(axis)
    return lax.ppermute(value, axis, [(i, i ^ distance) for i in range(count)])


def sums_kernel(plan, sv, *refs):
    count = sum(terms for _, _, parts in plan for _, terms in parts)
    ins, outs = list(refs[:count]), refs[count:]
    for (_, _, parts), out_ref in zip(plan, outs):
        low = 0
        for rows, terms in parts:
            total = ins.pop(0)[...].astype(F32)
            for _ in range(terms - 1):
                total += ins.pop(0)[...].astype(F32)
            out_ref[low : low + rows, :] = total.astype(out_ref.dtype)
            low += rows


def add_up(sv, outs, after, name, micros=0.05):
    ins, plan, results = [], [], []
    for dtype, parts in outs:
        for rows, terms in parts:
            for array, block, skip in terms:
                at = lambda i, sv, block=block, skip=skip: (skip if block is None else sv[block] + skip, 0)
                ins.append((array, (rows, 128), at))
        total = sum(rows for rows, _ in parts)
        plan.append((None, None, [(rows, len(terms)) for rows, terms in parts]))
        results.append(out_whole((total, 128), dtype))
    return list(launch(functools.partial(sums_kernel, plan), sv, (1,), ins, results, after=after, limit=8, micros=micros, name=name))


class Piece:
    def __init__(self, order, kept, rows, skip=0):
        self.order, self.rows, self.skip = order, rows, skip
        self.far, self.near, self.core_far, self.core = kept

    def two(self, share, block, far):
        a, b = (self.far, self.core_far) if far else (self.near, self.core)
        return [(a, block, share * self.skip), (b, block, share * self.skip)]

    def first(self):
        n = self.rows
        if self.order == "yxz":
            return [(n, self.two(1, None, True))], None
        far, mine = (FAR_X, X) if self.order[0] == "x" else (FAR_Z, Z)
        return tuple([(n // 2, self.two(2, block, True)), (n // 2, self.two(2, block, False))] for block in (far, mine))

    def both(self, rows, block, skip):
        assert self.kept[1] % rows == 0 and self.arrived[1] % rows == 0
        return [(array, block, skip + offset // rows) for array, offset in (self.kept, self.arrived)]

    def second(self):
        n = self.rows
        if self.order == "yxz":
            array, offset = self.arrived
            assert offset % (n // 2) == 0
            skip = offset // (n // 2)
            return tuple([(n // 2, self.two(2, at, False) + [(array, at, skip)])] for at in (FAR_X, X))
        if self.order == "xzy":
            return tuple([(n // 4, self.both(n // 4, at, skip)) for skip in (0, 2)] for at in (FAR_Z, Z))
        return tuple([(n // 2, self.both(n // 2, None, skip))] for skip in (0, 1))

    def third(self):
        n = self.rows
        if self.order == "xzy":
            return tuple([(n // 4, self.both(n // 4, None, skip))] for skip in (0, 1))
        far, mine = (FAR_X, X) if self.order[2] == "x" else (FAR_Z, Z)
        return tuple([(n // 4, self.both(n // 4, at, 0))] for at in (far, mine))

    def fourth(self):
        return (self.rows // 4, self.both(self.rows // 4, None, 0))


class Payload:
    def __init__(self, sv, name, *pieces, micros=0.05, vectors=None):
        self.sv, self.name, self.pieces, self.micros = sv, name, list(pieces), micros
        self.vectors = vectors
        if vectors is not None:
            self.more = [swap(vectors, "seq", d) for d in (1, 2, 3)]

    def ride(self, outs):
        if self.vectors is None:
            return outs
        terms = [(v, None, 0) for v in (self.vectors, *self.more)]
        return outs + [(F32, [(self.vectors.shape[0], terms)])]

    def rode(self, sums, distance):
        if self.vectors is not None:
            self.vectors = sums.pop()
            self.more = [swap(self.vectors, "dp", distance)]

    def step(self, number, after):
        plans = [(p, *(p.first, p.second, p.third)[number]()) for p in self.pieces]
        axes = sorted({p.order[number] for p in self.pieces})
        packs = {axis: [] for axis in axes}
        places, kept, keepers = [], [], []

        def put(pack, parts):
            at = sum(rows for rows, _ in pack)
            pack += parts
            return at

        for p, send, keep in plans:
            places.append((p, p.order[number], put(packs[p.order[number]], send)))
            if keep:
                keepers.append((p, put(kept, keep)))
        outs = [(BF16, packs[axis]) for axis in axes] + ([(F32, kept)] if kept else [])
        outs = self.ride(outs) if number == 2 else outs
        sums = add_up(self.sv, outs, after, f"{self.name}_{number + 1}", self.micros)
        if number == 2:
            self.rode(sums, 1)
        for p, at in keepers:
            p.kept = (sums[len(axes)], at)
        sent = sums[: len(axes)]
        where = {"y": ("seq", 2), "x": ("dp", 1), "z": ("dp", 2)}
        arrived = {axis: swap(value, *where[axis]) for axis, value in zip(axes, sent)}
        for p, axis, at in places:
            p.arrived = (arrived[axis], at)
        return sent, list(arrived.values())

    def far_z(self, after):
        outs = self.ride([(BF16, [p.fourth() for p in self.pieces])])
        sums = add_up(self.sv, outs, after, self.name + "_4", self.micros)
        self.rode(sums, 2)
        self.sums, self.arrived = sums, [swap(sums[0], "dp", 4)]
        return sums, self.arrived

    def far_z_halves(self, after):
        first, middle, last = self.pieces
        rows = middle.rows // 8
        low, high = [(rows, middle.both(rows, None, i)) for i in range(2)]
        self.sums = add_up(self.sv, [(BF16, [first.fourth(), low]), (BF16, [high, last.fourth()])], after, self.name + "_4")
        self.arrived = [swap(value, "dp", 4) for value in self.sums]
        return self.sums, self.arrived

    def back(self, after, micros=0.05):
        parts = [(mine.shape[0], [(mine, None, 0), (other, None, 0)]) for mine, other in zip(self.sums, self.arrived)]
        sums = add_up(self.sv, self.ride([(BF16, parts)]), after, self.name + "_5", micros)
        self.rode(sums, 4)
        (own,) = sums
        across = swap(own, "dp", 2)
        self.gathered = [own, across, swap(own, "dp", 1), swap(across, "dp", 1)]
        return [own], self.gathered[1:]

    def psum(self):
        gathered = []
        for p in self.pieces:
            terms = p.two(1, None, False) + [(p.arrived[0], None, p.arrived[1] // p.rows)]
            (out,) = add_up(self.sv, [(BF16, [(p.rows, terms)])], [], self.name + "_all")
            out, quarter = lax.psum(out, "dp"), p.rows // 4
            places = [self.sv[QUARTER_MINE] ^ d for d in range(4)]
            gathered.append([lax.dynamic_slice_in_dim(out, place * quarter, quarter, 0) for place in places])
        self.gathered = [jnp.concatenate(parts, 0) for parts in zip(*gathered)]

    def layout(self):
        return [(p.order, p.rows) for p in self.pieces]


def share(arrays):
    return [arrays[2], arrays[3], swap(arrays[0], "seq", 1), swap(arrays[1], "seq", 1)]


def copy_kernel(sv, in_ref, out_ref):
    out_ref[...] = in_ref[...]


def copy_rows(sv, array, part, after, name):
    ins = [(array, (PART, WIDTH), lambda i, sv: (part, 0))]
    return launch(copy_kernel, sv, (1,), ins, [out_whole((PART, WIDTH), array.dtype)], after=after, name=name)[0]


def order_pieces(sv, layout, refs, whole_ref):
    low = 0
    for order, rows in layout:
        quarter = rows // 4
        for d, ref in enumerate(refs):
            place = (sv[TURNED_MINE] ^ (0, 2, 1, 3)[d]) if order == "zyx" else (sv[QUARTER_MINE] ^ d)
            at = pl.multiple_of(low + place * quarter, 16)
            whole_ref[pl.ds(at, quarter), :] = ref[low // 4 : low // 4 + quarter, :]
        low += rows


def slab(whole_ref, at, rows):
    return whole_ref[at : at + rows, :].astype(F32)


def finish_ff_kernel(layout, sv, *refs):
    w1_ref, w2_ref, whole_ref = refs[-3:]
    order_pieces(sv, layout, refs[:4], whole_ref)
    for g in range(GROUPS):
        low = FF_ROWS * g
        for i in range(6):
            w2_ref[BLOCK * g : BLOCK * g + BLOCK, 128 * i : 128 * i + 128] = slab(whole_ref, low + 8 * QUARTER + BLOCK * i, BLOCK)
        for i in range(8):
            at = BLOCK * (GROUPS * (i // 2) + g) + 128 * (i % 2)
            w1_ref[:, at : at + 128] = slab(whole_ref, low + QUARTER * i, QUARTER)


def finish_ff(sv, payload, after):
    return launch(
        functools.partial(finish_ff_kernel, payload.layout()),
        sv,
        (1,),
        [whole(part) for part in payload.gathered],
        [out_whole((QUARTER, FF), F32), out_whole((FF // 4, WIDTH), F32)],
        scratch=[pltpu.VMEM((GROUPS * FF_ROWS, 128), BF16)],
        after=after,
        limit=20,
        micros=5,
        name="finish_ff",
    )


def finish_rest_kernel(layout, sv, *refs):
    proj_ref, qkv_ref, vec_ref, whole_ref = refs[-4:]
    vec = refs[4][...] + refs[5][...]
    for i in range(WIDTH // 128):
        vec_ref[:, 128 * i : 128 * i + 128] = vec[VECTORS * i : VECTORS * i + VECTORS]
    order_pieces(sv, layout, refs[:4], whole_ref)
    for i in range(6):
        proj_ref[:, 128 * i : 128 * i + 128] = slab(whole_ref, i * QUARTER, QUARTER)
    for i in range(18):
        qkv_ref[:, 128 * i : 128 * i + 128] = slab(whole_ref, (6 + i) * QUARTER, QUARTER)


def finish_rest(sv, payload, after):
    return launch(
        functools.partial(finish_rest_kernel, payload.layout()),
        sv,
        (1,),
        [whole(part) for part in (*payload.gathered, payload.vectors, *payload.more)],
        [
            out_whole((QUARTER, WIDTH), F32),
            out_whole((QUARTER, 3 * WIDTH), F32),
            out_whole((VECTORS, WIDTH), F32),
        ],
        scratch=[pltpu.VMEM((24 * QUARTER, 128), BF16)],
        after=after,
        limit=16,
        name="finish_rest",
    )


def per_device(
    patches, mask, mask_token, ln1_gain, ln1_bias, w_qkv, bias_q, bias_v, w_proj, bias_proj, scale_attn,
    ln2_gain, ln2_bias, w_fc1, bias_fc1, w_fc2, bias_fc2, scale_ffn, cotangent,
):
    slot_rows, images_here, width = patches.shape
    parts = lax.axis_size("seq")
    assert parts == 4 and images_here == 2 and width == WIDTH
    s = lax.axis_index("seq")
    dp = lax.axis_index("dp")
    y, core = s // 2, s % 2
    x, z = dp % 2, dp // 2 % 2

    def live_count(part):
        lead = (part == 0).astype(jnp.int32)
        return lead + (GRID // parts + (part < GRID % parts).astype(jnp.int32)) * GRID

    sv = jnp.stack(
        [core, y, 1 - y, x, 1 - x, z, 1 - z, 2 * x + z, 2 * x + 1 - z, 2 * z + x, 2 * z + 1 - x]
        + [live_count(s), live_count(s ^ 2), live_count(s ^ 1), live_count(s ^ 3)]
    ).astype(jnp.int32)
    table = jnp.concatenate(
        [
            bias_q, jnp.zeros_like(bias_q), bias_v, ln1_gain, ln1_bias, ln2_gain, ln2_bias, scale_attn, scale_ffn,
            bias_proj, bias_fc2, bias_fc1,
        ]
    ).astype(F32)[None, :]
    gain1, _shift1, gain2, shift2, sattn, sffn, bproj, b2 = [row_of(table, i) for i in range(3, 11)]

    chosen = mask[:, :, None] == 1
    entered = jnp.where(chosen, mask_token, patches)
    grow = ((0, PART - slot_rows), (0, 0))
    image = lambda array, i: lax.dynamic_index_in_dim(array, i, 1, keepdims=False)
    x1 = swap(jnp.pad(image(entered, 1 - y), grow), "seq", 2)
    x0 = jnp.pad(image(entered, y), grow)
    xb0 = swap(x0, "seq", 1)
    d_rows = jnp.concatenate(
        [
            jnp.where(chosen, cotangent, jnp.zeros_like(cotangent)),
            jnp.broadcast_to(chosen, (slot_rows, images_here, 128)).astype(BF16),
        ],
        -1,
    )
    d1 = swap(jnp.pad(image(d_rows, 1 - y), grow), "seq", 2)
    d0 = jnp.pad(image(d_rows, y), grow)

    own_first = qkv_part(True, 0, x0, table, w_qkv, [])
    other_first = qkv_part(False, 0, xb0, table, w_qkv, [])
    xb1 = swap(x1, "seq", 1)
    joined_a, normed, entered_a = qkv_part(True, 1, x1, table, w_qkv, own_first)
    (joined_b,) = qkv_part(False, 1, xb1, table, w_qkv, other_first)
    mixed, lse = attend(sv, joined_a, joined_b)
    fused = lax.axis_size("dp") == 8
    orders = ("yxz", "xzy", "zyx") if fused else ("yxz",) * 3
    branch, dout, second, secondt, dbt, branch2, g, gb1a, *shares = feed_forward(
        sv, (0, 1), [mixed, entered_a, d0, d1, w_proj, bproj, sattn, gain2, shift2, sffn], w_fc1, table, w_fc2, True
    )
    shares = share(shares)
    ff01 = Payload(sv, "ff01", *[Piece(orders[i], shares, FF_ROWS, i) for i in range(2)])
    branch2, g, gb1b, *shares = feed_forward(
        sv, (2,), [second, secondt, dbt, branch2, g], w_fc1, table, w_fc2, False
    )
    ff2 = Payload(sv, "ff2", Piece(orders[2], share(shares), FF_ROWS), micros=2)
    ff = Payload(sv, "ff", *ff01.pieces, *ff2.pieces)

    def halves(kept):
        rows = kept[0].shape[0] // 2
        return [Piece("yxz", kept, rows, 0), Piece("xyz" if fused else "yxz", kept, rows, 1)]

    def far_rows(array, after, name):
        return swap(copy_rows(sv, array, 1, after, name), "seq", 2)

    def place_rows(array, far):
        near, far = array[:slot_rows, None], far[:slot_rows, None]
        return jnp.where(y == 0, jnp.concatenate([near, far], 1), jnp.concatenate([far, near], 1))

    sent, arrived = ff01.step(0, [gb1b])
    sent, more = ff2.step(0, sent)
    out_a, d_middle, d_branch, d_mixed, vec_a = ff_tail(
        sv, branch2, g, branch, entered_a, dout, w_proj, [b2, sffn, sattn, gain2], sent
    )
    dq, dka, dva, dkb, dvb = attend_back(sv, joined_a, joined_b, mixed, d_mixed, lse, sent)
    rk, rv = swap(dkb, "seq", 1), swap(dvb, "seq", 1)
    sent = [dq]
    if fused:
        sent, arrived = ff01.step(1, sent + arrived)
        sent, more = ff2.step(1, sent + more)
    *shares, d_key, d_value = projection_grads(sv, mixed, d_branch, normed, [dq, dka, rk, dva, rv], sent)
    shares = share(shares)
    grad_a, vectors = entry_back(
        sv, [dq, d_key, d_value], w_qkv, entered_a, d_middle, dout, gain1, [vec_a, gb1a, gb1b], []
    )
    both = Payload(sv, "both", *halves(shares), vectors=vectors if fused else None)
    sent = [grad_a]
    if fused:
        sent, arrived = ff.step(2, sent + arrived + more)
    sent, more = both.step(0, sent)
    if fused:
        ff.micros = 3
        sent, arrived = ff.far_z(sent + arrived)
        sent, more = both.step(1, sent + more)
        sent, more = both.step(2, arrived + sent + more)
        sent, arrived = ff.back(sent + arrived)
        sent, more = both.far_z(sent + more)
        out_far = far_rows(out_a, sent, "layer_out_far")
        grad_far = far_rows(grad_a, sent, "input_grad_far")
        sent, more = both.back(sent + more + [arrived[1]], 10)
        layer_out = place_rows(out_a, out_far)
        input_grad = place_rows(grad_a, grad_far)
        grad_w1, grad_w2 = finish_ff(sv, ff, sent + arrived)
    else:
        ff.psum()
        both.psum()
        both.vectors, both.more = lax.psum(vectors, ("dp", "seq")), [jnp.zeros_like(vectors)]
        grad_w1, grad_w2 = finish_ff(sv, ff, [])
        layer_out = place_rows(out_a, far_rows(out_a, [], "layer_out_far"))
        input_grad = place_rows(grad_a, far_rows(grad_a, [], "input_grad_far"))
    grad_proj, grad_qkv, vectors = finish_rest(sv, both, [grad_w1, layer_out, input_grad])
    grad_b1 = lax.dynamic_index_in_dim(vectors[16:20], s, 0, keepdims=False)
    vectors = lax.dynamic_slice_in_dim(vectors[:16], s * QUARTER, QUARTER, 1)

    return (
        layer_out, input_grad,
        vectors[8], vectors[9], vectors[10], grad_qkv, vectors[11], vectors[12], grad_proj,
        vectors[5], vectors[4], vectors[2], vectors[3], grad_w1, grad_b1, grad_w2, vectors[1], vectors[0],
    )


def solution(mesh):
    rows, flat = P("seq", "dp", None), P("seq")
    deep = P("seq", None)
    return jax.shard_map(
        per_device,
        mesh=mesh,
        in_specs=(rows, P("seq", "dp")) + (P(),) * 16 + (rows,),
        out_specs=(
            rows, rows, flat, flat, flat, deep, flat, flat, deep, flat, flat, flat, flat, deep, flat, deep, flat, flat,
        ),
        check_vma=False,
    )
```
